128 devices in a mesh: dp: 8 (over x, z_lo), ctx: 8 (over y, core), tensor: 2 (over z_hi).
Axes of the slice: x: 4, y: 4, z: 4 (z_hi: 2, z_lo: 2; z = z_hi * 2 + z_lo), core: 2. Of those that a mesh axis runs over, the one named last changes fastest.
Arguments:
- tokens: bfloat16 [32768, 768], P(('dp', 'ctx', 'tensor')), may hold values from -24 to 24
- cotangent: bfloat16 [32768, 768], P(('dp', 'ctx', 'tensor')), may hold values from -24 to 24
- w_qkv: bfloat16 [3, 768, 768], P(None, ('dp', 'ctx'), 'tensor'), may hold values from -0.21875 to 0.21875
- w_out: bfloat16 [768, 768], P('tensor', ('dp', 'ctx')), may hold values from -1.25 to 1.25
- w_up: bfloat16 [768, 3072], P(('dp', 'ctx'), 'tensor'), may hold values from -0.21875 to 0.21875
- w_down: bfloat16 [3072, 768], P('tensor', ('dp', 'ctx')), may hold values from -0.109375 to 0.109375
- norm_gains: bfloat16 [2, 768], P(None, ('dp', 'ctx')), may hold values from 0.099609375 to 1.8984375
Outputs:
- result: bfloat16 [32768, 768], P(('dp', 'ctx', 'tensor'))
- grad_tokens: float32 [32768, 768], P(('dp', 'ctx', 'tensor'))
- grad_qkv: float32 [3, 768, 768], P(None, ('dp', 'ctx'), 'tensor')
- grad_out: float32 [768, 768], P('tensor', ('dp', 'ctx'))
- grad_up: float32 [768, 3072], P(('dp', 'ctx'), 'tensor')
- grad_down: float32 [3072, 768], P('tensor', ('dp', 'ctx'))
- grad_gains: float32 [2, 768], P(None, ('dp', 'ctx'))
The draws below stay inside these ranges and needn't reach their ends.
All inputs are finite; a program needn't handle non-finite values.
Results may differ from the reference program's by a relative error of at most 0.03.
Values may be sent and summed in bfloat16 or wider, within the bound.
A program may use at most 192 MiB of HBM per device.

```python
import jax
import jax.numpy as jnp
from jax import lax

D = 768
HEADS = 12
HEAD_DIM = 64
FF = 3072
LEN = 4096
TOKENS = 32768


def strengthened(entries, own_key, source, target, blocks, factor):
    def block_of(position):
        return (jnp.arange(entries.shape[position]) // (entries.shape[position] // blocks)).reshape((-1,) + (1,) * (entries.ndim - 1 - position))

    first = jax.random.permutation(own_key, blocks)[block_of(target)]
    far = (block_of(target) + blocks // 2) % blocks
    return jnp.where((block_of(source) == first) | (block_of(source) == far), factor * entries, entries)


def block_scale(own_key, extent, pieces, least, top_value):
    def one(axis_at, parts):
        steps = jax.random.uniform(jax.random.fold_in(jax.random.fold_in(own_key, 6), axis_at), (parts,), jnp.float32, least / len(pieces), top_value / len(pieces))
        return jnp.repeat(jnp.exp(steps), extent[axis_at] // parts).reshape((-1,) + (1,) * (len(extent) - axis_at - 1))

    level = one(*pieces[0])
    for cut in pieces[1:]:
        level = level * one(*cut)
    return level


def noise(stream_key, shape, deviation, limit, shards=(), kind=jnp.bfloat16):
    values = jax.random.normal(stream_key, shape, jnp.float32) * deviation
    if len(shards) > 0:
        values = block_scale(stream_key, shape, shards, -0.22, 0.18) * values
    return jnp.clip(values, min=-limit, max=limit).astype(kind)


def bell_draw_with(rng, dims, spread, bound, shards, heavy, kind=jnp.bfloat16):
    result = spread * jax.random.normal(rng, dims, jnp.float32)
    if shards:
        result = result * block_scale(rng, dims, shards, -0.22, 0.18)
    return jnp.clip(strengthened(result, jax.random.fold_in(rng, 3), *heavy), -bound, bound).astype(kind)


def setup_inputs(seed: int = 0) -> dict:
    key_of = jax.random.split(jax.random.key(seed), 8)
    tokens = bell_draw_with(key_of[0], (TOKENS, D), 1.0, 24.0, ((0, 128),), (0, 1, 128, 5.5))
    cotangent = bell_draw_with(key_of[1], (TOKENS, D), 1.0, 24.0, ((0, 128),), (0, 1, 128, 5.5))
    w_qkv = noise(key_of[2], (3, D, D), D ** -0.5, 0.21875, ((1, 64), (2, 2)))
    w_out = noise(key_of[3], (D, D), (D // 32) ** -0.5, 1.25, ((0, 2), (1, 64)))
    w_up = noise(key_of[4], (D, FF), D ** -0.5, 0.21875, ((0, 64), (1, 2)))
    w_down = noise(key_of[5], (FF, D), FF ** -0.5, 0.109375, ((0, 2), (1, 64)))
    norm_gains = jnp.clip(1.0 + 0.18 * jax.random.normal(key_of[6], (2, D), jnp.float32), 0.099609375, 1.8984375).astype(jnp.bfloat16)
    return dict(tokens=tokens, cotangent=cotangent, w_qkv=w_qkv, w_out=w_out, w_up=w_up, w_down=w_down, norm_gains=norm_gains)


@jax.custom_vjp
def low(v):
    return lax.optimization_barrier(v.astype(jnp.bfloat16)).astype(jnp.float32)

@jax.custom_vjp
def low_back(v):
    return v

def low_keep(v):
    return (low(v), None)

def low_pass(kept, grad):
    return (grad,)

def back_keep(v):
    return (v, None)

def back_low(kept, grad):
    return (low(grad),)
low.defvjp(low_keep, low_pass)
low_back.defvjp(back_keep, back_low)
epsilon = 1e-05
neg_large = -1e+30
highest = lax.Precision.HIGHEST

def normalize(values):
    center = values - lax.optimization_barrier(jnp.mean(values, axis=-1, keepdims=True))
    return center * lax.rsqrt(lax.optimization_barrier(jnp.mean(center * center, axis=-1, keepdims=True)) + epsilon)

def block_layer(inputs, w_qkv, w_out, w_up, w_down, norm_gains):
    length = inputs.shape[0]
    first_in = low(normalize(inputs) * norm_gains[0])
    projected = low(low_back(jnp.einsum('td,kdc->ktc', first_in, w_qkv, precision=highest)))
    head_parts = projected.reshape(3, length, HEADS, HEAD_DIM)
    rows_block = min(512, length)
    positions = jnp.arange(length, dtype=jnp.int32)
    score_scale = HEAD_DIM ** (-0.5)

    def attend(block_index):
        first_row = block_index * rows_block
        queries = lax.dynamic_slice_in_dim(head_parts[0], first_row, rows_block, 0)
        scores = low_back(jnp.einsum('bhe,the->hbt', queries, head_parts[1], precision=highest)) * score_scale
        query_pos = first_row + jnp.arange(rows_block, dtype=jnp.int32)
        allowed = query_pos[:, None] >= positions[None, :]
        masked = jnp.where(allowed[None], scores, neg_large)
        row_top = lax.optimization_barrier(jnp.max(masked, axis=-1, keepdims=True))
        raised = jnp.exp(masked - row_top)
        probabilities = raised / lax.optimization_barrier(jnp.sum(raised, axis=-1, keepdims=True))
        return jnp.einsum('hbt,the->bhe', low(probabilities), head_parts[2], precision=highest)
    attended = lax.map(jax.checkpoint(attend), jnp.arange(length // rows_block, dtype=jnp.int32))
    attended = low(low_back(attended.reshape(length, HEADS * HEAD_DIM)))
    middle = inputs + low_back(jnp.dot(attended, w_out, precision=highest))
    second_in = low(normalize(middle) * norm_gains[1])
    hidden = low_back(jnp.dot(second_in, w_up, precision=highest))
    activated = low(jax.nn.gelu(hidden, approximate=True))
    return middle + jnp.dot(activated, w_down, precision=highest)

def reference(tokens, cotangent, w_qkv, w_out, w_up, w_down, norm_gains):
    weight_set = tuple((weight.astype(jnp.float32) for weight in (w_qkv, w_out, w_up, w_down, norm_gains)))
    sequences = tokens.astype(jnp.float32).reshape(-1, LEN, D)
    grad_seqs = cotangent.astype(jnp.float32).reshape(-1, LEN, D)

    def per_sequence(totals, operands):
        values, grad_seq = operands
        outcome, pullback = jax.vjp(block_layer, values, *weight_set)
        pulled = pullback(grad_seq)
        totals = tuple((total_part + pulled_part for total_part, pulled_part in zip(totals, pulled[1:])))
        return (totals, (outcome.astype(jnp.bfloat16), pulled[0]))
    empty_sums = tuple((jnp.zeros_like(weight) for weight in weight_set))
    totals, (outcomes, grad_inputs) = lax.scan(per_sequence, empty_sums, (sequences, grad_seqs))
    return (outcomes.reshape(-1, D), grad_inputs.reshape(-1, D), totals[0], totals[1], totals[2], totals[3], totals[4])
```

```python
import functools

import jax
import jax.numpy as jnp
import numpy as np
from jax import lax
from jax.experimental import pallas as pl
from jax.experimental.pallas import tpu as pltpu
from jax.sharding import PartitionSpec as P

HEAD_DIM = 64
HEADS = 12
MEMBERS = 16
ROWS = 12
WIDTH = 384
SLOT = 4 * ROWS
ORDERS = (("z", "x", "y"), ("x", "y", "z"), ("y", "z", "x"))
MESH = pl.DeviceIdType.MESH
VMEM_BYTES = 60 * 1024 * 1024
epsilon = 1e-05
neg_large = -1e30


def place():
    dp, ctx, tensor = lax.axis_index("dp"), lax.axis_index("ctx"), lax.axis_index("tensor")
    return dict(x=dp // 2, y=ctx // 2, z=2 * tensor + dp % 2, c=ctx % 2)


def device_at(pos, axis, index):
    at = dict(pos)
    at[axis] = index
    return (at["x"] * 2 + at["z"] % 2, at["y"] * 2 + at["c"], at["z"] // 2)


def beside(pos, axis, by):
    if axis == "c":
        return device_at(pos, "c", 1 - pos["c"])
    return device_at(pos, axis, (pos[axis] + by) % 4)


def greet_axes(pos):
    barrier = pltpu.get_barrier_semaphore()
    for axis in ("x", "y", "z"):
        for by in (1, 2, 3):
            pl.semaphore_signal(
                barrier, inc=1, device_id=beside(pos, axis, by), device_id_type=MESH
            )
    pl.semaphore_signal(barrier, inc=1, device_id=beside(pos, "c", 1), device_id_type=MESH)
    pl.semaphore_wait(barrier, 10)


def remote(src, dst, send, recv, device):
    return pltpu.make_async_remote_copy(
        src_ref=src,
        dst_ref=dst,
        send_sem=send,
        recv_sem=recv,
        device_id=device,
        device_id_type=MESH,
    )


class SmallSum:
    def __init__(self, pos, ring, pair, send, recv):
        self.pos, self.ring, self.pair, self.send, self.recv = pos, ring, pair, send, recv

    def copy(self, n, by, coming=False):
        axis = ("x", "y", "z")[n]
        slot = (self.pos[axis] + 4 - by) % 4 if coming else self.pos[axis]
        ref, sem = self.ring.at[n, slot], n * 3 + by - 1
        return remote(
            ref, ref, self.send.at[sem], self.recv.at[sem], beside(self.pos, axis, by)
        )

    def start(self, n, value):
        self.ring[n, self.pos[("x", "y", "z")[n]]] = value
        for by in (1, 2, 3):
            self.copy(n, by).start()

    def finish(self, n):
        for by in (1, 2, 3):
            self.copy(n, by, coming=True).wait_recv()
            self.copy(n, by).wait_send()
        return (self.ring[n, 0] + self.ring[n, 1]) + (self.ring[n, 2] + self.ring[n, 3])

    def pair_copy(self, slot):
        ref = self.pair.at[slot]
        return remote(ref, ref, self.send.at[9], self.recv.at[9], beside(self.pos, "c", 1))

    def start_pair(self, value):
        self.pair[self.pos["c"]] = value
        self.pair_copy(self.pos["c"]).start()

    def finish_pair(self):
        self.pair_copy(1 - self.pos["c"]).wait_recv()
        self.pair_copy(self.pos["c"]).wait_send()
        return self.pair[0] + self.pair[1]


def half_of(stage, which):
    if stage == 0:
        return pl.ds(0, 32) if which == 0 else pl.ds(32, 16)
    return pl.ds(2 * which, 2)


def block_at(pos, order, stage, index):
    if stage == 2:
        return (pos["c"], index)
    if stage == 1:
        return (pos["c"], pos[order[2]], index)
    return (pos["c"], pos[order[2]], pos[order[1]], index)


def group_slots(k, group, tensor):
    x, z_lo, y_pair = group // 4, (group // 2) % 2, group % 2
    found = []
    for member in range(4):
        at = dict(x=x, z=2 * tensor + z_lo, y=2 * y_pair + member // 2)
        order = ORDERS[k]
        found.append((member % 2, at[order[2]], at[order[1]], at[order[0]]))
    return found


def column_of(k, tensor, piece):
    if k == 0:
        return (0, (piece * 2 + tensor) * WIDTH) if piece < 3 else (1, tensor * WIDTH)
    return (k + 1, (tensor * 4 + piece) * WIDTH)


def gather_kernel(
    a, b, c, gain, shuffle, w_qkv, w_out, w_up, w_down, gain_out,
    g0, g1, g2, ring, pair, send, recv, small_send, small_recv,
):
    pos = place()
    kept = (g0, g1, g2)
    for k, shard in enumerate((a, b, c)):
        order = ORDERS[k]
        kept[k][block_at(pos, order, 0, pos[order[0]])] = shard[...]
    small = SmallSum(pos, ring, pair, small_send, small_recv)
    greet_axes(pos)
    started = []

    def move(k, index, sem, device):
        ref = kept[k].at[index]
        copy = remote(ref, ref, send.at[sem], recv.at[sem], device)
        copy.start()
        started.append(copy)

    def arrived(k, index, sem):
        ref = kept[k].at[index]
        remote(ref, ref, send.at[sem], recv.at[sem], beside(pos, "c", 1)).wait_recv()

    def share(k, by, sem):
        move(
            k, (pos["c"], (pos[ORDERS[k][2]] + by) % 4), 36 + k * 4 + sem, beside(pos, "c", 1)
        )

    small_value = gain[...]
    for stage in range(3):
        small.start(stage, small_value)
        for k in range(3):
            order, base = ORDERS[k], (k * 3 + stage) * 4
            axis = order[stage]
            own = block_at(pos, order, stage, pos[axis])
            move(k, own, base, beside(pos, axis, 1))
            move(k, own, base + 1, beside(pos, axis, 3))
            if stage == 2:
                share(k, 0, 0)
        for k in range(3):
            order, base = ORDERS[k], (k * 3 + stage) * 4
            axis = order[stage]
            behind = block_at(pos, order, stage, (pos[axis] + 3) % 4)
            ahead = block_at(pos, order, stage, (pos[axis] + 1) % 4)
            arrived(k, behind, base)
            move(k, behind + (half_of(stage, 0),), base + 2, beside(pos, axis, 1))
            if stage == 2:
                share(k, 3, 1)
            arrived(k, ahead, base + 1)
            move(k, ahead + (half_of(stage, 1),), base + 3, beside(pos, axis, 3))
            if stage == 2:
                share(k, 1, 2)
        for k in range(3):
            order, base = ORDERS[k], (k * 3 + stage) * 4
            axis = order[stage]
            across = block_at(pos, order, stage, (pos[axis] + 2) % 4)
            arrived(k, across + (half_of(stage, 0),), base + 2)
            arrived(k, across + (half_of(stage, 1),), base + 3)
            if stage == 2:
                share(k, 2, 3)
        small_value = small.finish(stage)
    small.start_pair(small_value)
    for k in range(3):
        for by, sem in ((0, 0), (3, 1), (1, 2), (2, 3)):
            arrived(k, (1 - pos["c"], (pos[ORDERS[k][2]] + by) % 4), 36 + k * 4 + sem)
    gain_out[...] = small.finish_pair()
    for copy in started:
        copy.wait_send()
    whole = (w_qkv, w_out, w_up, w_down)

    def unpack(group, carry):
        rows = pl.ds(pl.multiple_of(group * SLOT, SLOT), SLOT)
        for k in range(3):
            for tensor in range(2):
                held = jnp.concatenate(
                    [kept[k][index] for index in group_slots(k, group, tensor)], axis=0
                )
                sorted_rows = jnp.dot(
                    shuffle[...], held, preferred_element_type=jnp.float32
                ).astype(jnp.bfloat16)
                for piece in range(4):
                    which, column = column_of(k, tensor, piece)
                    whole[which][rows, pl.ds(column, WIDTH)] = sorted_rows[
                        piece * SLOT : (piece + 1) * SLOT
                    ]
        return carry

    lax.fori_loop(0, 16, unpack, 0)


def reduce_kernel(
    w_qkv, w_out, w_up, w_down, gain, shuffle, out_a, out_b, out_c, gain_out,
    r0, r1, r2, cores, halves3, fulls3, halves2, fulls2, half1a, half1b, fulls1,
    ring, pair, send, recv, small_send, small_recv,
):
    pos = place()
    kept = (r0, r1, r2)
    whole = (w_qkv, w_out, w_up, w_down)
    outs = (out_a, out_b, out_c)
    small = SmallSum(pos, ring, pair, small_send, small_recv)
    sibling = beside(pos, "c", 1)
    mine, other = pos["c"], 1 - pos["c"]

    def pack(group, carry):
        rows = pl.ds(pl.multiple_of(group * SLOT, SLOT), SLOT)
        for k in range(3):
            for tensor in range(2):
                held = jnp.concatenate(
                    [
                        whole[which][rows, pl.ds(column, WIDTH)]
                        for which, column in (column_of(k, tensor, piece) for piece in range(4))
                    ],
                    axis=0,
                )
                sorted_rows = jnp.dot(
                    shuffle[...], held, preferred_element_type=jnp.float32
                ).astype(jnp.bfloat16)
                for member, index in enumerate(group_slots(k, group, tensor)):
                    kept[k][index] = sorted_rows[member * SLOT : (member + 1) * SLOT]
        return carry

    lax.fori_loop(0, 16, pack, 0)
    greet_axes(pos)
    started = []

    def move(src, dst, sem, device):
        copy = remote(src, dst, send.at[sem], recv.at[sem], device)
        copy.start()
        started.append(copy)

    def arrived(dst, sem):
        remote(dst, dst, send.at[sem], recv.at[sem], sibling).wait_recv()

    def wide(value):
        return value.astype(jnp.float32)

    def add(target, index, sources, count):
        def body(i, carry):
            slot = (i // 4, i % 4) if count == 16 else (i,)
            total = wide(target[index + slot])
            for source, at in sources:
                total = total + wide(source[at + slot])
            target[index + slot] = total.astype(jnp.bfloat16)
            return carry

        lax.fori_loop(0, count, body, 0)

    small.start(0, gain[...])
    for by, sem in ((2, 0), (1, 1), (3, 2), (0, 3)):
        for k in range(3):
            index = (pos[ORDERS[k][2]] + by) % 4
            move(kept[k].at[other, index], cores.at[k, index], 36 + k * 4 + sem, sibling)

    def take_core(k, by, sem):
        index = (pos[ORDERS[k][2]] + by) % 4
        arrived(cores.at[k, index], 36 + k * 4 + sem)
        add(kept[k], (mine, index), [(cores, (k, index))], 16)

    for k in range(3):
        axis, base = ORDERS[k][2], k * 12
        across = (pos[axis] + 2) % 4
        take_core(k, 2, 0)
        move(
            kept[k].at[mine, across, pl.ds(0, 2)], halves3.at[k, 0], base, beside(pos, axis, 1)
        )
        move(
            kept[k].at[mine, across, pl.ds(2, 2)], halves3.at[k, 1], base + 1, beside(pos, axis, 3)
        )
    for k in range(3):
        take_core(k, 1, 1)
        take_core(k, 3, 2)
    for k in range(3):
        axis, base = ORDERS[k][2], k * 12
        for side, by in ((0, 1), (1, 3)):
            index = (pos[axis] + by) % 4
            arrived(halves3.at[k, side], base + side)

            def body(i, carry, k=k, side=side, index=index):
                a2, a1 = i // 4, i % 4
                at = (mine, index, 2 * side + a2, a1)
                kept[k][at] = (
                    wide(kept[k][at]) + wide(halves3[k, side, a2, a1])
                ).astype(jnp.bfloat16)
                return carry

            lax.fori_loop(0, 8, body, 0)
            move(
                kept[k].at[mine, index], fulls3.at[k, side], base + 2 + side, beside(pos, axis, by)
            )
    small_value = small.finish(0)
    small.start(1, small_value)
    for k in range(3):
        take_core(k, 0, 3)
    for k in range(3):
        axis3, axis, base = ORDERS[k][2], ORDERS[k][1], k * 12
        for side in range(2):
            arrived(fulls3.at[k, side], base + 2 + side)
        add(kept[k], (mine, pos[axis3]), [(fulls3, (k, 0)), (fulls3, (k, 1))], 16)
        across = (pos[axis] + 2) % 4
        for side, by in ((0, 1), (1, 3)):
            move(
                kept[k].at[mine, pos[axis3], across, pl.ds(2 * side, 2)],
                halves2.at[k, side],
                base + 4 + side,
                beside(pos, axis, by),
            )
    for k in range(3):
        axis3, axis, base = ORDERS[k][2], ORDERS[k][1], k * 12
        for side, by in ((0, 1), (1, 3)):
            index = (pos[axis] + by) % 4
            arrived(halves2.at[k, side], base + 4 + side)
            for a1 in range(2):
                at = (mine, pos[axis3], index, 2 * side + a1)
                kept[k][at] = (wide(kept[k][at]) + wide(halves2[k, side, a1])).astype(
                    jnp.bfloat16
                )
            move(
                kept[k].at[mine, pos[axis3], index],
                fulls2.at[k, side],
                base + 6 + side,
                beside(pos, axis, by),
            )
    small_value = small.finish(1)
    small.start(2, small_value)
    for k in range(3):
        axis3, axis2, axis, base = ORDERS[k][2], ORDERS[k][1], ORDERS[k][0], k * 12
        for side in range(2):
            arrived(fulls2.at[k, side], base + 6 + side)
        add(kept[k], (mine, pos[axis3], pos[axis2]), [(fulls2, (k, 0)), (fulls2, (k, 1))], 4)
        lead = (mine, pos[axis3], pos[axis2])
        across = (pos[axis] + 2) % 4
        move(
            kept[k].at[lead + (across, pl.ds(0, 32))], half1a.at[k], base + 8, beside(pos, axis, 1)
        )
        move(
            kept[k].at[lead + (across, pl.ds(32, 16))], half1b.at[k], base + 9, beside(pos, axis, 3)
        )
    for k in range(3):
        axis3, axis2, axis, base = ORDERS[k][2], ORDERS[k][1], ORDERS[k][0], k * 12
        lead = (mine, pos[axis3], pos[axis2])
        ahead, behind = lead + ((pos[axis] + 1) % 4,), lead + ((pos[axis] + 3) % 4,)
        arrived(half1a.at[k], base + 8)
        at = ahead + (pl.ds(0, 32),)
        kept[k][at] = (wide(kept[k][at]) + wide(half1a[k])).astype(jnp.bfloat16)
        move(kept[k].at[ahead], fulls1.at[k, 0], base + 10, beside(pos, axis, 1))
        arrived(half1b.at[k], base + 9)
        at = behind + (pl.ds(32, 16),)
        kept[k][at] = (wide(kept[k][at]) + wide(half1b[k])).astype(jnp.bfloat16)
        move(kept[k].at[behind], fulls1.at[k, 1], base + 11, beside(pos, axis, 3))
    small_value = small.finish(2)
    small.start_pair(small_value)
    for k in range(3):
        axis3, axis2, axis, base = ORDERS[k][2], ORDERS[k][1], ORDERS[k][0], k * 12
        for side in range(2):
            arrived(fulls1.at[k, side], base + 10 + side)
        outs[k][...] = (
            wide(kept[k][mine, pos[axis3], pos[axis2], pos[axis]])
            + wide(fulls1[k, 0])
            + wide(fulls1[k, 1])
        )
    gain_out[...] = small.finish_pair()
    for copy in started:
        copy.wait_send()


def shuffle_matrix():
    matrix = np.zeros((4 * SLOT, 4 * SLOT), np.float32)
    for piece in range(4):
        for member in range(4):
            for row in range(ROWS):
                matrix[piece * SLOT + member * ROWS + row, member * SLOT + piece * ROWS + row] = 1
    return matrix


def vmem_specs(count):
    return [pl.BlockSpec(memory_space=pltpu.VMEM)] * count


SMALL_SCRATCH = [
    pltpu.VMEM((3, 4, 8, 768), jnp.float32),
    pltpu.VMEM((2, 8, 768), jnp.float32),
]
BIG_SEMS = [pltpu.SemaphoreType.DMA((48,))] * 2
SMALL_SEMS = [pltpu.SemaphoreType.DMA((10,))] * 2
BUFFER = (2, 4, 4, 4, SLOT, WIDTH)


def gather_weights(shards, gain):
    low = jnp.bfloat16
    return pl.pallas_call(
        gather_kernel,
        name="gather_weights",
        out_shape=[
            jax.ShapeDtypeStruct((768, 2304), low),
            jax.ShapeDtypeStruct((768, 768), low),
            jax.ShapeDtypeStruct((768, 3072), low),
            jax.ShapeDtypeStruct((768, 3072), low),
            jax.ShapeDtypeStruct((8, 768), jnp.float32),
        ],
        in_specs=vmem_specs(5),
        out_specs=vmem_specs(5),
        scratch_shapes=[pltpu.VMEM(BUFFER, low)] * 3 + SMALL_SCRATCH + BIG_SEMS + SMALL_SEMS,
        compiler_params=pltpu.CompilerParams(
            collective_id=0, has_side_effects=True, vmem_limit_bytes=VMEM_BYTES
        ),
    )(*shards, gain, jnp.asarray(shuffle_matrix(), low))


def reduce_gradients(grads, gain):
    low = jnp.bfloat16
    return pl.pallas_call(
        reduce_kernel,
        name="reduce_gradients",
        out_shape=[jax.ShapeDtypeStruct((SLOT, WIDTH), jnp.float32)] * 3
        + [jax.ShapeDtypeStruct((8, 768), jnp.float32)],
        in_specs=vmem_specs(6),
        out_specs=vmem_specs(4),
        scratch_shapes=[pltpu.VMEM(BUFFER, low)] * 3
        + [
            pltpu.VMEM((3, 4, 4, 4, SLOT, WIDTH), low),
            pltpu.VMEM((3, 2, 2, 4, SLOT, WIDTH), low),
            pltpu.VMEM((3, 2, 4, 4, SLOT, WIDTH), low),
            pltpu.VMEM((3, 2, 2, SLOT, WIDTH), low),
            pltpu.VMEM((3, 2, 4, SLOT, WIDTH), low),
            pltpu.VMEM((3, 32, WIDTH), low),
            pltpu.VMEM((3, 16, WIDTH), low),
            pltpu.VMEM((3, 2, SLOT, WIDTH), low),
        ]
        + SMALL_SCRATCH
        + BIG_SEMS
        + SMALL_SEMS,
        compiler_params=pltpu.CompilerParams(
            collective_id=1, has_side_effects=True, vmem_limit_bytes=VMEM_BYTES
        ),
    )(*grads, gain, jnp.asarray(shuffle_matrix().T, low))


def head_place(head):
    member = head % 6
    return (member * 2) % 8 + (member // 4) * (1 + (member % 4) * 2), head // 6


def own_head(ctx, tensor):
    core, y = ctx % 2, ctx // 2
    return tensor * 6 + (1 - core) * y + core * (4 + y // 2), core * (y % 2) == 0


def greet_sequence(dp, number):
    barrier = pltpu.get_barrier_semaphore()

    def signal(i, carry):
        to = (number + i) % MEMBERS
        pl.semaphore_signal(
            barrier, inc=1, device_id=(dp, to // 2, to % 2), device_id_type=MESH
        )
        return carry

    lax.fori_loop(1, MEMBERS, signal, 0)
    pl.semaphore_wait(barrier, MEMBERS - 1)


def to_heads_kernel(src, dst, send, recv):
    dp, ctx, tensor = lax.axis_index("dp"), lax.axis_index("ctx"), lax.axis_index("tensor")
    number = 2 * ctx + tensor
    head, active = own_head(ctx, tensor)
    greet_sequence(dp, number)

    def out(i):
        to_head = (number + i) % HEADS
        to_ctx, to_tensor = head_place(to_head)
        local = 2 * to_ctx + to_tensor == number
        return local, to_head, (dp, to_ctx, to_tensor)

    def start(i, carry):
        local, to_head, device = out(i)

        @pl.when(local)
        def _():
            pltpu.make_async_copy(src.at[:, to_head], dst.at[number], recv.at[number]).start()

        @pl.when(jnp.logical_not(local))
        def _():
            remote(
                src.at[:, to_head], dst.at[number], send.at[to_head], recv.at[number], device
            ).start()

        return carry

    lax.fori_loop(0, HEADS, start, 0)

    @pl.when(active)
    def _():
        def wait(i, carry):
            @pl.when(i == number)
            def _():
                pltpu.make_async_copy(src.at[:, 0], dst.at[i], recv.at[i]).wait()

            @pl.when(i != number)
            def _():
                remote(
                    src.at[:, 0], dst.at[i], send.at[0], recv.at[i], (dp, i // 2, i % 2)
                ).wait_recv()

            return carry

        lax.fori_loop(0, MEMBERS, wait, 0)

    def sent(i, carry):
        local, to_head, device = out(i)

        @pl.when(jnp.logical_not(local))
        def _():
            remote(
                src.at[:, to_head], dst.at[number], send.at[to_head], recv.at[number], device
            ).wait_send()

        return carry

    lax.fori_loop(0, HEADS, sent, 0)


def from_heads_kernel(src, dst, send, recv):
    dp, ctx, tensor = lax.axis_index("dp"), lax.axis_index("ctx"), lax.axis_index("tensor")
    number = 2 * ctx + tensor
    head, active = own_head(ctx, tensor)
    greet_sequence(dp, number)

    @pl.when(active)
    def _():
        pltpu.make_async_copy(src.at[number], dst.at[:, head], recv.at[head]).start()

        def start(i, carry):
            to = (number + i) % MEMBERS
            remote(
                src.at[to], dst.at[:, head], send.at[to], recv.at[head], (dp, to // 2, to % 2)
            ).start()
            return carry

        lax.fori_loop(1, MEMBERS, start, 0)

    def wait(i, carry):
        from_ctx, from_tensor = head_place(i)
        local = 2 * from_ctx + from_tensor == number

        @pl.when(local)
        def _():
            pltpu.make_async_copy(src.at[0], dst.at[:, i], recv.at[i]).wait()

        @pl.when(jnp.logical_not(local))
        def _():
            remote(
                src.at[0], dst.at[:, i], send.at[0], recv.at[i], (dp, from_ctx, from_tensor)
            ).wait_recv()

        return carry

    lax.fori_loop(0, HEADS, wait, 0)

    @pl.when(active)
    def _():
        def sent(i, carry):
            to = (number + i) % MEMBERS
            remote(
                src.at[to], dst.at[:, head], send.at[to], recv.at[head], (dp, to // 2, to % 2)
            ).wait_send()
            return carry

        lax.fori_loop(1, MEMBERS, sent, 0)


def exchange(kernel, array, shape, name, number):
    return pl.pallas_call(
        kernel,
        name=name,
        out_shape=jax.ShapeDtypeStruct(shape, jnp.bfloat16),
        in_specs=[pl.BlockSpec(memory_space=pl.ANY)],
        out_specs=pl.BlockSpec(memory_space=pl.ANY),
        scratch_shapes=[pltpu.SemaphoreType.DMA((MEMBERS,))] * 2,
        compiler_params=pltpu.CompilerParams(collective_id=number, has_side_effects=True),
    )(array)


def to_heads(array, name, number):
    return exchange(
        to_heads_kernel, array, (MEMBERS, array.shape[0], HEAD_DIM, 256), name, number
    )


def from_heads(array, name, number):
    return exchange(
        from_heads_kernel, array, (array.shape[1], HEADS, HEAD_DIM, 256), name, number
    )


TILE = 512
TILES = 8


def turned(value):
    return jnp.transpose(value.astype(jnp.float32)).astype(jnp.bfloat16)


def allowed_tile():
    key = lax.broadcasted_iota(jnp.int32, (TILE, TILE), 0)
    query = lax.broadcasted_iota(jnp.int32, (TILE, TILE), 1)
    return query >= key


def two(ref, tile, *index):
    return jnp.concatenate([ref[(2 * tile,) + index], ref[(2 * tile + 1,) + index]], axis=1)


def dot(a, b):
    return jnp.dot(a, b, preferred_element_type=jnp.float32)


def dot_right(a, b):
    return lax.dot_general(a, b, (((1,), (1,)), ((), ())), preferred_element_type=jnp.float32)


def forward_kernel(parts, out, lse, keys):
    head, active = own_head(lax.axis_index("ctx"), lax.axis_index("tensor"))

    @pl.when(active)
    def _():
        def prepare(j, carry):
            keys[pl.ds(pl.multiple_of(j * TILE, TILE), TILE), :] = turned(two(parts, j, 1))
            return carry

        lax.fori_loop(0, TILES, prepare, 0)

        def tile_scores(j, query):
            return dot(keys[pl.ds(pl.multiple_of(j * TILE, TILE), TILE), :], query)

        def per_queries(i, carry):
            query = two(parts, i, 0) * jnp.bfloat16(HEAD_DIM ** -0.5)

            def step(scores, j, state):
                top, total, weighted = state
                new_top = jnp.maximum(top, jnp.max(scores, axis=0, keepdims=True))
                fade = jnp.exp(top - new_top)
                raised = jnp.exp(scores - new_top)
                total = total * fade + jnp.sum(raised, axis=0, keepdims=True)
                weighted = weighted * fade + dot(two(parts, j, 2), raised.astype(jnp.bfloat16))
                return new_top, total, weighted

            state = (
                jnp.full((1, TILE), neg_large, jnp.float32),
                jnp.zeros((1, TILE), jnp.float32),
                jnp.zeros((HEAD_DIM, TILE), jnp.float32),
            )
            state = lax.fori_loop(
                0, i, lambda j, state: step(tile_scores(j, query), j, state), state
            )
            masked = jnp.where(allowed_tile(), tile_scores(i, query), neg_large)
            top, total, weighted = step(masked, i, state)
            attended = (weighted / total).astype(jnp.bfloat16)
            out[2 * i, 0] = attended[:, :256]
            out[2 * i + 1, 0] = attended[:, 256:]
            lse[i] = top + jnp.log(total)
            return carry

        lax.fori_loop(0, TILES, per_queries, 0)


def backward_kernel(parts, attended, grad_att, lse, out, query_sum, delta):
    head, active = own_head(lax.axis_index("ctx"), lax.axis_index("tensor"))

    @pl.when(active)
    def _():
        def prepare(i, carry):
            delta[i] = jnp.sum(
                two(attended, i, 0).astype(jnp.float32) * two(grad_att, i, 0).astype(jnp.float32),
                axis=0,
                keepdims=True,
            )
            query_sum[i] = jnp.zeros((HEAD_DIM, TILE), jnp.float32)
            return carry

        lax.fori_loop(0, TILES, prepare, 0)

        def per_keys(j, carry):
            key_cols, value_cols = two(parts, j, 1), two(parts, j, 2)
            key_rows, value_rows = turned(key_cols), turned(value_cols)

            def step(i, state, diagonal):
                key_sum, value_sum = state
                query = two(parts, i, 0) * jnp.bfloat16(HEAD_DIM ** -0.5)
                grad = two(grad_att, i, 0)
                shares = jnp.exp(dot(key_rows, query) - lse[i])
                if diagonal:
                    shares = jnp.where(allowed_tile(), shares, 0.0)
                grad_scores = (shares * (dot(value_rows, grad) - delta[i])).astype(jnp.bfloat16)
                query_sum[i] += dot(key_cols, grad_scores)
                key_sum = key_sum + dot_right(query, grad_scores)
                value_sum = value_sum + dot_right(grad, shares.astype(jnp.bfloat16))
                return key_sum, value_sum

            zero = jnp.zeros((HEAD_DIM, TILE), jnp.float32)
            state = step(j, (zero, zero), True)
            key_sum, value_sum = lax.fori_loop(
                j + 1, TILES, lambda i, state: step(i, state, False), state
            )
            for part, total in ((1, key_sum), (2, value_sum)):
                total = total.astype(jnp.bfloat16)
                out[2 * j, part] = total[:, :256]
                out[2 * j + 1, part] = total[:, 256:]
            return carry

        lax.fori_loop(0, TILES, per_keys, 0)

        def finish(i, carry):
            total = (query_sum[i] * HEAD_DIM ** -0.5).astype(jnp.bfloat16)
            out[2 * i, 0] = total[:, :256]
            out[2 * i + 1, 0] = total[:, 256:]
            return carry

        lax.fori_loop(0, TILES, finish, 0)


def attend(parts):
    return pl.pallas_call(
        forward_kernel,
        name="attend",
        out_shape=[
            jax.ShapeDtypeStruct((MEMBERS, 1, HEAD_DIM, 256), jnp.bfloat16),
            jax.ShapeDtypeStruct((TILES, 1, TILE), jnp.float32),
        ],
        in_specs=vmem_specs(1),
        out_specs=vmem_specs(2),
        scratch_shapes=[pltpu.VMEM((TILES * TILE, HEAD_DIM), jnp.bfloat16)],
        compiler_params=pltpu.CompilerParams(vmem_limit_bytes=VMEM_BYTES),
    )(parts)


def attend_back(parts, attended, grad_att, lse):
    return pl.pallas_call(
        backward_kernel,
        name="attend_back",
        out_shape=jax.ShapeDtypeStruct((MEMBERS, 3, HEAD_DIM, 256), jnp.bfloat16),
        in_specs=vmem_specs(4),
        out_specs=vmem_specs(1)[0],
        scratch_shapes=[
            pltpu.VMEM((TILES, HEAD_DIM, TILE), jnp.float32),
            pltpu.VMEM((TILES, 1, TILE), jnp.float32),
        ],
        compiler_params=pltpu.CompilerParams(vmem_limit_bytes=VMEM_BYTES),
    )(parts, attended, grad_att, lse)


def normalize(values):
    center = values - jnp.mean(values, axis=-1, keepdims=True)
    inv_std = lax.rsqrt(jnp.mean(center * center, axis=-1, keepdims=True) + epsilon)
    return (center * inv_std, inv_std)


def norm_back(upstream, gain_row, normed, inv_std):
    scaled = upstream * gain_row
    return inv_std * (
        scaled
        - jnp.mean(scaled, axis=-1, keepdims=True)
        - normed * jnp.mean(scaled * normed, axis=-1, keepdims=True)
    )


def gelu_tanh(values):
    return jax.nn.gelu(values, approximate=True)


def multiply(form, left, right):
    return jnp.einsum(form, left, right, preferred_element_type=jnp.float32)


def per_device(tokens, cotangent, w_qkv, w_out, w_up, w_down, norm_gains):
    low = jnp.bfloat16
    owner = lax.axis_index("dp") * lax.axis_size("ctx") + lax.axis_index("ctx")
    shards = (
        jnp.concatenate([w_qkv, w_out.T[None]], axis=0).reshape(SLOT, WIDTH),
        w_up.reshape(ROWS, 4, WIDTH).transpose(1, 0, 2).reshape(SLOT, WIDTH),
        w_down.reshape(4, WIDTH, ROWS).transpose(0, 2, 1).reshape(SLOT, WIDTH),
    )
    gain_part = lax.dynamic_update_slice(
        jnp.zeros((8, 768), jnp.float32),
        0.5 * norm_gains.astype(jnp.float32),
        (jnp.int32(0), owner * ROWS),
    )
    qkv, out, up, down, gains = gather_weights(shards, gain_part)
    gain_one, gain_two = gains[0], gains[1]
    inputs = tokens.astype(jnp.float32)
    normed_one, inv_one = normalize(inputs)
    first_in = (normed_one * gain_one).astype(low)
    projected = multiply("dc,bd->cb", qkv, first_in).astype(low).reshape(3, HEADS, HEAD_DIM, 256)
    parts = to_heads(projected, "projections_to_heads", 2)
    head_out, lse = attend(parts)
    attended = from_heads(head_out, "attended_from_heads", 3).reshape(768, 256)
    middle = inputs + multiply("cb,dc->bd", attended, out)
    normed_two, inv_two = normalize(middle)
    second_in = (normed_two * gain_two).astype(low)
    hidden = multiply("bd,df->bf", second_in, up)
    activated, gelu_pull = jax.vjp(gelu_tanh, hidden)
    act_low = activated.astype(low)
    result = (middle + multiply("bf,df->bd", act_low, down)).astype(low)
    grad_down = multiply("bd,bf->df", cotangent, act_low).astype(low)
    grad_act = multiply("bd,df->bf", cotangent, down)
    grad_hidden = gelu_pull(grad_act)[0].astype(low)
    grad_up = multiply("bd,bf->df", second_in, grad_hidden).astype(low)
    grad_second = multiply("bf,df->bd", grad_hidden, up)
    grad_middle = cotangent.astype(jnp.float32) + norm_back(
        grad_second, gain_two, normed_two, inv_two
    )
    gain_two_term = jnp.sum(grad_second * normed_two, axis=0)
    mid_low = grad_middle.astype(low)
    grad_out = multiply("bd,cb->dc", mid_low, attended).astype(low)
    grad_att = multiply("bd,dc->cb", mid_low, out).astype(low).reshape(1, HEADS, HEAD_DIM, 256)
    head_grad = to_heads(grad_att, "gradients_to_heads", 4)
    head_back = attend_back(parts, head_out, head_grad, lse)
    grad_projected = from_heads(head_back, "gradients_from_heads", 5).reshape(2304, 256)
    grad_qkv = multiply("bd,cb->dc", first_in, grad_projected).astype(low)
    grad_first = multiply("cb,dc->bd", grad_projected, qkv)
    grad_tokens = grad_middle + norm_back(grad_first, gain_one, normed_one, inv_one)
    gain_one_term = jnp.sum(grad_first * normed_one, axis=0)
    gain_terms = jnp.concatenate(
        [gain_one_term[None], gain_two_term[None], jnp.zeros((6, 768), jnp.float32)]
    )
    sum_a, sum_b, sum_c, gain_sum = reduce_gradients(
        (grad_qkv, grad_out, grad_up, grad_down), gain_terms
    )
    sum_a = sum_a.reshape(4, ROWS, WIDTH)
    return (
        result,
        grad_tokens,
        sum_a[:3],
        sum_a[3].T,
        sum_b.reshape(4, ROWS, WIDTH).transpose(1, 0, 2).reshape(ROWS, 4 * WIDTH),
        sum_c.reshape(4, ROWS, WIDTH).transpose(0, 2, 1).reshape(4 * WIDTH, ROWS),
        lax.dynamic_slice(gain_sum, (jnp.int32(0), owner * ROWS), (2, ROWS)),
    )


def solution(mesh):
    return jax.shard_map(
        per_device,
        mesh=mesh,
        in_specs=(
            P(("dp", "ctx", "tensor"), None),
            P(("dp", "ctx", "tensor"), None),
            P(None, ("dp", "ctx"), "tensor"),
            P("tensor", ("dp", "ctx")),
            P(("dp", "ctx"), "tensor"),
            P("tensor", ("dp", "ctx")),
            P(None, ("dp", "ctx")),
        ),
        out_specs=(
            P(("dp", "ctx", "tensor"), None),
            P(("dp", "ctx", "tensor"), None),
            P(None, ("dp", "ctx"), "tensor"),
            P("tensor", ("dp", "ctx")),
            P(("dp", "ctx"), "tensor"),
            P("tensor", ("dp", "ctx")),
            P(None, ("dp", "ctx")),
        ),
        check_vma=False,
    )
```

```python
import functools

import jax
import jax.numpy as jnp
import numpy as np
from jax import lax
from jax.experimental import pallas as pl
from jax.experimental.pallas import tpu as pltpu
from jax.sharding import PartitionSpec as P

HEAD_DIM = 64
HEADS = 12
MEMBERS = 16
ROWS = 12
WIDTH = 384
SLOT = 4 * ROWS
THIRDS = (("z", "x", "y"), ("x", "y", "z"), ("y", "z", "x"))
WHOLES = (("z", "y", "x"), ("z", "x", "y"))
MESH = pl.DeviceIdType.MESH
VMEM_BYTES = 60 * 1024 * 1024
epsilon = 1e-05
neg_large = -1e30


def place():
    dp, ctx, tensor = lax.axis_index("dp"), lax.axis_index("ctx"), lax.axis_index("tensor")
    return dict(x=dp // 2, y=ctx // 2, z=2 * tensor + dp % 2, c=ctx % 2)


def device_at(pos, axis, index):
    at = dict(pos)
    at[axis] = index
    return (at["x"] * 2 + at["z"] % 2, at["y"] * 2 + at["c"], at["z"] // 2)


def beside(pos, axis, by):
    if axis == "c":
        return device_at(pos, "c", 1 - pos["c"])
    return device_at(pos, axis, (pos[axis] + by) % 4)


def greet(pos):
    barrier = pltpu.get_barrier_semaphore()
    dp, number = lax.axis_index("dp"), member_number()

    def signal(i, carry):
        to = (number + i) % MEMBERS
        pl.semaphore_signal(
            barrier, inc=1, device_id=(dp, to // 2, to % 2), device_id_type=MESH
        )
        return carry

    lax.fori_loop(1, MEMBERS, signal, 0)
    for axis, by in (("x", 1), ("x", 2), ("x", 3), ("z", 1), ("z", 3)):
        pl.semaphore_signal(barrier, inc=1, device_id=beside(pos, axis, by), device_id_type=MESH)
    pl.semaphore_wait(barrier, MEMBERS - 1 + 5)


def member_number():
    return 2 * lax.axis_index("ctx") + lax.axis_index("tensor")


def remote(src, dst, send, recv, device):
    return pltpu.make_async_remote_copy(
        src_ref=src,
        dst_ref=dst,
        send_sem=send,
        recv_sem=recv,
        device_id=device,
        device_id_type=MESH,
    )


class SmallSum:
    def __init__(self, pos, ring, pair, send, recv):
        self.pos, self.ring, self.pair, self.send, self.recv = pos, ring, pair, send, recv

    def copy(self, n, by, coming=False):
        axis = ("x", "y", "z")[n]
        slot = (self.pos[axis] + 4 - by) % 4 if coming else self.pos[axis]
        ref, sem = self.ring.at[n, slot], n * 3 + by - 1
        return remote(
            ref, ref, self.send.at[sem], self.recv.at[sem], beside(self.pos, axis, by)
        )

    def start(self, n, value):
        self.ring[n, self.pos[("x", "y", "z")[n]]] = value
        for by in (1, 2, 3):
            self.copy(n, by).start()

    def finish(self, n):
        for by in (1, 2, 3):
            self.copy(n, by, coming=True).wait_recv()
            self.copy(n, by).wait_send()
        return (self.ring[n, 0] + self.ring[n, 1]) + (self.ring[n, 2] + self.ring[n, 3])

    def pair_copy(self, slot):
        ref = self.pair.at[slot]
        return remote(ref, ref, self.send.at[9], self.recv.at[9], beside(self.pos, "c", 1))

    def start_pair(self, value):
        self.pair[self.pos["c"]] = value
        self.pair_copy(self.pos["c"]).start()

    def finish_pair(self):
        self.pair_copy(1 - self.pos["c"]).wait_recv()
        self.pair_copy(self.pos["c"]).wait_send()
        return self.pair[0] + self.pair[1]


class Group:
    def __init__(self, pos, send, recv):
        self.pos, self.send, self.recv = pos, send, recv
        self.member = (pos["y"] % 2) * 2 + pos["c"]
        y = pos["y"] + 1 - 2 * (pos["y"] % 2)
        c = 1 - pos["c"]
        self.partners = []
        for to_y, to_c in ((pos["y"], c), (y, pos["c"]), (y, c)):
            device = device_at({**pos, "y": to_y}, "c", to_c)
            self.partners.append((device, (to_y % 2) * 2 + to_c))

    def copy(self, held, k, i, coming=False):
        device, member = self.partners[i]
        ref = held.at[k, member if coming else self.member]
        return remote(ref, ref, self.send.at[k * 3 + i], self.recv.at[k * 3 + i], device)

    def start(self, held, k):
        for i in range(3):
            self.copy(held, k, i).start()

    def finish(self, held, k):
        for i in range(3):
            self.copy(held, k, i, coming=True).wait_recv()
        return jnp.concatenate([held[k, member] for member in range(4)], axis=0)

    def sent(self, held, k):
        for i in range(3):
            self.copy(held, k, i).wait_send()


class Unit:
    def __init__(self, pos, order, unit, send, recv, started):
        self.pos, self.order, self.unit = pos, order, unit
        self.send, self.recv, self.started = send, recv, started
        self.sibling = beside(pos, "c", 1)

    def move(self, src, dst, sem, device):
        sem = self.unit * 16 + sem
        copy = remote(src, dst, self.send.at[sem], self.recv.at[sem], device)
        copy.start()
        self.started.append(copy)

    def arrived(self, dst, sem):
        sem = self.unit * 16 + sem
        remote(dst, dst, self.send.at[sem], self.recv.at[sem], self.sibling).wait_recv()

    def along(self, stage, by):
        return beside(self.pos, self.order[stage], by)

    def at(self, stage, by):
        index = ((self.pos[self.order[stage]] + by) % 4,)
        for later in range(stage + 1, 3):
            index = (self.pos[self.order[later]],) + index
        return (self.unit, self.pos["c"]) + index


class Gather(Unit):
    def __init__(self, pos, order, unit, held, send, recv, started):
        super().__init__(pos, order, unit, send, recv, started)
        self.held = held

    def halves(self, stage, which):
        return () if stage == 0 else (pl.ds(2 * which, 2),)

    def pass_on(self, index, sem, device):
        self.move(self.held.at[index], self.held.at[index], sem, device)

    def begin(self, stage):
        for side, by in ((0, 1), (1, 3)):
            self.pass_on(self.at(stage, 0), stage * 4 + side, self.along(stage, by))
        if stage == 2:
            self.share(0, 12)

    def relay(self, stage):
        for side, by, back in ((0, 1, 3), (1, 3, 1)):
            block = self.at(stage, back)
            self.arrived(self.held.at[block], stage * 4 + side)
            if stage > 0 or side == 0:
                self.pass_on(
                    block + self.halves(stage, side), stage * 4 + 2 + side, self.along(stage, by)
                )
            if stage == 2:
                self.share(back, 13 + side)

    def finish(self, stage):
        for side in range(2):
            if stage > 0 or side == 0:
                block = self.at(stage, 2) + self.halves(stage, side)
                self.arrived(self.held.at[block], stage * 4 + 2 + side)
        if stage == 2:
            self.share(2, 15)

    def share(self, by, sem):
        self.pass_on(self.at(2, by), sem, self.sibling)

    def settle(self):
        place3 = self.pos[self.order[2]]
        for by, sem in ((0, 12), (3, 13), (1, 14), (2, 15)):
            index = (self.unit, 1 - self.pos["c"], (place3 + by) % 4)
            self.arrived(self.held.at[index], sem)


def wide(value):
    return value.astype(jnp.float32)


class Reduce(Unit):
    def __init__(self, pos, order, unit, held, landing, send, recv, started):
        super().__init__(pos, order, unit, send, recv, started)
        self.held = held
        self.cores, self.halves3, self.fulls3, self.halves2, self.fulls2, self.half1, self.fulls1 = (
            landing
        )

    def add(self, index, sources, *counts):
        held = self.held
        if not counts:
            total = wide(held[index])
            for source, at in sources:
                total = total + wide(source[at])
            held[index] = total.astype(jnp.bfloat16)
            return

        def body(i, carry):
            slot = (i // counts[1], i % counts[1]) if len(counts) == 2 else (i,)
            total = wide(held[index + slot])
            for source, at in sources:
                total = total + wide(source[at + slot])
            held[index + slot] = total.astype(jnp.bfloat16)
            return carry

        lax.fori_loop(0, counts[0] * counts[-1] if len(counts) == 2 else counts[0], body, 0)

    def cross(self):
        place3, u = self.pos[self.order[2]], self.unit
        for by, sem in ((2, 12), (1, 13), (3, 14), (0, 15)):
            index = (place3 + by) % 4
            self.move(
                self.held.at[u, 1 - self.pos["c"], index], self.cores.at[u, index], sem, self.sibling
            )

    def take_core(self, by, sem):
        index = (self.pos[self.order[2]] + by) % 4
        self.arrived(self.cores.at[self.unit, index], sem)
        self.add(self.at(2, by), [(self.cores, (self.unit, index))], 4, 4)

    def begin(self, stage):
        u = self.unit
        if stage == 2:
            self.take_core(2, 12)
        if stage == 0:
            self.move(self.held.at[self.at(0, 2)], self.half1.at[u], 8, self.along(0, 1))
            self.move(self.held.at[self.at(0, 3)], self.fulls1.at[u, 1], 11, self.along(0, 3))
            return
        landing = self.halves3 if stage == 2 else self.halves2
        for side, by in ((0, 1), (1, 3)):
            self.move(
                self.held.at[self.at(stage, 2) + (pl.ds(2 * side, 2),)],
                landing.at[u, side],
                (2 - stage) * 4 + side,
                self.along(stage, by),
            )
        if stage == 2:
            self.take_core(1, 13)
            self.take_core(3, 14)

    def relay(self, stage):
        u = self.unit
        if stage == 0:
            self.arrived(self.half1.at[u], 8)
            self.add(self.at(0, 1), [(self.half1, (u,))])
            self.move(self.held.at[self.at(0, 1)], self.fulls1.at[u, 0], 10, self.along(0, 1))
            return
        halves = self.halves3 if stage == 2 else self.halves2
        fulls = self.fulls3 if stage == 2 else self.fulls2
        base = (2 - stage) * 4
        for side, by in ((0, 1), (1, 3)):
            self.arrived(halves.at[u, side], base + side)
            index = self.at(stage, by)
            for row in range(2):
                if stage == 2:
                    self.add(index + (2 * side + row,), [(halves, (u, side, row))], 4)
                else:
                    self.add(index + (2 * side + row,), [(halves, (u, side, row))])
            self.move(
                self.held.at[index], fulls.at[u, side], base + 2 + side, self.along(stage, by)
            )

    def finish(self, stage):
        u = self.unit
        if stage == 2:
            self.take_core(0, 15)
        fulls = (self.fulls1, self.fulls2, self.fulls3)[stage]
        for side in range(2):
            self.arrived(fulls.at[u, side], (2 - stage) * 4 + 2 + side)
        self.add(
            self.at(stage, 0),
            [(fulls, (u, 0)), (fulls, (u, 1))],
            *((), (4,), (4, 4))[stage],
        )


def landing_scratch(units, rows):
    low, slot = jnp.bfloat16, (rows, WIDTH)
    return [
        pltpu.VMEM((units, 4, 4, 4) + slot, low),
        pltpu.VMEM((units, 2, 2, 4) + slot, low),
        pltpu.VMEM((units, 2, 4, 4) + slot, low),
        pltpu.VMEM((units, 2, 2) + slot, low),
        pltpu.VMEM((units, 2, 4) + slot, low),
        pltpu.VMEM((units,) + slot, low),
        pltpu.VMEM((units, 2) + slot, low),
    ]


def slots_of(group, orders):
    x, z_lo, y_half = group // 4, (group // 2) % 2, group % 2
    for tensor in range(2):
        for piece in range(4):
            at = dict(x=x, z=2 * tensor + z_lo, y=2 * y_half + piece // 2)
            yield tensor, piece, [
                (piece % 2, at[order[2]], at[order[1]], at[order[0]]) for order in orders
            ]


def column_of(tensor, piece):
    return (0, (piece * 2 + tensor) * WIDTH) if piece < 3 else (1, tensor * WIDTH)


def copy_thirds(thirds, whole, to_whole):
    def body(group, carry):
        for tensor, piece, indices in slots_of(group, THIRDS):
            which, column = column_of(tensor, piece)
            for third, index in enumerate(indices):
                rows = pl.ds(pl.multiple_of(group * SLOT + 16 * third, 16), 16)
                if to_whole:
                    whole[which][rows, pl.ds(column, WIDTH)] = thirds[(third,) + index]
                else:
                    thirds[(third,) + index] = whole[which][rows, pl.ds(column, WIDTH)]
        return carry

    lax.fori_loop(0, 16, body, 0)


def copy_wholes(slots, whole, to_whole):
    def body(group, carry):
        rows = pl.ds(pl.multiple_of(group * SLOT, SLOT), SLOT)
        for tensor, piece, indices in slots_of(group, WHOLES):
            columns = pl.ds((tensor * 4 + piece) * WIDTH, WIDTH)
            for k, index in enumerate(indices):
                if to_whole:
                    whole[k][rows, columns] = slots[(k,) + index]
                else:
                    slots[(k,) + index] = whole[k][rows, columns]
        return carry

    lax.fori_loop(0, 16, body, 0)


def head_place(head):
    member = head % 6
    return (member * 2) % 8 + (member // 4) * (1 + (member % 4) * 2), head // 6


def own_head(ctx, tensor):
    core, y = ctx % 2, ctx // 2
    return tensor * 6 + (1 - core) * y + core * (4 + y // 2), core * (y % 2) == 0


class ToHeads:
    def __init__(self, src, dst, send, recv):
        self.src, self.dst, self.send, self.recv = src, dst, send, recv
        self.dp, self.number = lax.axis_index("dp"), member_number()

    def copies(self, i):
        head = (self.number + i) % HEADS
        ctx, tensor = head_place(head)
        local = 2 * ctx + tensor == self.number
        src, dst = self.src.at[:, head], self.dst.at[self.number]
        recv = self.recv.at[self.number]
        return (
            local,
            lambda: pltpu.make_async_copy(src, dst, recv),
            lambda: remote(src, dst, self.send.at[head], recv, (self.dp, ctx, tensor)),
        )

    def start(self):
        def body(i, carry):
            local, inside, outside = self.copies(i)

            @pl.when(local)
            def _():
                inside().start()

            @pl.when(jnp.logical_not(local))
            def _():
                outside().start()

            return carry

        lax.fori_loop(0, HEADS, body, 0)

    def wait(self, first, last):
        def body(i, carry):
            src, dst, recv = self.src.at[:, 0], self.dst.at[i], self.recv.at[i]

            @pl.when(i == self.number)
            def _():
                pltpu.make_async_copy(src, dst, recv).wait()

            @pl.when(i != self.number)
            def _():
                remote(src, dst, self.send.at[0], recv, (self.dp, i // 2, i % 2)).wait_recv()

            return carry

        lax.fori_loop(first, last, body, 0)

    def sent(self):
        def body(i, carry):
            local, inside, outside = self.copies(i)

            @pl.when(jnp.logical_not(local))
            def _():
                outside().wait_send()

            return carry

        lax.fori_loop(0, HEADS, body, 0)


class FromHeads:
    def __init__(self, src, dst, send, recv):
        self.src, self.dst, self.send, self.recv = src, dst, send, recv
        self.dp, self.number = lax.axis_index("dp"), member_number()
        self.head = own_head(lax.axis_index("ctx"), lax.axis_index("tensor"))[0]

    def outside(self, to):
        return remote(
            self.src.at[to],
            self.dst.at[:, self.head],
            self.send.at[to],
            self.recv.at[self.head],
            (self.dp, to // 2, to % 2),
        )

    def start(self, to):
        @pl.when(to == self.number)
        def _():
            pltpu.make_async_copy(
                self.src.at[to], self.dst.at[:, self.head], self.recv.at[self.head]
            ).start()

        @pl.when(to != self.number)
        def _():
            self.outside(to).start()

    def wait(self):
        def body(i, carry):
            ctx, tensor = head_place(i)
            local = 2 * ctx + tensor == self.number
            src, dst, recv = self.src.at[0], self.dst.at[:, i], self.recv.at[i]

            @pl.when(local)
            def _():
                pltpu.make_async_copy(src, dst, recv).wait()

            @pl.when(jnp.logical_not(local))
            def _():
                remote(src, dst, self.send.at[0], recv, (self.dp, ctx, tensor)).wait_recv()

            return carry

        lax.fori_loop(0, HEADS, body, 0)

    def sent(self):
        def body(i, carry):
            self.outside((self.number + i) % MEMBERS).wait_send()
            return carry

        lax.fori_loop(1, MEMBERS, body, 0)


TILE = 512
TILES = 8


def turned(value):
    return jnp.transpose(value.astype(jnp.float32)).astype(jnp.bfloat16)


def allowed_tile():
    key = lax.broadcasted_iota(jnp.int32, (TILE, TILE), 0)
    query = lax.broadcasted_iota(jnp.int32, (TILE, TILE), 1)
    return query >= key


def two(ref, tile, *index):
    return jnp.concatenate([ref[(2 * tile,) + index], ref[(2 * tile + 1,) + index]], axis=1)


def put_two(ref, tile, part, value):
    ref[2 * tile, part] = value[:, :256]
    ref[2 * tile + 1, part] = value[:, 256:]


def dot(a, b):
    return jnp.dot(a, b, preferred_element_type=jnp.float32)


def dot_right(a, b):
    return lax.dot_general(a, b, (((1,), (1,)), ((), ())), preferred_element_type=jnp.float32)


def attend_tile(i, parts, keys, out, lse):
    own_rows = pl.ds(pl.multiple_of(i * TILE, TILE), TILE)
    keys[own_rows, :] = turned(two(parts, i, 1))
    query = two(parts, i, 0) * jnp.bfloat16(HEAD_DIM ** -0.5)

    def step(scores, j, state):
        top, total, weighted = state
        new_top = jnp.maximum(top, jnp.max(scores, axis=0, keepdims=True))
        fade = jnp.exp(top - new_top)
        raised = jnp.exp(scores - new_top)
        total = total * fade + jnp.sum(raised, axis=0, keepdims=True)
        weighted = weighted * fade + dot(two(parts, j, 2), raised.astype(jnp.bfloat16))
        return new_top, total, weighted

    def before(j, state):
        return step(dot(keys[pl.ds(pl.multiple_of(j * TILE, TILE), TILE), :], query), j, state)

    state = (
        jnp.full((1, TILE), neg_large, jnp.float32),
        jnp.zeros((1, TILE), jnp.float32),
        jnp.zeros((HEAD_DIM, TILE), jnp.float32),
    )
    state = lax.fori_loop(0, i, before, state)
    masked = jnp.where(allowed_tile(), dot(keys[own_rows, :], query), neg_large)
    top, total, weighted = step(masked, i, state)
    put_two(out, i, 0, (weighted / total).astype(jnp.bfloat16))
    lse[i] = top + jnp.log(total)


def forward_kernel(
    tokens, a, b, c, gain, shuffle,
    normed_out, inv_out, first_out, parts, head_out, lse, attended, gain_out,
    w_qkv, w_out, w_up, w_down,
    pre, thirds, wholes, qkv, out, up, down, projected, keys, ring, pair,
    third_send, third_recv, whole_send, whole_recv, pre_send, pre_recv, small_send, small_recv,
    to_send, to_recv, from_send, from_recv, write_sem,
):
    pos = place()
    active = own_head(lax.axis_index("ctx"), lax.axis_index("tensor"))[1]
    group = Group(pos, pre_send, pre_recv)
    small = SmallSum(pos, ring, pair, small_send, small_recv)
    started = []
    first = [
        Gather(pos, order, u, thirds, third_send, third_recv, started)
        for u, order in enumerate(THIRDS)
    ]
    later = [
        Gather(pos, order, u, wholes, whole_send, whole_recv, started)
        for u, order in enumerate(WHOLES)
    ]
    spread = ToHeads(projected, parts, to_send, to_recv)
    back = FromHeads(head_out, attended, from_send, from_recv)
    for k, shard in enumerate((a, b, c)):
        pre[k, group.member] = shard[...]
    greet(pos)
    for k in range(3):
        group.start(pre, k)
    small.start(0, gain[...])

    def sorted_piece(k):
        return dot(shuffle[group.member], group.finish(pre, k)).astype(jnp.bfloat16)

    piece = sorted_piece(0)
    for u, unit in enumerate(first):
        thirds[unit.at(0, 0)] = piece[16 * u : 16 * (u + 1)]
        unit.begin(0)
    for u, unit in enumerate(later):
        wholes[unit.at(0, 0)] = sorted_piece(1 + u)
    values = tokens[...].astype(jnp.float32)
    center = values - jnp.mean(values, axis=-1, keepdims=True)
    inv_std = lax.rsqrt(jnp.mean(center * center, axis=-1, keepdims=True) + epsilon)
    normed_out[...] = center * inv_std
    inv_out[...] = inv_std
    for stage in range(3):
        for unit in first:
            unit.relay(stage)
        if stage == 1:
            for unit in later:
                unit.begin(0)
        for unit in first:
            unit.finish(stage)
        if stage < 2:
            for unit in first:
                unit.begin(stage + 1)
        total = small.finish(stage)
        if stage < 2:
            small.start(stage + 1, total)
        else:
            small.start_pair(total)
    for unit in later:
        unit.relay(0)
    for unit in later:
        unit.finish(0)
        unit.begin(1)
    for unit in first:
        unit.settle()
    copy_thirds(thirds, (qkv, out), True)
    writes = [
        pltpu.make_async_copy(src, dst, write_sem.at[n])
        for n, (src, dst) in enumerate(((qkv, w_qkv), (out, w_out), (up, w_up), (down, w_down)))
    ]
    writes[0].start()
    writes[1].start()
    gains = small.finish_pair()
    gain_out[...] = gains
    first_in = (normed_out[...] * gains[0:1]).astype(jnp.bfloat16)
    first_out[...] = first_in
    for part in range(3):
        for tensor in range(2):
            column = (part * 2 + tensor) * WIDTH
            cols = jnp.transpose(dot(first_in, qkv[:, pl.ds(column, WIDTH)])).astype(jnp.bfloat16)
            for head in range(6):
                projected[part, tensor * 6 + head] = cols[head * HEAD_DIM : (head + 1) * HEAD_DIM]
    spread.start()
    for unit in later:
        unit.relay(1)
    for unit in later:
        unit.finish(1)
        unit.begin(2)

    def per_queries(i, carry):
        @pl.when(active)
        def _():
            spread.wait(2 * i, 2 * i + 2)
            attend_tile(i, parts, keys, head_out, lse)
            back.start(2 * i)
            back.start(2 * i + 1)

        return carry

    lax.fori_loop(0, 5, per_queries, 0)
    for unit in later:
        unit.relay(2)
    lax.fori_loop(5, 7, per_queries, 0)
    for unit in later:
        unit.finish(2)
    lax.fori_loop(7, 8, per_queries, 0)
    for unit in later:
        unit.settle()
    copy_wholes(wholes, (up, down), True)
    writes[2].start()
    writes[3].start()
    back.wait()
    spread.sent()

    @pl.when(active)
    def _():
        back.sent()

    for k in range(3):
        group.sent(pre, k)
    for copy in started:
        copy.wait_send()
    for write in writes:
        write.wait()


def back_tile(j, parts, grad_att, lse, delta, query_sum, out):
    key_cols, value_cols = two(parts, j, 1), two(parts, j, 2)
    key_rows, value_rows = turned(key_cols), turned(value_cols)

    def step(i, state, diagonal):
        key_sum, value_sum = state
        query = two(parts, i, 0) * jnp.bfloat16(HEAD_DIM ** -0.5)
        grad = two(grad_att, i, 0)
        shares = jnp.exp(dot(key_rows, query) - lse[i])
        if diagonal:
            shares = jnp.where(allowed_tile(), shares, 0.0)
        grad_scores = (shares * (dot(value_rows, grad) - delta[i])).astype(jnp.bfloat16)
        query_sum[i] += dot(key_cols, grad_scores)
        key_sum = key_sum + dot_right(query, grad_scores)
        value_sum = value_sum + dot_right(grad, shares.astype(jnp.bfloat16))
        return key_sum, value_sum

    zero = jnp.zeros((HEAD_DIM, TILE), jnp.float32)
    state = step(j, (zero, zero), True)
    key_sum, value_sum = lax.fori_loop(
        j + 1, TILES, lambda i, state: step(i, state, False), state
    )
    put_two(out, j, 0, (query_sum[j] * HEAD_DIM ** -0.5).astype(jnp.bfloat16))
    put_two(out, j, 1, key_sum.astype(jnp.bfloat16))
    put_two(out, j, 2, value_sum.astype(jnp.bfloat16))


def backward_kernel(
    grad_att, parts, head_out, lse, grad_up, grad_down, unshuffle,
    grad_projected, out_b, out_c,
    head_grad, head_back, query_sum, delta, wholes, post,
    cores, halves3, fulls3, halves2, fulls2, half1, fulls1,
    whole_send, whole_recv, post_send, post_recv, to_send, to_recv, from_send, from_recv,
):
    pos = place()
    active = own_head(lax.axis_index("ctx"), lax.axis_index("tensor"))[1]
    group = Group(pos, post_send, post_recv)
    started = []
    landing = (cores, halves3, fulls3, halves2, fulls2, half1, fulls1)
    units = [
        Reduce(pos, order, u, wholes, landing, whole_send, whole_recv, started)
        for u, order in enumerate(WHOLES)
    ]
    spread = ToHeads(grad_att, head_grad, to_send, to_recv)
    back = FromHeads(head_back, grad_projected, from_send, from_recv)
    greet(pos)
    spread.start()
    copy_wholes(wholes, (grad_up, grad_down), False)
    for unit in units:
        unit.cross()
    for unit in units:
        unit.begin(2)

    @pl.when(active)
    def _():
        spread.wait(0, MEMBERS)

        def prepare(i, carry):
            delta[i] = jnp.sum(
                wide(two(head_out, i, 0)) * wide(two(head_grad, i, 0)), axis=0, keepdims=True
            )
            query_sum[i] = jnp.zeros((HEAD_DIM, TILE), jnp.float32)
            return carry

        lax.fori_loop(0, TILES, prepare, 0)

    def per_keys(j, carry):
        @pl.when(active)
        def _():
            back_tile(j, parts, head_grad, lse, delta, query_sum, head_back)
            back.start(2 * j)
            back.start(2 * j + 1)

        return carry

    lax.fori_loop(0, 1, per_keys, 0)
    for unit in units:
        unit.relay(2)
    lax.fori_loop(1, 3, per_keys, 0)
    for unit in units:
        unit.finish(2)
        unit.begin(1)
    lax.fori_loop(3, 4, per_keys, 0)
    for unit in units:
        unit.relay(1)
    lax.fori_loop(4, 5, per_keys, 0)
    for unit in units:
        unit.finish(1)
        unit.begin(0)
    lax.fori_loop(5, 6, per_keys, 0)
    for unit in units:
        unit.relay(0)
    lax.fori_loop(6, 7, per_keys, 0)
    for u, unit in enumerate(units):
        unit.finish(0)
        post[u, group.member] = wholes[unit.at(0, 0)]
        group.start(post, u)
    lax.fori_loop(7, 8, per_keys, 0)
    for u, out in enumerate((out_b, out_c)):
        out[...] = dot(unshuffle[group.member], group.finish(post, u))
        group.sent(post, u)
    back.wait()
    spread.sent()

    @pl.when(active)
    def _():
        back.sent()

    for copy in started:
        copy.wait_send()


def reduce_kernel(
    grad_qkv, grad_out, gain, unshuffle, out_a, gain_out,
    thirds, post, cores, halves3, fulls3, halves2, fulls2, half1, fulls1, ring, pair,
    third_send, third_recv, post_send, post_recv, small_send, small_recv,
):
    pos = place()
    group = Group(pos, post_send, post_recv)
    small = SmallSum(pos, ring, pair, small_send, small_recv)
    started = []
    landing = (cores, halves3, fulls3, halves2, fulls2, half1, fulls1)
    units = [
        Reduce(pos, order, u, thirds, landing, third_send, third_recv, started)
        for u, order in enumerate(THIRDS)
    ]
    copy_thirds(thirds, (grad_qkv, grad_out), False)
    greet(pos)
    for unit in units:
        unit.cross()
    small.start(0, gain[...])
    for stage in (2, 1, 0):
        for unit in units:
            unit.begin(stage)
        for unit in units:
            unit.relay(stage)
        total = small.finish(2 - stage)
        if stage > 0:
            small.start(3 - stage, total)
        else:
            small.start_pair(total)
        for unit in units:
            unit.finish(stage)
    for u, unit in enumerate(units):
        post[0, group.member, pl.ds(16 * u, 16)] = thirds[unit.at(0, 0)]
    group.start(post, 0)
    gain_out[...] = small.finish_pair()
    out_a[...] = dot(unshuffle[group.member], group.finish(post, 0))
    group.sent(post, 0)
    for copy in started:
        copy.wait_send()


def shuffle_matrix():
    matrix = np.zeros((4, SLOT, 4 * SLOT), np.float32)
    for piece in range(4):
        for member in range(4):
            for row in range(ROWS):
                matrix[piece, member * ROWS + row, member * SLOT + piece * ROWS + row] = 1
    return jnp.asarray(matrix, jnp.bfloat16)


def unshuffle_matrix():
    matrix = np.zeros((4, SLOT, 4 * SLOT), np.float32)
    for member in range(4):
        for piece in range(4):
            for row in range(ROWS):
                matrix[member, piece * ROWS + row, piece * SLOT + member * ROWS + row] = 1
    return jnp.asarray(matrix, jnp.bfloat16)


def vmem_specs(count):
    return [pl.BlockSpec(memory_space=pltpu.VMEM)] * count


def any_specs(count):
    return [pl.BlockSpec(memory_space=pl.ANY)] * count


def sems(count):
    return [pltpu.SemaphoreType.DMA((count,))] * 2


def low_array(*shape):
    return jax.ShapeDtypeStruct(shape, jnp.bfloat16)


def wide_array(*shape):
    return jax.ShapeDtypeStruct(shape, jnp.float32)


SMALL_SCRATCH = [
    pltpu.VMEM((3, 4, 8, 768), jnp.float32),
    pltpu.VMEM((2, 8, 768), jnp.float32),
]


def kernel_params(number):
    return pltpu.CompilerParams(
        collective_id=number, has_side_effects=True, vmem_limit_bytes=VMEM_BYTES
    )


def forward_attention(tokens, shards, gain):
    low = jnp.bfloat16
    return pl.pallas_call(
        forward_kernel,
        name="forward_attention",
        out_shape=[
            wide_array(256, 768),
            wide_array(256, 1),
            low_array(256, 768),
            low_array(MEMBERS, 3, HEAD_DIM, 256),
            low_array(MEMBERS, 1, HEAD_DIM, 256),
            wide_array(TILES, 1, TILE),
            low_array(1, HEADS, HEAD_DIM, 256),
            wide_array(8, 768),
            low_array(768, 2304),
            low_array(768, 768),
            low_array(768, 3072),
            low_array(768, 3072),
        ],
        in_specs=vmem_specs(6),
        out_specs=vmem_specs(8) + any_specs(4),
        scratch_shapes=[
            pltpu.VMEM((3, 4, SLOT, WIDTH), low),
            pltpu.VMEM((3, 2, 4, 4, 4, 16, WIDTH), low),
            pltpu.VMEM((2, 2, 4, 4, 4, SLOT, WIDTH), low),
            pltpu.VMEM((768, 2304), low),
            pltpu.VMEM((768, 768), low),
            pltpu.VMEM((768, 3072), low),
            pltpu.VMEM((768, 3072), low),
            pltpu.VMEM((3, HEADS, HEAD_DIM, 256), low),
            pltpu.VMEM((TILES * TILE, HEAD_DIM), low),
        ]
        + SMALL_SCRATCH
        + sems(48)
        + sems(32)
        + sems(9)
        + sems(10)
        + sems(MEMBERS)
        + sems(MEMBERS)
        + [pltpu.SemaphoreType.DMA((4,))],
        compiler_params=kernel_params(0),
    )(tokens, *shards, gain, shuffle_matrix())


def backward_attention(grad_att, parts, head_out, lse, grad_up, grad_down, unshuffle):
    low = jnp.bfloat16
    return pl.pallas_call(
        backward_kernel,
        name="backward_attention",
        out_shape=[
            low_array(3, HEADS, HEAD_DIM, 256),
            wide_array(SLOT, WIDTH),
            wide_array(SLOT, WIDTH),
        ],
        in_specs=vmem_specs(7),
        out_specs=vmem_specs(3),
        scratch_shapes=[
            pltpu.VMEM((MEMBERS, 1, HEAD_DIM, 256), low),
            pltpu.VMEM((MEMBERS, 3, HEAD_DIM, 256), low),
            pltpu.VMEM((TILES, HEAD_DIM, TILE), jnp.float32),
            pltpu.VMEM((TILES, 1, TILE), jnp.float32),
            pltpu.VMEM((2, 2, 4, 4, 4, SLOT, WIDTH), low),
            pltpu.VMEM((2, 4, SLOT, WIDTH), low),
        ]
        + landing_scratch(2, SLOT)
        + sems(32)
        + sems(6)
        + sems(MEMBERS)
        + sems(MEMBERS),
        compiler_params=kernel_params(1),
    )(grad_att, parts, head_out, lse, grad_up, grad_down, unshuffle)


def reduce_projections(grad_qkv, grad_out, gain, unshuffle):
    low = jnp.bfloat16
    return pl.pallas_call(
        reduce_kernel,
        name="reduce_projections",
        out_shape=[wide_array(SLOT, WIDTH), wide_array(8, 768)],
        in_specs=vmem_specs(4),
        out_specs=vmem_specs(2),
        scratch_shapes=[
            pltpu.VMEM((3, 2, 4, 4, 4, 16, WIDTH), low),
            pltpu.VMEM((1, 4, SLOT, WIDTH), low),
        ]
        + landing_scratch(3, 16)
        + SMALL_SCRATCH
        + sems(48)
        + sems(3)
        + sems(10),
        compiler_params=kernel_params(2),
    )(grad_qkv, grad_out, gain, unshuffle)


def normalize(values):
    center = values - jnp.mean(values, axis=-1, keepdims=True)
    inv_std = lax.rsqrt(jnp.mean(center * center, axis=-1, keepdims=True) + epsilon)
    return (center * inv_std, inv_std)


def norm_back(upstream, gain_row, normed, inv_std):
    scaled = upstream * gain_row
    return inv_std * (
        scaled
        - jnp.mean(scaled, axis=-1, keepdims=True)
        - normed * jnp.mean(scaled * normed, axis=-1, keepdims=True)
    )


def gelu_tanh(values):
    return jax.nn.gelu(values, approximate=True)


def multiply(form, left, right):
    return jnp.einsum(form, left, right, preferred_element_type=jnp.float32)


def per_device(tokens, cotangent, w_qkv, w_out, w_up, w_down, norm_gains):
    low = jnp.bfloat16
    owner = lax.axis_index("dp") * lax.axis_size("ctx") + lax.axis_index("ctx")
    shards = (
        jnp.concatenate([w_qkv, w_out.T[None]], axis=0).reshape(SLOT, WIDTH),
        w_up.reshape(ROWS, 4, WIDTH).transpose(1, 0, 2).reshape(SLOT, WIDTH),
        w_down.reshape(4, WIDTH, ROWS).transpose(0, 2, 1).reshape(SLOT, WIDTH),
    )
    gain_part = lax.dynamic_update_slice(
        jnp.zeros((8, 768), jnp.float32),
        0.5 * norm_gains.astype(jnp.float32),
        (jnp.int32(0), owner * ROWS),
    )
    (
        normed_one, inv_one, first_in, parts, head_out, lse, attended, gains, qkv, out, up, down
    ) = forward_attention(tokens, shards, gain_part)
    gain_one, gain_two = gains[0], gains[1]
    inputs = tokens.astype(jnp.float32)
    attended = attended.reshape(768, 256)
    middle = inputs + multiply("cb,dc->bd", attended, out)
    normed_two, inv_two = normalize(middle)
    second_in = (normed_two * gain_two).astype(low)
    hidden = multiply("bd,df->bf", second_in, up)
    activated, gelu_pull = jax.vjp(gelu_tanh, hidden)
    act_low = activated.astype(low)
    result = (middle + multiply("bf,df->bd", act_low, down)).astype(low)
    grad_down = multiply("bd,bf->df", cotangent, act_low).astype(low)
    grad_act = multiply("bd,df->bf", cotangent, down)
    grad_hidden = gelu_pull(grad_act)[0].astype(low)
    grad_up = multiply("bd,bf->df", second_in, grad_hidden).astype(low)
    grad_second = multiply("bf,df->bd", grad_hidden, up)
    grad_middle = cotangent.astype(jnp.float32) + norm_back(
        grad_second, gain_two, normed_two, inv_two
    )
    gain_two_term = jnp.sum(grad_second * normed_two, axis=0)
    mid_low = grad_middle.astype(low)
    grad_out = multiply("bd,cb->dc", mid_low, attended).astype(low)
    grad_att = multiply("bd,dc->cb", mid_low, out).astype(low).reshape(1, HEADS, HEAD_DIM, 256)
    unshuffle = unshuffle_matrix()
    grad_projected, sum_b, sum_c = backward_attention(
        grad_att, parts, head_out, lse, grad_up, grad_down, unshuffle
    )
    grad_projected = grad_projected.reshape(2304, 256)
    grad_qkv = multiply("bd,cb->dc", first_in, grad_projected).astype(low)
    grad_first = multiply("cb,dc->bd", grad_projected, qkv)
    grad_tokens = grad_middle + norm_back(grad_first, gain_one, normed_one, inv_one)
    gain_one_term = jnp.sum(grad_first * normed_one, axis=0)
    gain_terms = jnp.concatenate(
        [gain_one_term[None], gain_two_term[None], jnp.zeros((6, 768), jnp.float32)]
    )
    sum_a, gain_sum = reduce_projections(grad_qkv, grad_out, gain_terms, unshuffle)
    sum_a = sum_a.reshape(4, ROWS, WIDTH)
    return (
        result,
        grad_tokens,
        sum_a[:3],
        sum_a[3].T,
        sum_b.reshape(4, ROWS, WIDTH).transpose(1, 0, 2).reshape(ROWS, 4 * WIDTH),
        sum_c.reshape(4, ROWS, WIDTH).transpose(0, 2, 1).reshape(4 * WIDTH, ROWS),
        lax.dynamic_slice(gain_sum, (jnp.int32(0), owner * ROWS), (2, ROWS)),
    )


def solution(mesh):
    return jax.shard_map(
        per_device,
        mesh=mesh,
        in_specs=(
            P(("dp", "ctx", "tensor"), None),
            P(("dp", "ctx", "tensor"), None),
            P(None, ("dp", "ctx"), "tensor"),
            P("tensor", ("dp", "ctx")),
            P(("dp", "ctx"), "tensor"),
            P("tensor", ("dp", "ctx")),
            P(None, ("dp", "ctx")),
        ),
        out_specs=(
            P(("dp", "ctx", "tensor"), None),
            P(("dp", "ctx", "tensor"), None),
            P(None, ("dp", "ctx"), "tensor"),
            P("tensor", ("dp", "ctx")),
            P(("dp", "ctx"), "tensor"),
            P("tensor", ("dp", "ctx")),
            P(None, ("dp", "ctx")),
        ),
        check_vma=False,
    )
```

```python
import functools

import jax
import jax.numpy as jnp
import numpy as np
from jax import lax
from jax.experimental import pallas as pl
from jax.experimental.pallas import tpu as pltpu
from jax.sharding import PartitionSpec as P

HEAD_DIM = 64
HEADS = 12
MEMBERS = 16
ROWS = 12
WIDTH = 384
SLOT = 4 * ROWS
THIRDS = (("z", "x", "y"), ("x", "y", "z"), ("y", "z", "x"))
WHOLES = (("z", "y", "x"), ("z", "x", "y"))
MESH = pl.DeviceIdType.MESH
VMEM_BYTES = 60 * 1024 * 1024
epsilon = 1e-05
neg_large = -1e30


def place():
    dp, ctx, tensor = lax.axis_index("dp"), lax.axis_index("ctx"), lax.axis_index("tensor")
    return dict(x=dp // 2, y=ctx // 2, z=2 * tensor + dp % 2, c=ctx % 2)


def device_at(pos, axis, index):
    at = dict(pos)
    at[axis] = index
    return (at["x"] * 2 + at["z"] % 2, at["y"] * 2 + at["c"], at["z"] // 2)


def beside(pos, axis, by):
    if axis == "c":
        return device_at(pos, "c", 1 - pos["c"])
    return device_at(pos, axis, (pos[axis] + by) % 4)


def greet(pos):
    barrier = pltpu.get_barrier_semaphore()
    dp, number = lax.axis_index("dp"), member_number()

    def signal(i, carry):
        to = (number + i) % MEMBERS
        pl.semaphore_signal(
            barrier, inc=1, device_id=(dp, to // 2, to % 2), device_id_type=MESH
        )
        return carry

    lax.fori_loop(1, MEMBERS, signal, 0)
    for axis, by in (("x", 1), ("x", 2), ("x", 3), ("z", 1), ("z", 3)):
        pl.semaphore_signal(barrier, inc=1, device_id=beside(pos, axis, by), device_id_type=MESH)
    pl.semaphore_wait(barrier, MEMBERS - 1 + 5)


def member_number():
    return 2 * lax.axis_index("ctx") + lax.axis_index("tensor")


def remote(src, dst, send, recv, device):
    return pltpu.make_async_remote_copy(
        src_ref=src,
        dst_ref=dst,
        send_sem=send,
        recv_sem=recv,
        device_id=device,
        device_id_type=MESH,
    )


class SmallSum:
    def __init__(self, pos, ring, pair, send, recv):
        self.pos, self.ring, self.pair, self.send, self.recv = pos, ring, pair, send, recv

    def copy(self, n, by, coming=False):
        axis = ("x", "y", "z")[n]
        slot = (self.pos[axis] + 4 - by) % 4 if coming else self.pos[axis]
        ref, sem = self.ring.at[n, slot], n * 3 + by - 1
        return remote(
            ref, ref, self.send.at[sem], self.recv.at[sem], beside(self.pos, axis, by)
        )

    def start(self, n, value):
        self.ring[n, self.pos[("x", "y", "z")[n]]] = value
        for by in (1, 2, 3):
            self.copy(n, by).start()

    def finish(self, n):
        for by in (1, 2, 3):
            self.copy(n, by, coming=True).wait_recv()
            self.copy(n, by).wait_send()
        return (self.ring[n, 0] + self.ring[n, 1]) + (self.ring[n, 2] + self.ring[n, 3])

    def pair_copy(self, slot):
        ref = self.pair.at[slot]
        return remote(ref, ref, self.send.at[9], self.recv.at[9], beside(self.pos, "c", 1))

    def start_pair(self, value):
        self.pair[self.pos["c"]] = value
        self.pair_copy(self.pos["c"]).start()

    def finish_pair(self):
        self.pair_copy(1 - self.pos["c"]).wait_recv()
        self.pair_copy(self.pos["c"]).wait_send()
        return self.pair[0] + self.pair[1]


class Group:
    def __init__(self, pos, send, recv):
        self.pos, self.send, self.recv = pos, send, recv
        self.member = (pos["y"] % 2) * 2 + pos["c"]
        y = pos["y"] + 1 - 2 * (pos["y"] % 2)
        c = 1 - pos["c"]
        self.partners = []
        for to_y, to_c in ((pos["y"], c), (y, pos["c"]), (y, c)):
            device = device_at({**pos, "y": to_y}, "c", to_c)
            self.partners.append((device, (to_y % 2) * 2 + to_c))

    def copy(self, held, k, i, coming=False):
        device, member = self.partners[i]
        ref = held.at[k, member if coming else self.member]
        return remote(ref, ref, self.send.at[k * 3 + i], self.recv.at[k * 3 + i], device)

    def start(self, held, k):
        for i in range(3):
            self.copy(held, k, i).start()

    def finish(self, held, k):
        for i in range(3):
            self.copy(held, k, i, coming=True).wait_recv()
        return jnp.concatenate([held[k, member] for member in range(4)], axis=0)

    def sent(self, held, k):
        for i in range(3):
            self.copy(held, k, i).wait_send()


class Unit:
    def __init__(self, pos, order, unit, send, recv, started):
        self.pos, self.order, self.unit = pos, order, unit
        self.send, self.recv, self.started = send, recv, started
        self.sibling = beside(pos, "c", 1)

    def move(self, src, dst, sem, device):
        sem = self.unit * 16 + sem
        copy = remote(src, dst, self.send.at[sem], self.recv.at[sem], device)
        copy.start()
        self.started.append(copy)

    def arrived(self, dst, sem):
        sem = self.unit * 16 + sem
        remote(dst, dst, self.send.at[sem], self.recv.at[sem], self.sibling).wait_recv()

    def along(self, stage, by):
        return beside(self.pos, self.order[stage], by)

    def at(self, stage, by):
        index = ((self.pos[self.order[stage]] + by) % 4,)
        for later in range(stage + 1, 3):
            index = (self.pos[self.order[later]],) + index
        return (self.unit, self.pos["c"]) + index


class Gather(Unit):
    def __init__(self, pos, order, unit, held, send, recv, started):
        super().__init__(pos, order, unit, send, recv, started)
        self.held = held

    def pass_on(self, index, sem, device):
        self.move(self.held.at[index], self.held.at[index], sem, device)

    def begin(self, stage):
        for by in (1, 3, 2):
            self.pass_on(self.at(stage, 0), stage * 3 + by - 1, self.along(stage, by))
        if stage == 2:
            self.share(0)

    def finish(self, stage):
        for by in (1, 3, 2):
            self.arrived(self.held.at[self.at(stage, 4 - by)], stage * 3 + by - 1)
            if stage == 2:
                self.share(4 - by)

    def share(self, by):
        self.pass_on(self.at(2, by), 9 + by, self.sibling)

    def settle(self):
        place3 = self.pos[self.order[2]]
        for by in (0, 3, 1, 2):
            index = (self.unit, 1 - self.pos["c"], (place3 + by) % 4)
            self.arrived(self.held.at[index], 9 + by)


def wide(value):
    return value.astype(jnp.float32)


class Reduce(Unit):
    def __init__(self, pos, order, unit, held, landing, send, recv, started):
        super().__init__(pos, order, unit, send, recv, started)
        self.held, self.cores, self.coming = held, landing[0], landing[1:]

    def add(self, index, sources, *counts):
        held = self.held

        def one(slot):
            total = wide(held[index + slot])
            for source, at in sources:
                total = total + wide(source[at + slot])
            held[index + slot] = total.astype(jnp.bfloat16)

        def body(i, carry):
            one((i // 4, i % 4) if len(counts) == 2 else (i,))
            return carry

        if counts:
            lax.fori_loop(0, 4 ** len(counts), body, 0)
        else:
            one(())

    def cross(self):
        place3, u = self.pos[self.order[2]], self.unit
        for by in (1, 3, 2, 0):
            index = (place3 + by) % 4
            self.move(
                self.held.at[u, 1 - self.pos["c"], index],
                self.cores.at[u, index],
                9 + by,
                self.sibling,
            )

    def take_core(self, by):
        index = (self.pos[self.order[2]] + by) % 4
        self.arrived(self.cores.at[self.unit, index], 9 + by)
        self.add(self.at(2, by), [(self.cores, (self.unit, index))], 4, 4)

    def begin(self, stage):
        for by in (1, 3, 2):
            if stage == 2:
                self.take_core(by)
            self.move(
                self.held.at[self.at(stage, by)],
                self.coming[stage].at[self.unit, by - 1],
                stage * 3 + by - 1,
                self.along(stage, by),
            )

    def finish(self, stage):
        if stage == 2:
            self.take_core(0)
        for by in (1, 3, 2):
            self.arrived(self.coming[stage].at[self.unit, by - 1], stage * 3 + by - 1)
        self.add(
            self.at(stage, 0),
            [(self.coming[stage], (self.unit, i)) for i in range(3)],
            *(4,) * stage,
        )


def landing_scratch(units, rows):
    low, slot = jnp.bfloat16, (rows, WIDTH)
    return [
        pltpu.VMEM((units, 4, 4, 4) + slot, low),
        pltpu.VMEM((units, 3) + slot, low),
        pltpu.VMEM((units, 3, 4) + slot, low),
        pltpu.VMEM((units, 3, 4, 4) + slot, low),
    ]


def slots_of(group, orders):
    x, z_lo, y_half = group // 4, (group // 2) % 2, group % 2
    for tensor in range(2):
        for piece in range(4):
            at = dict(x=x, z=2 * tensor + z_lo, y=2 * y_half + piece // 2)
            yield tensor, piece, [
                (piece % 2, at[order[2]], at[order[1]], at[order[0]]) for order in orders
            ]


def column_of(tensor, piece):
    return (0, (piece * 2 + tensor) * WIDTH) if piece < 3 else (1, tensor * WIDTH)


def copy_thirds(thirds, whole):
    def body(group, carry):
        for tensor, piece, indices in slots_of(group, THIRDS):
            which, column = column_of(tensor, piece)
            for third, index in enumerate(indices):
                rows = pl.ds(pl.multiple_of(group * SLOT + 16 * third, 16), 16)
                whole[which][rows, pl.ds(column, WIDTH)] = thirds[(third,) + index]
        return carry

    lax.fori_loop(0, 16, body, 0)


def copy_wholes(slots, whole):
    def body(group, carry):
        rows = pl.ds(pl.multiple_of(group * SLOT, SLOT), SLOT)
        for tensor, piece, indices in slots_of(group, WHOLES):
            columns = pl.ds((tensor * 4 + piece) * WIDTH, WIDTH)
            for k, index in enumerate(indices):
                whole[k][rows, columns] = slots[(k,) + index]
        return carry

    lax.fori_loop(0, 16, body, 0)


def slot_index(order, group, tensor, piece):
    at = dict(x=group // 4, z=2 * tensor + (group // 2) % 2, y=2 * (group % 2) + piece // 2)
    return (piece % 2, at[order[2]], at[order[1]], at[order[0]])


def fill_thirds(thirds, tensor, piece, value):
    for group in range(16):
        for third, order in enumerate(THIRDS):
            row = group * SLOT + 16 * third
            thirds[(third,) + slot_index(order, group, tensor, piece)] = value[row : row + 16]


def fill_wholes(slots, k, tensor, piece, value):
    for group in range(16):
        row = group * SLOT
        slots[(k,) + slot_index(WHOLES[k], group, tensor, piece)] = value[row : row + SLOT]


def head_place(head):
    member = head % 6
    return (member * 2) % 8 + (member // 4) * (1 + (member % 4) * 2), head // 6


def own_head(ctx, tensor):
    core, y = ctx % 2, ctx // 2
    return tensor * 6 + (1 - core) * y + core * (4 + y // 2), core * (y % 2) == 0


class ToHeads:
    def __init__(self, src, dst, send, recv):
        self.src, self.dst, self.send, self.recv = src, dst, send, recv
        self.dp, self.number = lax.axis_index("dp"), member_number()

    def copies(self, i):
        head = (self.number + i) % HEADS
        ctx, tensor = head_place(head)
        local = 2 * ctx + tensor == self.number
        src, dst = self.src.at[:, head], self.dst.at[self.number]
        recv = self.recv.at[self.number]
        return (
            local,
            lambda: pltpu.make_async_copy(src, dst, recv),
            lambda: remote(src, dst, self.send.at[head], recv, (self.dp, ctx, tensor)),
        )

    def start(self):
        def body(i, carry):
            local, inside, outside = self.copies(i)

            @pl.when(local)
            def _():
                inside().start()

            @pl.when(jnp.logical_not(local))
            def _():
                outside().start()

            return carry

        lax.fori_loop(0, HEADS, body, 0)

    def wait(self, first, last):
        def body(i, carry):
            src, dst, recv = self.src.at[:, 0], self.dst.at[i], self.recv.at[i]

            @pl.when(i == self.number)
            def _():
                pltpu.make_async_copy(src, dst, recv).wait()

            @pl.when(i != self.number)
            def _():
                remote(src, dst, self.send.at[0], recv, (self.dp, i // 2, i % 2)).wait_recv()

            return carry

        lax.fori_loop(first, last, body, 0)

    def sent(self):
        def body(i, carry):
            local, inside, outside = self.copies(i)

            @pl.when(jnp.logical_not(local))
            def _():
                outside().wait_send()

            return carry

        lax.fori_loop(0, HEADS, body, 0)


class FromHeads:
    def __init__(self, src, dst, send, recv):
        self.src, self.dst, self.send, self.recv = src, dst, send, recv
        self.dp, self.number = lax.axis_index("dp"), member_number()
        self.head = own_head(lax.axis_index("ctx"), lax.axis_index("tensor"))[0]

    def outside(self, to):
        return remote(
            self.src.at[to],
            self.dst.at[:, self.head],
            self.send.at[to],
            self.recv.at[self.head],
            (self.dp, to // 2, to % 2),
        )

    def start(self, to):
        @pl.when(to == self.number)
        def _():
            pltpu.make_async_copy(
                self.src.at[to], self.dst.at[:, self.head], self.recv.at[self.head]
            ).start()

        @pl.when(to != self.number)
        def _():
            self.outside(to).start()

    def wait(self):
        def body(i, carry):
            ctx, tensor = head_place(i)
            local = 2 * ctx + tensor == self.number
            src, dst, recv = self.src.at[0], self.dst.at[:, i], self.recv.at[i]

            @pl.when(local)
            def _():
                pltpu.make_async_copy(src, dst, recv).wait()

            @pl.when(jnp.logical_not(local))
            def _():
                remote(src, dst, self.send.at[0], recv, (self.dp, ctx, tensor)).wait_recv()

            return carry

        lax.fori_loop(0, HEADS, body, 0)

    def sent(self):
        def body(i, carry):
            self.outside((self.number + i) % MEMBERS).wait_send()
            return carry

        lax.fori_loop(1, MEMBERS, body, 0)


TILE = 512
TILES = 8


def turned(value):
    return jnp.transpose(value.astype(jnp.float32)).astype(jnp.bfloat16)


def allowed_tile():
    key = lax.broadcasted_iota(jnp.int32, (TILE, TILE), 0)
    query = lax.broadcasted_iota(jnp.int32, (TILE, TILE), 1)
    return query >= key


def two(ref, tile, *index):
    return jnp.concatenate([ref[(2 * tile,) + index], ref[(2 * tile + 1,) + index]], axis=1)


def put_two(ref, tile, part, value):
    ref[2 * tile, part] = value[:, :256]
    ref[2 * tile + 1, part] = value[:, 256:]


def dot(a, b):
    return jnp.dot(a, b, preferred_element_type=jnp.float32)


def dot_right(a, b):
    return lax.dot_general(a, b, (((1,), (1,)), ((), ())), preferred_element_type=jnp.float32)


def attend_tile(i, parts, keys, out, lse):
    own_rows = pl.ds(pl.multiple_of(i * TILE, TILE), TILE)
    keys[own_rows, :] = turned(two(parts, i, 1))
    query = two(parts, i, 0) * jnp.bfloat16(HEAD_DIM ** -0.5)

    def step(scores, j, state):
        top, total, weighted = state
        new_top = jnp.maximum(top, jnp.max(scores, axis=0, keepdims=True))
        fade = jnp.exp(top - new_top)
        raised = jnp.exp(scores - new_top)
        total = total * fade + jnp.sum(raised, axis=0, keepdims=True)
        weighted = weighted * fade + dot(two(parts, j, 2), raised.astype(jnp.bfloat16))
        return new_top, total, weighted

    def before(j, state):
        return step(dot(keys[pl.ds(pl.multiple_of(j * TILE, TILE), TILE), :], query), j, state)

    state = (
        jnp.full((1, TILE), neg_large, jnp.float32),
        jnp.zeros((1, TILE), jnp.float32),
        jnp.zeros((HEAD_DIM, TILE), jnp.float32),
    )
    state = lax.fori_loop(0, i, before, state)
    masked = jnp.where(allowed_tile(), dot(keys[own_rows, :], query), neg_large)
    top, total, weighted = step(masked, i, state)
    put_two(out, i, 0, (weighted / total).astype(jnp.bfloat16))
    lse[i] = top + jnp.log(total)


def norm_parts(values):
    center = values - jnp.mean(values, axis=-1, keepdims=True)
    inv_std = lax.rsqrt(jnp.mean(center * center, axis=-1, keepdims=True) + epsilon)
    return center * inv_std, inv_std


def norm_back(upstream, gain_row, normed, inv_std):
    scaled = upstream * gain_row
    return inv_std * (
        scaled
        - jnp.mean(scaled, axis=-1, keepdims=True)
        - normed * jnp.mean(scaled * normed, axis=-1, keepdims=True)
    )


def gelu_and_slope(v):
    scale, cubic = (2.0 / np.pi) ** 0.5, 0.044715
    square = v * v
    bend = jnp.tanh(scale * v * (1.0 + cubic * square))
    half = 0.5 * (1.0 + bend)
    slope = half + (0.5 * scale) * v * (1.0 - bend * bend) * (1.0 + 3.0 * cubic * square)
    return v * half, slope


def forward_kernel(
    tokens, cotangent, a, b, c, gain, shuffle,
    normed_out, inv_out, first_out, parts, head_out, lse, attended, gain_out,
    result, second_out, act_out, hid_out, middle_grad, grad_att, gain_two_out, w_qkv,
    pre, thirds, wholes, qkv, out, up, down, projected, keys, ring, pair, forth_sum, back_sum,
    third_send, third_recv, whole_send, whole_recv, pre_send, pre_recv, small_send, small_recv,
    to_send, to_recv, from_send, from_recv, write_sem,
):
    pos = place()
    active = own_head(lax.axis_index("ctx"), lax.axis_index("tensor"))[1]
    group = Group(pos, pre_send, pre_recv)
    small = SmallSum(pos, ring, pair, small_send, small_recv)
    started = []
    first = [
        Gather(pos, order, u, thirds, third_send, third_recv, started)
        for u, order in enumerate(THIRDS)
    ]
    later = [
        Gather(pos, order, u, wholes, whole_send, whole_recv, started)
        for u, order in enumerate(WHOLES)
    ]
    spread = ToHeads(projected, parts, to_send, to_recv)
    back = FromHeads(head_out, attended, from_send, from_recv)
    for k, shard in enumerate((a, b, c)):
        pre[k, group.member] = shard[...]
    greet(pos)
    for k in range(3):
        group.start(pre, k)
    small.start(0, gain[...])

    def sorted_piece(k):
        return dot(shuffle[group.member], group.finish(pre, k)).astype(jnp.bfloat16)

    piece = sorted_piece(0)
    for u, unit in enumerate(first):
        thirds[unit.at(0, 0)] = piece[16 * u : 16 * (u + 1)]
        unit.begin(0)
    for u, unit in enumerate(later):
        wholes[unit.at(0, 0)] = sorted_piece(1 + u)
    normed_one, inv_one = norm_parts(wide(tokens[...]))
    normed_out[...] = normed_one
    inv_out[...] = inv_one
    for stage in range(3):
        for unit in first:
            unit.finish(stage)
            if stage < 2:
                unit.begin(stage + 1)
        total = small.finish(stage)
        if stage < 2:
            small.start(stage + 1, total)
        else:
            small.start_pair(total)
        if stage == 1:
            for unit in later:
                unit.begin(0)
    for unit in later:
        unit.finish(0)
        unit.begin(1)
    for unit in first:
        unit.settle()
    copy_thirds(thirds, (qkv, out))
    write = pltpu.make_async_copy(qkv, w_qkv, write_sem)
    write.start()
    gains = small.finish_pair()
    gain_out[...] = gains
    first_in = (normed_out[...] * gains[0:1]).astype(jnp.bfloat16)
    first_out[...] = first_in
    for part in range(3):
        for tensor in range(2):
            column = (part * 2 + tensor) * WIDTH
            cols = jnp.transpose(dot(first_in, qkv[:, pl.ds(column, WIDTH)])).astype(jnp.bfloat16)
            for head in range(6):
                projected[part, tensor * 6 + head] = cols[head * HEAD_DIM : (head + 1) * HEAD_DIM]
    spread.start()
    for unit in later:
        unit.finish(1)
        unit.begin(2)

    def per_queries(i, carry):
        @pl.when(active)
        def _():
            spread.wait(2 * i, 2 * i + 2)
            attend_tile(i, parts, keys, head_out, lse)
            back.start(2 * i)
            back.start(2 * i + 1)

        return carry

    lax.fori_loop(0, 7, per_queries, 0)
    for unit in later:
        unit.finish(2)
    lax.fori_loop(7, 8, per_queries, 0)
    for unit in later:
        unit.settle()
    copy_wholes(wholes, (up, down))
    back.wait()
    weighted = jnp.transpose(dot(out[...], attended[0].reshape(768, 256)))
    middle = wide(tokens[...]) + weighted
    normed_two, inv_two = norm_parts(middle)
    second_in = (normed_two * gain_out[1:2]).astype(jnp.bfloat16)
    second_out[...] = second_in
    forth_sum[...] = middle
    back_sum[...] = jnp.zeros_like(back_sum)

    def feed(p, carry):
        columns = pl.ds(pl.multiple_of(p * 768, 768), 768)
        act, slope = gelu_and_slope(dot(second_out[...], up[:, columns]))
        act = act.astype(jnp.bfloat16)
        act_out[:, columns] = act
        hid = (dot(cotangent[...], down[:, columns]) * slope).astype(jnp.bfloat16)
        hid_out[:, columns] = hid
        forth_sum[...] += dot_right(act, down[:, columns])
        back_sum[...] += dot_right(hid, up[:, columns])
        return carry

    lax.fori_loop(0, 4, feed, 0)
    result[...] = forth_sum[...].astype(jnp.bfloat16)
    grad_second = back_sum[...]
    gain_two_out[...] = jnp.sum(grad_second * normed_two, axis=0, keepdims=True)
    grad_middle = wide(cotangent[...]) + norm_back(
        grad_second, gain_out[1:2], normed_two, inv_two
    )
    middle_grad[...] = grad_middle
    grads = jnp.transpose(dot(grad_middle.astype(jnp.bfloat16), out[...])).astype(jnp.bfloat16)
    for head in range(HEADS):
        grad_att[0, head] = grads[head * HEAD_DIM : (head + 1) * HEAD_DIM]
    spread.sent()

    @pl.when(active)
    def _():
        back.sent()

    for k in range(3):
        group.sent(pre, k)
    for copy in started:
        copy.wait_send()
    write.wait()


def back_tile(j, parts, grad_att, lse, delta, query_sum, out):
    key_cols, value_cols = two(parts, j, 1), two(parts, j, 2)
    key_rows, value_rows = turned(key_cols), turned(value_cols)

    def step(i, state, diagonal):
        key_sum, value_sum = state
        query = two(parts, i, 0) * jnp.bfloat16(HEAD_DIM ** -0.5)
        grad = two(grad_att, i, 0)
        shares = jnp.exp(dot(key_rows, query) - lse[i])
        if diagonal:
            shares = jnp.where(allowed_tile(), shares, 0.0)
        grad_scores = (shares * (dot(value_rows, grad) - delta[i])).astype(jnp.bfloat16)
        query_sum[i] += dot(key_cols, grad_scores)
        key_sum = key_sum + dot_right(query, grad_scores)
        value_sum = value_sum + dot_right(grad, shares.astype(jnp.bfloat16))
        return key_sum, value_sum

    zero = jnp.zeros((HEAD_DIM, TILE), jnp.float32)
    state = step(j, (zero, zero), True)
    key_sum, value_sum = lax.fori_loop(
        j + 1, TILES, lambda i, state: step(i, state, False), state
    )
    put_two(out, j, 0, (query_sum[j] * HEAD_DIM ** -0.5).astype(jnp.bfloat16))
    put_two(out, j, 1, key_sum.astype(jnp.bfloat16))
    put_two(out, j, 2, value_sum.astype(jnp.bfloat16))


def backward_kernel(
    grad_att, unshuffle, gain, gain_two, inv_one, lse_in, parts_in, head_out_in, act_in, hid_in,
    second_in, cot_in, middle_in, attended_in, first_in, normed_in, w_qkv_in,
    grad_tokens, out_a, out_b, out_c, gain_out,
    lse, parts, head_out, act, hid, second, cot, middle, attended, first, normed, w_qkv,
    turned_in, grad_projected, head_grad, head_back, query_sum, delta, wholes, thirds, post,
    cores_w, ends1_w, ends2_w, ends3_w, cores_t, ends1_t, ends2_t, ends3_t, ring, pair,
    load_sem, whole_send, whole_recv, third_send, third_recv, post_send, post_recv,
    small_send, small_recv, to_send, to_recv, from_send, from_recv,
):
    pos = place()
    active = own_head(lax.axis_index("ctx"), lax.axis_index("tensor"))[1]
    group = Group(pos, post_send, post_recv)
    small = SmallSum(pos, ring, pair, small_send, small_recv)
    started = []
    units = [
        Reduce(
            pos, order, u, wholes, (cores_w, ends1_w, ends2_w, ends3_w), whole_send, whole_recv,
            started,
        )
        for u, order in enumerate(WHOLES)
    ]
    last = [
        Reduce(
            pos, order, u, thirds, (cores_t, ends1_t, ends2_t, ends3_t), third_send, third_recv,
            started,
        )
        for u, order in enumerate(THIRDS)
    ]
    spread = ToHeads(grad_att, head_grad, to_send, to_recv)
    back = FromHeads(head_back, grad_projected, from_send, from_recv)
    loads = [
        pltpu.make_async_copy(src, dst, load_sem.at[n])
        for n, (src, dst) in enumerate(
            (
                (cot_in, cot), (act_in, act), (second_in, second), (hid_in, hid),
                (middle_in, middle), (attended_in, attended), (lse_in, lse), (parts_in, parts),
                (head_out_in, head_out), (first_in, first), (normed_in, normed),
                (w_qkv_in, w_qkv),
            )
        )
    ]
    for load in loads:
        load.start()
    greet(pos)
    spread.start()
    for load in loads[:4]:
        load.wait()

    def flip(n, value):
        turned_in[n] = jnp.transpose(value).astype(jnp.bfloat16)

    flip(0, wide(cot[...]))
    flip(1, wide(second[...]))

    def feed(p, carry):
        columns = pl.ds(pl.multiple_of(p * WIDTH, WIDTH), WIDTH)
        for k, (left, right) in enumerate(((1, hid), (0, act))):
            value = dot(turned_in[left], right[:, columns]).astype(jnp.bfloat16)
            fill_wholes(wholes, k, p // 4, p % 4, value)
        return carry

    lax.fori_loop(0, 8, feed, 0)
    for unit in units:
        unit.cross()
    for load in loads[4:]:
        load.wait()
    flip(0, middle[...])
    flip(1, wide(first[...]))
    for tensor in range(2):
        rows = attended[0, 6 * tensor : 6 * (tensor + 1)].reshape(WIDTH, 256)
        fill_thirds(thirds, tensor, 3, dot_right(turned_in[0], rows).astype(jnp.bfloat16))
    for unit in units:
        unit.begin(2)

    @pl.when(active)
    def _():
        spread.wait(0, MEMBERS)

        def prepare(i, carry):
            delta[i] = jnp.sum(
                wide(two(head_out, i, 0)) * wide(two(head_grad, i, 0)), axis=0, keepdims=True
            )
            query_sum[i] = jnp.zeros((HEAD_DIM, TILE), jnp.float32)
            return carry

        lax.fori_loop(0, TILES, prepare, 0)

    def per_keys(j, carry):
        @pl.when(active)
        def _():
            back_tile(j, parts, head_grad, lse, delta, query_sum, head_back)
            back.start(2 * j)
            back.start(2 * j + 1)

        return carry

    lax.fori_loop(0, 2, per_keys, 0)
    for unit in units:
        unit.finish(2)
        unit.begin(1)
    lax.fori_loop(2, 4, per_keys, 0)
    for unit in units:
        unit.finish(1)
        unit.begin(0)
    lax.fori_loop(4, 6, per_keys, 0)
    for u, unit in enumerate(units):
        unit.finish(0)
        post[u, group.member] = wholes[unit.at(0, 0)]
        group.start(post, u)
    lax.fori_loop(6, 8, per_keys, 0)
    back.wait()

    def project(p, carry):
        part, tensor = p // 2, p % 2
        rows = grad_projected[part, pl.ds(6 * tensor, 6)].reshape(WIDTH, 256)
        fill_thirds(thirds, tensor, part, dot_right(turned_in[1], rows).astype(jnp.bfloat16))
        return carry

    lax.fori_loop(0, 6, project, 0)
    for unit in last:
        unit.cross()
    grad_first = jnp.transpose(dot(w_qkv[...], grad_projected[...].reshape(2304, 256)))
    term = jnp.sum(grad_first * normed[...], axis=0, keepdims=True)
    row = lax.broadcasted_iota(jnp.int32, (8, 768), 0)
    small.start(0, jnp.where(row == 0, term, jnp.where(row == 1, gain_two[...], 0.0)))
    for unit in last:
        unit.begin(2)
    grad_tokens[...] = middle[...] + norm_back(grad_first, gain[0:1], normed[...], inv_one[...])
    for u, out in enumerate((out_b, out_c)):
        out[...] = dot(unshuffle[group.member], group.finish(post, u))
    for stage in (2, 1, 0):
        total = small.finish(2 - stage)
        if stage > 0:
            small.start(3 - stage, total)
        else:
            small.start_pair(total)
        for unit in last:
            unit.finish(stage)
            if stage > 0:
                unit.begin(stage - 1)
    for u, unit in enumerate(last):
        post[2, group.member, pl.ds(16 * u, 16)] = thirds[unit.at(0, 0)]
    group.start(post, 2)
    gain_out[...] = small.finish_pair()
    out_a[...] = dot(unshuffle[group.member], group.finish(post, 2))
    for k in range(3):
        group.sent(post, k)
    spread.sent()

    @pl.when(active)
    def _():
        back.sent()

    for copy in started:
        copy.wait_send()


def shuffle_matrix():
    matrix = np.zeros((4, SLOT, 4 * SLOT), np.float32)
    for piece in range(4):
        for member in range(4):
            for row in range(ROWS):
                matrix[piece, member * ROWS + row, member * SLOT + piece * ROWS + row] = 1
    return jnp.asarray(matrix, jnp.bfloat16)


def unshuffle_matrix():
    matrix = np.zeros((4, SLOT, 4 * SLOT), np.float32)
    for member in range(4):
        for piece in range(4):
            for row in range(ROWS):
                matrix[member, piece * ROWS + row, piece * SLOT + member * ROWS + row] = 1
    return jnp.asarray(matrix, jnp.bfloat16)


def vmem_specs(count):
    return [pl.BlockSpec(memory_space=pltpu.VMEM)] * count


def any_specs(count):
    return [pl.BlockSpec(memory_space=pl.ANY)] * count


def sems(count):
    return [pltpu.SemaphoreType.DMA((count,))] * 2


def low_array(*shape):
    return jax.ShapeDtypeStruct(shape, jnp.bfloat16)


def wide_array(*shape):
    return jax.ShapeDtypeStruct(shape, jnp.float32)


SMALL_SCRATCH = [
    pltpu.VMEM((3, 4, 8, 768), jnp.float32),
    pltpu.VMEM((2, 8, 768), jnp.float32),
]


def kernel_params(number):
    return pltpu.CompilerParams(
        collective_id=number, has_side_effects=True, vmem_limit_bytes=VMEM_BYTES
    )


def forward_pass(tokens, cotangent, shards, gain):
    low = jnp.bfloat16
    return pl.pallas_call(
        forward_kernel,
        name="forward_pass",
        out_shape=[
            wide_array(256, 768),
            wide_array(256, 1),
            low_array(256, 768),
            low_array(MEMBERS, 3, HEAD_DIM, 256),
            low_array(MEMBERS, 1, HEAD_DIM, 256),
            wide_array(TILES, 1, TILE),
            low_array(1, HEADS, HEAD_DIM, 256),
            wide_array(8, 768),
            low_array(256, 768),
            low_array(256, 768),
            low_array(256, 3072),
            low_array(256, 3072),
            wide_array(256, 768),
            low_array(1, HEADS, HEAD_DIM, 256),
            wide_array(1, 768),
            low_array(768, 2304),
        ],
        in_specs=vmem_specs(7),
        out_specs=vmem_specs(15) + any_specs(1),
        scratch_shapes=[
            pltpu.VMEM((3, 4, SLOT, WIDTH), low),
            pltpu.VMEM((3, 2, 4, 4, 4, 16, WIDTH), low),
            pltpu.VMEM((2, 2, 4, 4, 4, SLOT, WIDTH), low),
            pltpu.VMEM((768, 2304), low),
            pltpu.VMEM((768, 768), low),
            pltpu.VMEM((768, 3072), low),
            pltpu.VMEM((768, 3072), low),
            pltpu.VMEM((3, HEADS, HEAD_DIM, 256), low),
            pltpu.VMEM((TILES * TILE, HEAD_DIM), low),
        ]
        + SMALL_SCRATCH
        + [pltpu.VMEM((256, 768), jnp.float32)] * 2
        + sems(48)
        + sems(32)
        + sems(9)
        + sems(10)
        + sems(MEMBERS)
        + sems(MEMBERS)
        + [pltpu.SemaphoreType.DMA],
        compiler_params=kernel_params(0),
    )(tokens, cotangent, *shards, gain, shuffle_matrix())


def backward_pass(grad_att, gain, gain_two, inv_one, arrays):
    low = jnp.bfloat16
    return pl.pallas_call(
        backward_kernel,
        name="backward_pass",
        out_shape=[wide_array(256, 768)]
        + [wide_array(SLOT, WIDTH)] * 3
        + [wide_array(8, 768)],
        in_specs=any_specs(1) + vmem_specs(4) + any_specs(12),
        out_specs=vmem_specs(5),
        scratch_shapes=[pltpu.VMEM(array.shape, array.dtype) for array in arrays]
        + [
            pltpu.VMEM((2, 768, 256), low),
            pltpu.VMEM((3, HEADS, HEAD_DIM, 256), low),
            pltpu.VMEM((MEMBERS, 1, HEAD_DIM, 256), low),
            pltpu.VMEM((MEMBERS, 3, HEAD_DIM, 256), low),
            pltpu.VMEM((TILES, HEAD_DIM, TILE), jnp.float32),
            pltpu.VMEM((TILES, 1, TILE), jnp.float32),
            pltpu.VMEM((2, 2, 4, 4, 4, SLOT, WIDTH), low),
            pltpu.VMEM((3, 2, 4, 4, 4, 16, WIDTH), low),
            pltpu.VMEM((3, 4, SLOT, WIDTH), low),
        ]
        + landing_scratch(2, SLOT)
        + landing_scratch(3, 16)
        + SMALL_SCRATCH
        + [pltpu.SemaphoreType.DMA((12,))]
        + sems(32)
        + sems(48)
        + sems(9)
        + sems(10)
        + sems(MEMBERS)
        + sems(MEMBERS),
        compiler_params=kernel_params(1),
    )(grad_att, unshuffle_matrix(), gain, gain_two, inv_one, *arrays)


def per_device(tokens, cotangent, w_qkv, w_out, w_up, w_down, norm_gains):
    owner = lax.axis_index("dp") * lax.axis_size("ctx") + lax.axis_index("ctx")
    shards = (
        jnp.concatenate([w_qkv, w_out.T[None]], axis=0).reshape(SLOT, WIDTH),
        w_up.reshape(ROWS, 4, WIDTH).transpose(1, 0, 2).reshape(SLOT, WIDTH),
        w_down.reshape(4, WIDTH, ROWS).transpose(0, 2, 1).reshape(SLOT, WIDTH),
    )
    gain_part = lax.dynamic_update_slice(
        jnp.zeros((8, 768), jnp.float32),
        0.5 * norm_gains.astype(jnp.float32),
        (jnp.int32(0), owner * ROWS),
    )
    (
        normed_one, inv_one, first_in, parts, head_out, lse, attended, gains,
        result, second_in, act, hid, grad_middle, grad_att, gain_two_term, qkv,
    ) = forward_pass(tokens, cotangent, shards, gain_part)
    grad_tokens, sum_a, sum_b, sum_c, gain_sum = backward_pass(
        grad_att,
        gains,
        gain_two_term,
        inv_one,
        (
            lse, parts, head_out, act, hid, second_in, cotangent, grad_middle, attended,
            first_in, normed_one, qkv,
        ),
    )
    sum_a = sum_a.reshape(4, ROWS, WIDTH)
    return (
        result,
        grad_tokens,
        sum_a[:3],
        sum_a[3].T,
        sum_b.reshape(4, ROWS, WIDTH).transpose(1, 0, 2).reshape(ROWS, 4 * WIDTH),
        sum_c.reshape(4, ROWS, WIDTH).transpose(0, 2, 1).reshape(4 * WIDTH, ROWS),
        lax.dynamic_slice(gain_sum, (jnp.int32(0), owner * ROWS), (2, ROWS)),
    )


def solution(mesh):
    return jax.shard_map(
        per_device,
        mesh=mesh,
        in_specs=(
            P(("dp", "ctx", "tensor"), None),
            P(("dp", "ctx", "tensor"), None),
            P(None, ("dp", "ctx"), "tensor"),
            P("tensor", ("dp", "ctx")),
            P(("dp", "ctx"), "tensor"),
            P("tensor", ("dp", "ctx")),
            P(None, ("dp", "ctx")),
        ),
        out_specs=(
            P(("dp", "ctx", "tensor"), None),
            P(("dp", "ctx", "tensor"), None),
            P(None, ("dp", "ctx"), "tensor"),
            P("tensor", ("dp", "ctx")),
            P(("dp", "ctx"), "tensor"),
            P("tensor", ("dp", "ctx")),
            P(None, ("dp", "ctx")),
        ),
        check_vma=False,
    )
```

```python
import functools

import jax
import jax.numpy as jnp
import numpy as np
from jax import lax
from jax.experimental import pallas as pl
from jax.experimental.pallas import tpu as pltpu
from jax.sharding import PartitionSpec as P

HEAD_DIM = 64
HEADS = 12
MEMBERS = 16
ROWS = 12
WIDTH = 384
SLOT = 4 * ROWS
THIRDS = (("z", "x", "y"), ("x", "y", "z"), ("y", "z", "x"))
LATER = THIRDS + (("z", "y", "x"), ("y", "x", "z"), ("z", "y", "x"))
MESH = pl.DeviceIdType.MESH
VMEM_BYTES = 60 * 1024 * 1024
epsilon = 1e-05
neg_large = -1e30


def place():
    dp, ctx, tensor = lax.axis_index("dp"), lax.axis_index("ctx"), lax.axis_index("tensor")
    return dict(x=dp // 2, y=ctx // 2, z=2 * tensor + dp % 2, c=ctx % 2)


def device_at(pos, axis, index):
    at = dict(pos)
    at[axis] = index
    return (at["x"] * 2 + at["z"] % 2, at["y"] * 2 + at["c"], at["z"] // 2)


def beside(pos, axis, by):
    if axis == "c":
        return device_at(pos, "c", 1 - pos["c"])
    return device_at(pos, axis, (pos[axis] + by) % 4)


def greet(pos):
    barrier = pltpu.get_barrier_semaphore()
    dp, number = lax.axis_index("dp"), member_number()

    def signal(i, carry):
        to = (number + i) % MEMBERS
        pl.semaphore_signal(
            barrier, inc=1, device_id=(dp, to // 2, to % 2), device_id_type=MESH
        )
        return carry

    lax.fori_loop(1, MEMBERS, signal, 0)
    for axis, by in (("x", 1), ("x", 2), ("x", 3), ("z", 1), ("z", 3)):
        pl.semaphore_signal(barrier, inc=1, device_id=beside(pos, axis, by), device_id_type=MESH)
    pl.semaphore_wait(barrier, MEMBERS - 1 + 5)


def member_number():
    return 2 * lax.axis_index("ctx") + lax.axis_index("tensor")


def remote(src, dst, send, recv, device):
    return pltpu.make_async_remote_copy(
        src_ref=src,
        dst_ref=dst,
        send_sem=send,
        recv_sem=recv,
        device_id=device,
        device_id_type=MESH,
    )


class SmallSum:
    def __init__(self, pos, ring, pair, send, recv):
        self.pos, self.ring, self.pair, self.send, self.recv = pos, ring, pair, send, recv

    def copy(self, n, by, coming=False):
        axis = ("x", "y", "z")[n]
        slot = (self.pos[axis] + 4 - by) % 4 if coming else self.pos[axis]
        ref, sem = self.ring.at[n, slot], n * 3 + by - 1
        return remote(
            ref, ref, self.send.at[sem], self.recv.at[sem], beside(self.pos, axis, by)
        )

    def start(self, n, value):
        self.ring[n, self.pos[("x", "y", "z")[n]]] = value
        for by in (1, 2, 3):
            self.copy(n, by).start()

    def finish(self, n):
        for by in (1, 2, 3):
            self.copy(n, by, coming=True).wait_recv()
            self.copy(n, by).wait_send()
        return (self.ring[n, 0] + self.ring[n, 1]) + (self.ring[n, 2] + self.ring[n, 3])

    def pair_copy(self, slot):
        ref = self.pair.at[slot]
        return remote(ref, ref, self.send.at[9], self.recv.at[9], beside(self.pos, "c", 1))

    def start_pair(self, value):
        self.pair[self.pos["c"]] = value
        self.pair_copy(self.pos["c"]).start()

    def finish_pair(self):
        self.pair_copy(1 - self.pos["c"]).wait_recv()
        self.pair_copy(self.pos["c"]).wait_send()
        return self.pair[0] + self.pair[1]


class Group:
    def __init__(self, pos, send, recv):
        self.pos, self.send, self.recv = pos, send, recv
        self.member = (pos["y"] % 2) * 2 + pos["c"]
        y = pos["y"] + 1 - 2 * (pos["y"] % 2)
        c = 1 - pos["c"]
        self.partners = []
        for to_y, to_c in ((pos["y"], c), (y, pos["c"]), (y, c)):
            device = device_at({**pos, "y": to_y}, "c", to_c)
            self.partners.append((device, (to_y % 2) * 2 + to_c))

    def copy(self, held, k, i, coming=False):
        device, member = self.partners[i]
        ref = held.at[k, member if coming else self.member]
        return remote(ref, ref, self.send.at[k * 3 + i], self.recv.at[k * 3 + i], device)

    def start(self, held, k):
        for i in range(3):
            self.copy(held, k, i).start()

    def finish(self, held, k):
        for i in range(3):
            self.copy(held, k, i, coming=True).wait_recv()
        return jnp.concatenate([held[k, member] for member in range(4)], axis=0)

    def sent(self, held, k):
        for i in range(3):
            self.copy(held, k, i).wait_send()


class Unit:
    def __init__(self, pos, order, unit, send, recv, started):
        self.pos, self.order, self.unit = pos, order, unit
        self.send, self.recv, self.started = send, recv, started
        self.sibling = beside(pos, "c", 1)

    def move(self, src, dst, sem, device):
        sem = self.unit * 16 + sem
        copy = remote(src, dst, self.send.at[sem], self.recv.at[sem], device)
        copy.start()
        self.started.append(copy)

    def arrived(self, dst, sem):
        sem = self.unit * 16 + sem
        remote(dst, dst, self.send.at[sem], self.recv.at[sem], self.sibling).wait_recv()

    def along(self, stage, by):
        return beside(self.pos, self.order[stage], by)

    def at(self, stage, by):
        index = ((self.pos[self.order[stage]] + by) % 4,)
        for later in range(stage + 1, 3):
            index = (self.pos[self.order[later]],) + index
        return (self.unit, self.pos["c"]) + index


class Gather(Unit):
    def __init__(self, pos, order, unit, held, send, recv, started):
        super().__init__(pos, order, unit, send, recv, started)
        self.held = held

    def pass_on(self, index, sem, device):
        self.move(self.held.at[index], self.held.at[index], sem, device)

    def begin(self, stage):
        for by in (1, 3, 2):
            self.pass_on(self.at(stage, 0), stage * 3 + by - 1, self.along(stage, by))
        if stage == 2:
            self.share(0)

    def finish(self, stage):
        for by in (1, 3, 2):
            self.arrived(self.held.at[self.at(stage, 4 - by)], stage * 3 + by - 1)
            if stage == 2:
                self.share(4 - by)

    def share(self, by):
        self.pass_on(self.at(2, by), 9 + by, self.sibling)

    def settle(self):
        place3 = self.pos[self.order[2]]
        for by in (0, 3, 1, 2):
            index = (self.unit, 1 - self.pos["c"], (place3 + by) % 4)
            self.arrived(self.held.at[index], 9 + by)


def wide(value):
    return value.astype(jnp.float32)


class Reduce(Unit):
    def __init__(self, pos, order, unit, held, landing, send, recv, started):
        super().__init__(pos, order, unit, send, recv, started)
        self.held, self.cores, self.coming = held, landing[0], landing[1:]

    def add(self, index, sources, *counts):
        held = self.held

        def one(slot):
            total = wide(held[index + slot])
            for source, at in sources:
                total = total + wide(source[at + slot])
            held[index + slot] = total.astype(jnp.bfloat16)

        def body(i, carry):
            one((i // 4, i % 4) if len(counts) == 2 else (i,))
            return carry

        if counts:
            lax.fori_loop(0, 4 ** len(counts), body, 0)
        else:
            one(())

    def cross(self):
        place3, u = self.pos[self.order[2]], self.unit
        for by in (1, 3, 2, 0):
            index = (place3 + by) % 4
            self.move(
                self.held.at[u, 1 - self.pos["c"], index],
                self.cores.at[u, index],
                9 + by,
                self.sibling,
            )

    def take_core(self, by):
        index = (self.pos[self.order[2]] + by) % 4
        self.arrived(self.cores.at[self.unit, index], 9 + by)
        self.add(self.at(2, by), [(self.cores, (self.unit, index))], 4, 4)

    def begin(self, stage):
        for by in (1, 3, 2):
            if stage == 2:
                self.take_core(by)
            self.move(
                self.held.at[self.at(stage, by)],
                self.coming[stage].at[self.unit, by - 1],
                stage * 3 + by - 1,
                self.along(stage, by),
            )

    def finish(self, stage):
        if stage == 2:
            self.take_core(0)
        for by in (1, 3, 2):
            self.arrived(self.coming[stage].at[self.unit, by - 1], stage * 3 + by - 1)
        self.add(
            self.at(stage, 0),
            [(self.coming[stage], (self.unit, i)) for i in range(3)],
            *(4,) * stage,
        )


def landing_scratch(units, rows):
    low, slot = jnp.bfloat16, (rows, WIDTH)
    return [
        pltpu.VMEM((units, 4, 4, 4) + slot, low),
        pltpu.VMEM((units, 3) + slot, low),
        pltpu.VMEM((units, 3, 4) + slot, low),
        pltpu.VMEM((units, 3, 4, 4) + slot, low),
    ]


def slots_of(group, orders):
    x, z_lo, y_half = group // 4, (group // 2) % 2, group % 2
    for tensor in range(2):
        for piece in range(4):
            at = dict(x=x, z=2 * tensor + z_lo, y=2 * y_half + piece // 2)
            yield tensor, piece, [
                (piece % 2, at[order[2]], at[order[1]], at[order[0]]) for order in orders
            ]


def column_of(tensor, piece):
    return (0, (piece * 2 + tensor) * WIDTH) if piece < 3 else (1, tensor * WIDTH)


def copy_thirds(thirds, whole):
    def body(group, carry):
        for tensor, piece, indices in slots_of(group, THIRDS):
            which, column = column_of(tensor, piece)
            for third, index in enumerate(indices):
                rows = pl.ds(pl.multiple_of(group * SLOT + 16 * third, 16), 16)
                whole[which][rows, pl.ds(column, WIDTH)] = thirds[(third,) + index]
        return carry

    lax.fori_loop(0, 16, body, 0)


def copy_later(slots, whole):
    def body(group, carry):
        for tensor, piece, indices in slots_of(group, LATER):
            columns = pl.ds((tensor * 4 + piece) * WIDTH, WIDTH)
            for u, index in enumerate(indices):
                rows = pl.ds(pl.multiple_of(group * SLOT + 16 * (u % 3), 16), 16)
                whole[u // 3][rows, columns] = slots[(u,) + index]
        return carry

    lax.fori_loop(0, 16, body, 0)


def slot_index(order, group, tensor, piece):
    at = dict(x=group // 4, z=2 * tensor + (group // 2) % 2, y=2 * (group % 2) + piece // 2)
    return (piece % 2, at[order[2]], at[order[1]], at[order[0]])


def fill(slots, first, orders, tensor, piece, value):
    for group in range(16):
        for third, order in enumerate(orders):
            row = group * SLOT + 16 * third
            index = (first + third,) + slot_index(order, group, tensor, piece)
            slots[index] = value[row : row + 16]


def head_place(head):
    member = head % 6
    return (member * 2) % 8 + (member // 4) * (1 + (member % 4) * 2), head // 6


def own_head(ctx, tensor):
    core, y = ctx % 2, ctx // 2
    return tensor * 6 + (1 - core) * y + core * (4 + y // 2), core * (y % 2) == 0


class ToHeads:
    def __init__(self, src, dst, send, recv):
        self.src, self.dst, self.send, self.recv = src, dst, send, recv
        self.dp, self.number = lax.axis_index("dp"), member_number()

    def copies(self, i):
        head = (self.number + i) % HEADS
        ctx, tensor = head_place(head)
        local = 2 * ctx + tensor == self.number
        src, dst = self.src.at[:, head], self.dst.at[self.number]
        recv = self.recv.at[self.number]
        return (
            local,
            lambda: pltpu.make_async_copy(src, dst, recv),
            lambda: remote(src, dst, self.send.at[head], recv, (self.dp, ctx, tensor)),
        )

    def start(self):
        def body(i, carry):
            local, inside, outside = self.copies(i)

            @pl.when(local)
            def _():
                inside().start()

            @pl.when(jnp.logical_not(local))
            def _():
                outside().start()

            return carry

        lax.fori_loop(0, HEADS, body, 0)

    def wait(self, first, last):
        def body(i, carry):
            src, dst, recv = self.src.at[:, 0], self.dst.at[i], self.recv.at[i]

            @pl.when(i == self.number)
            def _():
                pltpu.make_async_copy(src, dst, recv).wait()

            @pl.when(i != self.number)
            def _():
                remote(src, dst, self.send.at[0], recv, (self.dp, i // 2, i % 2)).wait_recv()

            return carry

        lax.fori_loop(first, last, body, 0)

    def sent(self):
        def body(i, carry):
            local, inside, outside = self.copies(i)

            @pl.when(jnp.logical_not(local))
            def _():
                outside().wait_send()

            return carry

        lax.fori_loop(0, HEADS, body, 0)


class FromHeads:
    def __init__(self, src, dst, send, recv):
        self.src, self.dst, self.send, self.recv = src, dst, send, recv
        self.dp, self.number = lax.axis_index("dp"), member_number()
        self.head = own_head(lax.axis_index("ctx"), lax.axis_index("tensor"))[0]

    def outside(self, to):
        return remote(
            self.src.at[to],
            self.dst.at[:, self.head],
            self.send.at[to],
            self.recv.at[self.head],
            (self.dp, to // 2, to % 2),
        )

    def start(self, to):
        @pl.when(to == self.number)
        def _():
            pltpu.make_async_copy(
                self.src.at[to], self.dst.at[:, self.head], self.recv.at[self.head]
            ).start()

        @pl.when(to != self.number)
        def _():
            self.outside(to).start()

    def wait(self):
        def body(i, carry):
            ctx, tensor = head_place(i)
            local = 2 * ctx + tensor == self.number
            src, dst, recv = self.src.at[0], self.dst.at[:, i], self.recv.at[i]

            @pl.when(local)
            def _():
                pltpu.make_async_copy(src, dst, recv).wait()

            @pl.when(jnp.logical_not(local))
            def _():
                remote(src, dst, self.send.at[0], recv, (self.dp, ctx, tensor)).wait_recv()

            return carry

        lax.fori_loop(0, HEADS, body, 0)

    def sent(self):
        def body(i, carry):
            self.outside((self.number + i) % MEMBERS).wait_send()
            return carry

        lax.fori_loop(1, MEMBERS, body, 0)


TILE = 512
TILES = 8


def turned(value):
    return jnp.transpose(value.astype(jnp.float32)).astype(jnp.bfloat16)


def allowed_tile():
    key = lax.broadcasted_iota(jnp.int32, (TILE, TILE), 0)
    query = lax.broadcasted_iota(jnp.int32, (TILE, TILE), 1)
    return query >= key


def two(ref, tile, *index):
    return jnp.concatenate([ref[(2 * tile,) + index], ref[(2 * tile + 1,) + index]], axis=1)


def put_two(ref, tile, part, value):
    ref[2 * tile, part] = value[:, :256]
    ref[2 * tile + 1, part] = value[:, 256:]


def dot(a, b):
    return jnp.dot(a, b, preferred_element_type=jnp.float32)


def dot_right(a, b):
    return lax.dot_general(a, b, (((1,), (1,)), ((), ())), preferred_element_type=jnp.float32)


def attend_tile(i, parts, keys, out, lse):
    own_rows = pl.ds(pl.multiple_of(i * TILE, TILE), TILE)
    keys[own_rows, :] = turned(two(parts, i, 1))
    query = two(parts, i, 0) * jnp.bfloat16(HEAD_DIM ** -0.5)

    def step(scores, values, state):
        top, total, weighted = state
        new_top = jnp.maximum(top, jnp.max(scores, axis=0, keepdims=True))
        fade = jnp.exp(top - new_top)
        raised = jnp.exp(scores - new_top)
        total = total * fade + jnp.sum(raised, axis=0, keepdims=True)
        weighted = weighted * fade + dot(values, raised.astype(jnp.bfloat16))
        return new_top, total, weighted

    def rows_of(j, tiles):
        return keys[pl.ds(pl.multiple_of(j * TILE, TILE), tiles * TILE), :]

    def pair(n, state):
        values = jnp.concatenate([two(parts, 2 * n, 2), two(parts, 2 * n + 1, 2)], axis=1)
        return step(dot(rows_of(2 * n, 2), query), values, state)

    def single(j, state):
        return step(dot(rows_of(j, 1), query), two(parts, j, 2), state)

    state = (
        jnp.full((1, TILE), neg_large, jnp.float32),
        jnp.zeros((1, TILE), jnp.float32),
        jnp.zeros((HEAD_DIM, TILE), jnp.float32),
    )
    state = lax.fori_loop(0, i // 2, pair, state)
    state = lax.fori_loop(2 * (i // 2), i, single, state)
    masked = jnp.where(allowed_tile(), dot(rows_of(i, 1), query), neg_large)
    top, total, weighted = step(masked, two(parts, i, 2), state)
    put_two(out, i, 0, (weighted / total).astype(jnp.bfloat16))
    lse[i] = top + jnp.log(total)


def norm_parts(values):
    center = values - jnp.mean(values, axis=-1, keepdims=True)
    inv_std = lax.rsqrt(jnp.mean(center * center, axis=-1, keepdims=True) + epsilon)
    return center * inv_std, inv_std


def norm_back(upstream, gain_row, normed, inv_std):
    scaled = upstream * gain_row
    return inv_std * (
        scaled
        - jnp.mean(scaled, axis=-1, keepdims=True)
        - normed * jnp.mean(scaled * normed, axis=-1, keepdims=True)
    )


def gelu_and_slope(v):
    scale, cubic = (2.0 / np.pi) ** 0.5, 0.044715
    square = v * v
    bend = jnp.tanh(scale * v * (1.0 + cubic * square))
    half = 0.5 * (1.0 + bend)
    slope = half + (0.5 * scale) * v * (1.0 - bend * bend) * (1.0 + 3.0 * cubic * square)
    return v * half, slope


def owned_columns():
    owner = lax.axis_index("dp") * 8 + lax.axis_index("ctx")
    column = lax.broadcasted_iota(jnp.int32, (ROWS, 768), 1)
    row = lax.broadcasted_iota(jnp.int32, (ROWS, 768), 0)
    return jnp.where(column == owner * ROWS + row, 1.0, 0.0)


def forward_kernel(
    tokens, cotangent, a_qkv, a_out, b, c, gain, select, shuffle,
    normed_out, inv_out, first_out, parts, head_out, lse, attended, gain_out,
    result, second_out, act_out, hid_out, middle_grad, grad_att, gain_two_out, w_qkv,
    pre, thirds, wholes, qkv, out, up, down, projected, keys, ring, pair, forth_sum, back_sum,
    own_gain,
    third_send, third_recv, whole_send, whole_recv, pre_send, pre_recv, small_send, small_recv,
    to_send, to_recv, from_send, from_recv, write_sem,
):
    pos = place()
    active = own_head(lax.axis_index("ctx"), lax.axis_index("tensor"))[1]
    group = Group(pos, pre_send, pre_recv)
    small = SmallSum(pos, ring, pair, small_send, small_recv)
    started = []
    first = [
        Gather(pos, order, u, thirds, third_send, third_recv, started)
        for u, order in enumerate(THIRDS)
    ]
    later = [
        Gather(pos, order, u, wholes, whole_send, whole_recv, started)
        for u, order in enumerate(LATER)
    ]
    spread = ToHeads(projected, parts, to_send, to_recv)
    back = FromHeads(head_out, attended, from_send, from_recv)
    slots = (
        sum(dot(select[j], a_qkv[j]) for j in range(3)) + dot(select[3], a_out[...]),
        sum(dot(select[j], b[:, j * WIDTH : (j + 1) * WIDTH]) for j in range(4)),
        sum(dot(select[j], c[:, j * WIDTH : (j + 1) * WIDTH]) for j in range(4)),
    )
    for k in range(3):
        pre[k, group.member] = slots[k].astype(jnp.bfloat16)
    own_gain[...] = jnp.zeros_like(own_gain)
    own_gain[0:2] = 0.5 * dot(gain[...], owned_columns().astype(jnp.bfloat16))
    greet(pos)
    for k in range(3):
        group.start(pre, k)
    small.start(0, own_gain[...])

    def sorted_piece(k):
        return dot(shuffle[group.member], group.finish(pre, k)).astype(jnp.bfloat16)

    piece = sorted_piece(0)
    for u, unit in enumerate(first):
        thirds[unit.at(0, 0)] = piece[16 * u : 16 * (u + 1)]
        unit.begin(0)
    for k in (1, 2):
        piece = sorted_piece(k)
        for u in range(3):
            wholes[later[3 * k - 3 + u].at(0, 0)] = piece[16 * u : 16 * (u + 1)]
    normed_one, inv_one = norm_parts(wide(tokens[...]))
    normed_out[...] = normed_one
    inv_out[...] = inv_one
    for stage in range(3):
        for unit in first:
            unit.finish(stage)
            if stage < 2:
                unit.begin(stage + 1)
        total = small.finish(stage)
        if stage < 2:
            small.start(stage + 1, total)
        else:
            small.start_pair(total)
        if stage == 1:
            for unit in later:
                unit.begin(0)
    for unit in later:
        unit.finish(0)
        unit.begin(1)
    for unit in first:
        unit.settle()
    copy_thirds(thirds, (qkv, out))
    write = pltpu.make_async_copy(qkv, w_qkv, write_sem)
    write.start()
    gains = small.finish_pair()
    gain_out[...] = gains
    first_in = (normed_out[...] * gains[0:1]).astype(jnp.bfloat16)
    first_out[...] = first_in
    for part in range(3):
        for tensor in range(2):
            column = (part * 2 + tensor) * WIDTH
            cols = jnp.transpose(dot(first_in, qkv[:, pl.ds(column, WIDTH)])).astype(jnp.bfloat16)
            for head in range(6):
                projected[part, tensor * 6 + head] = cols[head * HEAD_DIM : (head + 1) * HEAD_DIM]
    spread.start()
    for unit in later:
        unit.finish(1)
        unit.begin(2)

    def per_queries(i, carry):
        @pl.when(active)
        def _():
            spread.wait(2 * i, 2 * i + 2)
            attend_tile(i, parts, keys, head_out, lse)
            back.start(2 * i)
            back.start(2 * i + 1)

        return carry

    lax.fori_loop(0, 7, per_queries, 0)
    for unit in later:
        unit.finish(2)
    lax.fori_loop(7, 8, per_queries, 0)
    for unit in later:
        unit.settle()
    copy_later(wholes, (up, down))
    back.wait()
    weighted = jnp.transpose(dot(out[...], attended[0].reshape(768, 256)))
    middle = wide(tokens[...]) + weighted
    normed_two, inv_two = norm_parts(middle)
    second_in = (normed_two * gain_out[1:2]).astype(jnp.bfloat16)
    second_out[...] = second_in
    forth_sum[...] = middle
    back_sum[...] = jnp.zeros_like(back_sum)

    def feed(p, carry):
        columns = pl.ds(pl.multiple_of(p * 768, 768), 768)
        act, slope = gelu_and_slope(dot(second_out[...], up[:, columns]))
        act = act.astype(jnp.bfloat16)
        act_out[:, columns] = act
        hid = (dot(cotangent[...], down[:, columns]) * slope).astype(jnp.bfloat16)
        hid_out[:, columns] = hid
        forth_sum[...] += dot_right(act, down[:, columns])
        back_sum[...] += dot_right(hid, up[:, columns])
        return carry

    lax.fori_loop(0, 4, feed, 0)
    result[...] = forth_sum[...].astype(jnp.bfloat16)
    grad_second = back_sum[...]
    gain_two_out[...] = jnp.sum(grad_second * normed_two, axis=0, keepdims=True)
    grad_middle = wide(cotangent[...]) + norm_back(
        grad_second, gain_out[1:2], normed_two, inv_two
    )
    middle_grad[...] = grad_middle
    grads = jnp.transpose(dot(grad_middle.astype(jnp.bfloat16), out[...])).astype(jnp.bfloat16)
    for head in range(HEADS):
        grad_att[0, head] = grads[head * HEAD_DIM : (head + 1) * HEAD_DIM]
    spread.sent()

    @pl.when(active)
    def _():
        back.sent()

    for k in range(3):
        group.sent(pre, k)
    for copy in started:
        copy.wait_send()
    write.wait()


def back_tile(j, parts, grad_att, lse, delta, query_sum, out):
    key_cols, value_cols = two(parts, j, 1), two(parts, j, 2)
    key_rows, value_rows = turned(key_cols), turned(value_cols)

    def step(i, state, diagonal):
        key_sum, value_sum = state
        query = two(parts, i, 0) * jnp.bfloat16(HEAD_DIM ** -0.5)
        grad = two(grad_att, i, 0)
        shares = jnp.exp(dot(key_rows, query) - lse[i])
        if diagonal:
            shares = jnp.where(allowed_tile(), shares, 0.0)
        grad_scores = (shares * (dot(value_rows, grad) - delta[i])).astype(jnp.bfloat16)
        query_sum[i] += dot(key_cols, grad_scores)
        key_sum = key_sum + dot_right(query, grad_scores)
        value_sum = value_sum + dot_right(grad, shares.astype(jnp.bfloat16))
        return key_sum, value_sum

    zero = jnp.zeros((HEAD_DIM, TILE), jnp.float32)
    state = step(j, (zero, zero), True)
    pairs = (TILES - 1 - j) // 2
    rest = j + 1 + 2 * pairs

    def pair(n, state):
        i = j + 1 + 2 * n
        return step(i + 1, step(i, state, False), False)

    state = lax.fori_loop(0, pairs, pair, state)
    key_sum, value_sum = lax.fori_loop(
        rest, TILES, lambda i, state: step(i, state, False), state
    )
    put_two(out, j, 0, (query_sum[j] * HEAD_DIM ** -0.5).astype(jnp.bfloat16))
    put_two(out, j, 1, key_sum.astype(jnp.bfloat16))
    put_two(out, j, 2, value_sum.astype(jnp.bfloat16))


def backward_kernel(
    grad_att, unshuffle, gain, gain_two, inv_one, lse_in, parts_in, head_out_in, act_in, hid_in,
    second_in, cot_in, middle_in, attended_in, first_in, normed_in, w_qkv_in,
    grad_tokens, grad_qkv, grad_out, grad_up, grad_down, grad_gains,
    lse, parts, head_out, act, hid, second, cot, middle, attended, first, normed, w_qkv,
    turned_in, grad_projected, head_grad, head_back, query_sum, delta, wholes, thirds, post,
    cores_w, ends1_w, ends2_w, ends3_w, cores_t, ends1_t, ends2_t, ends3_t, ring, pair,
    load_sem, whole_send, whole_recv, third_send, third_recv, post_send, post_recv,
    small_send, small_recv, to_send, to_recv, from_send, from_recv,
):
    pos = place()
    active = own_head(lax.axis_index("ctx"), lax.axis_index("tensor"))[1]
    group = Group(pos, post_send, post_recv)
    small = SmallSum(pos, ring, pair, small_send, small_recv)
    started = []
    units = [
        Reduce(
            pos, order, u, wholes, (cores_w, ends1_w, ends2_w, ends3_w), whole_send, whole_recv,
            started,
        )
        for u, order in enumerate(LATER)
    ]
    last = [
        Reduce(
            pos, order, u, thirds, (cores_t, ends1_t, ends2_t, ends3_t), third_send, third_recv,
            started,
        )
        for u, order in enumerate(THIRDS)
    ]
    spread = ToHeads(grad_att, head_grad, to_send, to_recv)
    back = FromHeads(head_back, grad_projected, from_send, from_recv)
    loads = [
        pltpu.make_async_copy(src, dst, load_sem.at[n])
        for n, (src, dst) in enumerate(
            (
                (cot_in, cot), (act_in, act), (second_in, second), (hid_in, hid),
                (middle_in, middle), (attended_in, attended), (lse_in, lse), (parts_in, parts),
                (head_out_in, head_out), (first_in, first), (normed_in, normed),
                (w_qkv_in, w_qkv),
            )
        )
    ]
    for load in loads:
        load.start()
    greet(pos)
    spread.start()
    for load in loads[:4]:
        load.wait()

    def flip(n, value):
        turned_in[n] = jnp.transpose(value).astype(jnp.bfloat16)

    flip(0, wide(cot[...]))
    flip(1, wide(second[...]))

    def feed(p, carry):
        columns = pl.ds(pl.multiple_of(p * WIDTH, WIDTH), WIDTH)
        for k, (left, right) in enumerate(((1, hid), (0, act))):
            value = dot(turned_in[left], right[:, columns]).astype(jnp.bfloat16)
            fill(wholes, 3 * k, LATER[3 * k : 3 * k + 3], p // 4, p % 4, value)
        return carry

    lax.fori_loop(0, 8, feed, 0)
    for unit in units:
        unit.cross()
    for load in loads[4:]:
        load.wait()
    flip(0, middle[...])
    flip(1, wide(first[...]))
    for tensor in range(2):
        rows = attended[0, 6 * tensor : 6 * (tensor + 1)].reshape(WIDTH, 256)
        fill(thirds, 0, THIRDS, tensor, 3, dot_right(turned_in[0], rows).astype(jnp.bfloat16))

    @pl.when(active)
    def _():
        spread.wait(0, MEMBERS)

        def prepare(i, carry):
            delta[i] = jnp.sum(
                wide(two(head_out, i, 0)) * wide(two(head_grad, i, 0)), axis=0, keepdims=True
            )
            query_sum[i] = jnp.zeros((HEAD_DIM, TILE), jnp.float32)
            return carry

        lax.fori_loop(0, TILES, prepare, 0)

    def per_keys(j, carry):
        @pl.when(active)
        def _():
            back_tile(j, parts, head_grad, lse, delta, query_sum, head_back)
            back.start(2 * j)
            back.start(2 * j + 1)

        return carry

    lax.fori_loop(0, 1, per_keys, 0)
    for unit in units:
        unit.begin(2)
    lax.fori_loop(1, 5, per_keys, 0)
    for unit in units:
        unit.finish(2)
        unit.begin(1)
    lax.fori_loop(5, 8, per_keys, 0)
    for unit in units:
        unit.finish(1)
        unit.begin(0)
    back.wait()

    def project(p, carry):
        part, tensor = p // 2, p % 2
        rows = grad_projected[part, pl.ds(6 * tensor, 6)].reshape(WIDTH, 256)
        fill(thirds, 0, THIRDS, tensor, part, dot_right(turned_in[1], rows).astype(jnp.bfloat16))
        return carry

    lax.fori_loop(0, 6, project, 0)
    for unit in last:
        unit.cross()
    grad_first = jnp.transpose(dot(w_qkv[...], grad_projected[...].reshape(2304, 256)))
    term = jnp.sum(grad_first * normed[...], axis=0, keepdims=True)
    row = lax.broadcasted_iota(jnp.int32, (8, 768), 0)
    small.start(0, jnp.where(row == 0, term, jnp.where(row == 1, gain_two[...], 0.0)))
    for unit in last:
        unit.begin(2)
    grad_tokens[...] = middle[...] + norm_back(grad_first, gain[0:1], normed[...], inv_one[...])
    for u, unit in enumerate(units):
        unit.finish(0)
        post[u // 3, group.member, pl.ds(16 * (u % 3), 16)] = wholes[unit.at(0, 0)]
    for k in range(2):
        group.start(post, k)
    for stage in (2, 1, 0):
        total = small.finish(2 - stage)
        if stage > 0:
            small.start(3 - stage, total)
        else:
            small.start_pair(total)
        for unit in last:
            unit.finish(stage)
            if stage > 0:
                unit.begin(stage - 1)
    for u, unit in enumerate(last):
        post[2, group.member, pl.ds(16 * u, 16)] = thirds[unit.at(0, 0)]
    group.start(post, 2)
    grad_gains[...] = lax.dot_general(
        small.finish_pair(),
        owned_columns(),
        (((1,), (1,)), ((), ())),
        precision=lax.Precision.HIGHEST,
        preferred_element_type=jnp.float32,
    )[0:2]

    def own_rows(held, piece):
        return dot(unshuffle[group.member, piece], held)

    for k, out in enumerate((grad_up, grad_down)):
        held = group.finish(post, k)
        for piece in range(4):
            out[:, piece * WIDTH : (piece + 1) * WIDTH] = own_rows(held, piece)[:ROWS]
    held = group.finish(post, 2)
    for piece in range(3):
        grad_qkv[piece] = own_rows(held, piece)[:ROWS]
    grad_out[...] = own_rows(held, 3)[:ROWS]
    for k in range(3):
        group.sent(post, k)
    spread.sent()

    @pl.when(active)
    def _():
        back.sent()

    for copy in started:
        copy.wait_send()


def shuffle_matrix():
    matrix = np.zeros((4, SLOT, 4 * SLOT), np.float32)
    for piece in range(4):
        for member in range(4):
            for row in range(ROWS):
                matrix[piece, member * ROWS + row, member * SLOT + piece * ROWS + row] = 1
    return jnp.asarray(matrix, jnp.bfloat16)


def unshuffle_matrix():
    matrix = np.zeros((4, 4, 16, 4 * SLOT), np.float32)
    for member in range(4):
        for piece in range(4):
            for row in range(ROWS):
                matrix[member, piece, row, piece * SLOT + member * ROWS + row] = 1
    return jnp.asarray(matrix, jnp.bfloat16)


def select_matrix():
    matrix = np.zeros((4, SLOT, ROWS), np.float32)
    for piece in range(4):
        for row in range(ROWS):
            matrix[piece, piece * ROWS + row, row] = 1
    return jnp.asarray(matrix, jnp.bfloat16)


def vmem_specs(count):
    return [pl.BlockSpec(memory_space=pltpu.VMEM)] * count


def any_specs(count):
    return [pl.BlockSpec(memory_space=pl.ANY)] * count


def sems(count):
    return [pltpu.SemaphoreType.DMA((count,))] * 2


def low_array(*shape):
    return jax.ShapeDtypeStruct(shape, jnp.bfloat16)


def wide_array(*shape):
    return jax.ShapeDtypeStruct(shape, jnp.float32)


SMALL_SCRATCH = [
    pltpu.VMEM((3, 4, 8, 768), jnp.float32),
    pltpu.VMEM((2, 8, 768), jnp.float32),
]


def kernel_params(number):
    return pltpu.CompilerParams(
        collective_id=number, has_side_effects=True, vmem_limit_bytes=VMEM_BYTES
    )


def forward_pass(tokens, cotangent, shards):
    low = jnp.bfloat16
    return pl.pallas_call(
        forward_kernel,
        name="forward_pass",
        out_shape=[
            wide_array(256, 768),
            wide_array(256, 1),
            low_array(256, 768),
            low_array(MEMBERS, 3, HEAD_DIM, 256),
            low_array(MEMBERS, 1, HEAD_DIM, 256),
            wide_array(TILES, 1, TILE),
            low_array(1, HEADS, HEAD_DIM, 256),
            wide_array(8, 768),
            low_array(256, 768),
            low_array(256, 768),
            low_array(256, 3072),
            low_array(256, 3072),
            wide_array(256, 768),
            low_array(1, HEADS, HEAD_DIM, 256),
            wide_array(1, 768),
            low_array(768, 2304),
        ],
        in_specs=vmem_specs(9),
        out_specs=vmem_specs(15) + any_specs(1),
        scratch_shapes=[
            pltpu.VMEM((3, 4, SLOT, WIDTH), low),
            pltpu.VMEM((3, 2, 4, 4, 4, 16, WIDTH), low),
            pltpu.VMEM((6, 2, 4, 4, 4, 16, WIDTH), low),
            pltpu.VMEM((768, 2304), low),
            pltpu.VMEM((768, 768), low),
            pltpu.VMEM((768, 3072), low),
            pltpu.VMEM((768, 3072), low),
            pltpu.VMEM((3, HEADS, HEAD_DIM, 256), low),
            pltpu.VMEM((TILES * TILE, HEAD_DIM), low),
        ]
        + SMALL_SCRATCH
        + [pltpu.VMEM((256, 768), jnp.float32)] * 2
        + [pltpu.VMEM((8, 768), jnp.float32)]
        + sems(48)
        + sems(96)
        + sems(9)
        + sems(10)
        + sems(MEMBERS)
        + sems(MEMBERS)
        + [pltpu.SemaphoreType.DMA],
        compiler_params=kernel_params(0),
    )(tokens, cotangent, *shards, select_matrix(), shuffle_matrix())


def backward_pass(grad_att, gain, gain_two, inv_one, arrays):
    low = jnp.bfloat16
    return pl.pallas_call(
        backward_kernel,
        name="backward_pass",
        out_shape=[
            wide_array(256, 768),
            wide_array(3, ROWS, WIDTH),
            wide_array(ROWS, WIDTH),
            wide_array(ROWS, 4 * WIDTH),
            wide_array(ROWS, 4 * WIDTH),
            wide_array(2, ROWS),
        ],
        in_specs=any_specs(1) + vmem_specs(4) + any_specs(12),
        out_specs=vmem_specs(6),
        scratch_shapes=[pltpu.VMEM(array.shape, array.dtype) for array in arrays]
        + [
            pltpu.VMEM((2, 768, 256), low),
            pltpu.VMEM((3, HEADS, HEAD_DIM, 256), low),
            pltpu.VMEM((MEMBERS, 1, HEAD_DIM, 256), low),
            pltpu.VMEM((MEMBERS, 3, HEAD_DIM, 256), low),
            pltpu.VMEM((TILES, HEAD_DIM, TILE), jnp.float32),
            pltpu.VMEM((TILES, 1, TILE), jnp.float32),
            pltpu.VMEM((6, 2, 4, 4, 4, 16, WIDTH), low),
            pltpu.VMEM((3, 2, 4, 4, 4, 16, WIDTH), low),
            pltpu.VMEM((3, 4, SLOT, WIDTH), low),
        ]
        + landing_scratch(6, 16)
        + landing_scratch(3, 16)
        + SMALL_SCRATCH
        + [pltpu.SemaphoreType.DMA((12,))]
        + sems(96)
        + sems(48)
        + sems(9)
        + sems(10)
        + sems(MEMBERS)
        + sems(MEMBERS),
        compiler_params=kernel_params(1),
    )(grad_att, unshuffle_matrix(), gain, gain_two, inv_one, *arrays)


def per_device(tokens, cotangent, w_qkv, w_out, w_up, w_down, norm_gains):
    (
        normed_one, inv_one, first_in, parts, head_out, lse, attended, gains,
        result, second_in, act, hid, grad_middle, grad_att, gain_two_term, qkv,
    ) = forward_pass(tokens, cotangent, (w_qkv, w_out.T, w_up, w_down.T, norm_gains))
    grad_tokens, grad_qkv, grad_out, grad_up, grad_down, grad_gains = backward_pass(
        grad_att,
        gains,
        gain_two_term,
        inv_one,
        (
            lse, parts, head_out, act, hid, second_in, cotangent, grad_middle, attended,
            first_in, normed_one, qkv,
        ),
    )
    return (result, grad_tokens, grad_qkv, grad_out.T, grad_up, grad_down.T, grad_gains)


def solution(mesh):
    return jax.shard_map(
        per_device,
        mesh=mesh,
        in_specs=(
            P(("dp", "ctx", "tensor"), None),
            P(("dp", "ctx", "tensor"), None),
            P(None, ("dp", "ctx"), "tensor"),
            P("tensor", ("dp", "ctx")),
            P(("dp", "ctx"), "tensor"),
            P("tensor", ("dp", "ctx")),
            P(None, ("dp", "ctx")),
        ),
        out_specs=(
            P(("dp", "ctx", "tensor"), None),
            P(("dp", "ctx", "tensor"), None),
            P(None, ("dp", "ctx"), "tensor"),
            P("tensor", ("dp", "ctx")),
            P(("dp", "ctx"), "tensor"),
            P("tensor", ("dp", "ctx")),
            P(None, ("dp", "ctx")),
        ),
        check_vma=False,
    )
```

```python
import functools

import jax
import jax.numpy as jnp
import numpy as np
from jax import lax
from jax.experimental import pallas as pl
from jax.experimental.pallas import tpu as pltpu
from jax.sharding import PartitionSpec as P

HEAD_DIM = 64
HEADS = 12
MEMBERS = 16
ROWS = 12
WIDTH = 384
SLOT = 4 * ROWS
THIRDS = (("z", "x", "y"), ("x", "y", "z"), ("y", "z", "x"))
LATER = THIRDS + (("z", "y", "x"), ("y", "x", "z"), ("z", "y", "x"))
MESH = pl.DeviceIdType.MESH
VMEM_BYTES = 60 * 1024 * 1024
epsilon = 1e-05
neg_large = -1e30


def place():
    dp, ctx, tensor = lax.axis_index("dp"), lax.axis_index("ctx"), lax.axis_index("tensor")
    return dict(x=dp // 2, y=ctx // 2, z=2 * tensor + dp % 2, c=ctx % 2)


def device_at(pos, axis, index):
    at = dict(pos)
    at[axis] = index
    return (at["x"] * 2 + at["z"] % 2, at["y"] * 2 + at["c"], at["z"] // 2)


def beside(pos, axis, by):
    if axis == "c":
        return device_at(pos, "c", 1 - pos["c"])
    return device_at(pos, axis, (pos[axis] + by) % 4)


def greet(pos):
    barrier = pltpu.get_barrier_semaphore()
    dp, number = lax.axis_index("dp"), member_number()

    def signal(i, carry):
        to = (number + i) % MEMBERS
        pl.semaphore_signal(
            barrier, inc=1, device_id=(dp, to // 2, to % 2), device_id_type=MESH
        )
        return carry

    lax.fori_loop(1, MEMBERS, signal, 0)
    for axis, by in (("x", 1), ("x", 2), ("x", 3), ("z", 1), ("z", 3)):
        pl.semaphore_signal(barrier, inc=1, device_id=beside(pos, axis, by), device_id_type=MESH)
    pl.semaphore_wait(barrier, MEMBERS - 1 + 5)


def member_number():
    return 2 * lax.axis_index("ctx") + lax.axis_index("tensor")


def remote(src, dst, send, recv, device):
    return pltpu.make_async_remote_copy(
        src_ref=src,
        dst_ref=dst,
        send_sem=send,
        recv_sem=recv,
        device_id=device,
        device_id_type=MESH,
    )


class SmallSum:
    def __init__(self, pos, ring, pair, send, recv):
        self.pos, self.ring, self.pair, self.send, self.recv = pos, ring, pair, send, recv

    def copy(self, n, by, coming=False):
        axis = ("x", "y", "z")[n]
        slot = (self.pos[axis] + 4 - by) % 4 if coming else self.pos[axis]
        ref, sem = self.ring.at[n, slot], n * 3 + by - 1
        return remote(
            ref, ref, self.send.at[sem], self.recv.at[sem], beside(self.pos, axis, by)
        )

    def start(self, n, value):
        self.ring[n, self.pos[("x", "y", "z")[n]]] = value
        for by in (1, 2, 3):
            self.copy(n, by).start()

    def finish(self, n):
        for by in (1, 2, 3):
            self.copy(n, by, coming=True).wait_recv()
            self.copy(n, by).wait_send()
        return (self.ring[n, 0] + self.ring[n, 1]) + (self.ring[n, 2] + self.ring[n, 3])

    def pair_copy(self, slot):
        ref = self.pair.at[slot]
        return remote(ref, ref, self.send.at[9], self.recv.at[9], beside(self.pos, "c", 1))

    def start_pair(self, value):
        self.pair[self.pos["c"]] = value
        self.pair_copy(self.pos["c"]).start()

    def finish_pair(self):
        self.pair_copy(1 - self.pos["c"]).wait_recv()
        self.pair_copy(self.pos["c"]).wait_send()
        return self.pair[0] + self.pair[1]


class Group:
    def __init__(self, pos, send, recv):
        self.pos, self.send, self.recv = pos, send, recv
        self.member = (pos["y"] % 2) * 2 + pos["c"]
        y = pos["y"] + 1 - 2 * (pos["y"] % 2)
        c = 1 - pos["c"]
        self.partners = []
        for to_y, to_c in ((pos["y"], c), (y, pos["c"]), (y, c)):
            device = device_at({**pos, "y": to_y}, "c", to_c)
            self.partners.append((device, (to_y % 2) * 2 + to_c))

    def copy(self, held, k, i, coming=False):
        device, member = self.partners[i]
        ref = held.at[k, member if coming else self.member]
        return remote(ref, ref, self.send.at[k * 3 + i], self.recv.at[k * 3 + i], device)

    def start(self, held, k):
        for i in range(3):
            self.copy(held, k, i).start()

    def finish(self, held, k):
        for i in range(3):
            self.copy(held, k, i, coming=True).wait_recv()
        return jnp.concatenate([held[k, member] for member in range(4)], axis=0)

    def sent(self, held, k):
        for i in range(3):
            self.copy(held, k, i).wait_send()


class Unit:
    def __init__(self, pos, order, unit, send, recv, started):
        self.pos, self.order, self.unit = pos, order, unit
        self.send, self.recv, self.started = send, recv, started
        self.sibling = beside(pos, "c", 1)

    def move(self, src, dst, sem, device):
        sem = self.unit * 16 + sem
        copy = remote(src, dst, self.send.at[sem], self.recv.at[sem], device)
        copy.start()
        self.started.append(copy)

    def arrived(self, dst, sem):
        sem = self.unit * 16 + sem
        remote(dst, dst, self.send.at[sem], self.recv.at[sem], self.sibling).wait_recv()

    def along(self, stage, by):
        return beside(self.pos, self.order[stage], by)

    def at(self, stage, by):
        index = ((self.pos[self.order[stage]] + by) % 4,)
        for later in range(stage + 1, 3):
            index = (self.pos[self.order[later]],) + index
        return (self.unit, self.pos["c"]) + index


class Gather(Unit):
    def __init__(self, pos, order, unit, held, send, recv, started):
        super().__init__(pos, order, unit, send, recv, started)
        self.held = held

    def pass_on(self, index, sem, device):
        self.move(self.held.at[index], self.held.at[index], sem, device)

    def begin(self, stage):
        for by in (1, 3, 2):
            self.pass_on(self.at(stage, 0), stage * 3 + by - 1, self.along(stage, by))
        if stage == 2:
            self.share(0)

    def finish(self, stage):
        for by in (1, 3, 2):
            self.arrived(self.held.at[self.at(stage, 4 - by)], stage * 3 + by - 1)
            if stage == 2:
                self.share(4 - by)

    def share(self, by):
        self.pass_on(self.at(2, by), 9 + by, self.sibling)

    def settle(self):
        place3 = self.pos[self.order[2]]
        for by in (0, 3, 1, 2):
            index = (self.unit, 1 - self.pos["c"], (place3 + by) % 4)
            self.arrived(self.held.at[index], 9 + by)


def wide(value):
    return value.astype(jnp.float32)


class Reduce(Unit):
    def __init__(self, pos, order, unit, held, landing, send, recv, started):
        super().__init__(pos, order, unit, send, recv, started)
        self.held, self.cores, self.coming = held, landing[0], landing[1:]

    def add(self, index, sources, *counts):
        held = self.held

        def one(slot):
            total = wide(held[index + slot])
            for source, at in sources:
                total = total + wide(source[at + slot])
            held[index + slot] = total.astype(jnp.bfloat16)

        def body(i, carry):
            one((i // 4, i % 4) if len(counts) == 2 else (i,))
            return carry

        if counts:
            lax.fori_loop(0, 4 ** len(counts), body, 0)
        else:
            one(())

    def cross(self):
        place3, u = self.pos[self.order[2]], self.unit
        for by in (1, 3, 2, 0):
            index = (place3 + by) % 4
            self.move(
                self.held.at[u, 1 - self.pos["c"], index],
                self.cores.at[u, index],
                9 + by,
                self.sibling,
            )

    def take_core(self, by):
        index = (self.pos[self.order[2]] + by) % 4
        self.arrived(self.cores.at[self.unit, index], 9 + by)
        self.add(self.at(2, by), [(self.cores, (self.unit, index))], 4, 4)

    def begin(self, stage):
        for by in (1, 3, 2):
            if stage == 2:
                self.take_core(by)
            self.move(
                self.held.at[self.at(stage, by)],
                self.coming[stage].at[self.unit, by - 1],
                stage * 3 + by - 1,
                self.along(stage, by),
            )

    def finish(self, stage):
        if stage == 2:
            self.take_core(0)
        for by in (1, 3, 2):
            self.arrived(self.coming[stage].at[self.unit, by - 1], stage * 3 + by - 1)
        self.add(
            self.at(stage, 0),
            [(self.coming[stage], (self.unit, i)) for i in range(3)],
            *(4,) * stage,
        )


def landing_scratch(units, rows):
    low, slot = jnp.bfloat16, (rows, WIDTH)
    return [
        pltpu.VMEM((units, 4, 4, 4) + slot, low),
        pltpu.VMEM((units, 3) + slot, low),
        pltpu.VMEM((units, 3, 4) + slot, low),
        pltpu.VMEM((units, 3, 4, 4) + slot, low),
    ]


def slots_of(group, orders):
    x, z_lo, y_half = group // 4, (group // 2) % 2, group % 2
    for tensor in range(2):
        for piece in range(4):
            at = dict(x=x, z=2 * tensor + z_lo, y=2 * y_half + piece // 2)
            yield tensor, piece, [
                (piece % 2, at[order[2]], at[order[1]], at[order[0]]) for order in orders
            ]


def column_of(tensor, piece):
    return (0, (piece * 2 + tensor) * WIDTH) if piece < 3 else (1, tensor * WIDTH)


def copy_thirds(thirds, whole):
    def body(group, carry):
        for tensor, piece, indices in slots_of(group, THIRDS):
            which, column = column_of(tensor, piece)
            for third, index in enumerate(indices):
                rows = pl.ds(pl.multiple_of(group * SLOT + 16 * third, 16), 16)
                whole[which][rows, pl.ds(column, WIDTH)] = thirds[(third,) + index]
        return carry

    lax.fori_loop(0, 16, body, 0)


def slot_index(order, group, tensor, piece):
    at = dict(x=group // 4, z=2 * tensor + (group // 2) % 2, y=2 * (group % 2) + piece // 2)
    return (piece % 2, at[order[2]], at[order[1]], at[order[0]])


def collect(slots, first, orders, tensor, piece):
    return jnp.concatenate(
        [
            slots[(first + third,) + slot_index(order, group, tensor, piece)]
            for group in range(16)
            for third, order in enumerate(orders)
        ],
        axis=0,
    )


def fill(slots, first, orders, tensor, piece, value):
    for group in range(16):
        for third, order in enumerate(orders):
            row = group * SLOT + 16 * third
            index = (first + third,) + slot_index(order, group, tensor, piece)
            slots[index] = value[row : row + 16]


def head_place(head):
    member = head % 6
    return (member * 2) % 8 + (member // 4) * (1 + (member % 4) * 2), head // 6


def own_head(ctx, tensor):
    core, y = ctx % 2, ctx // 2
    return tensor * 6 + (1 - core) * y + core * (4 + y // 2), core * (y % 2) == 0


class ToHeads:
    def __init__(self, src, dst, send, recv):
        self.src, self.dst, self.send, self.recv = src, dst, send, recv
        self.dp, self.number = lax.axis_index("dp"), member_number()

    def copies(self, i):
        head = (self.number + i) % HEADS
        ctx, tensor = head_place(head)
        local = 2 * ctx + tensor == self.number
        src, dst = self.src.at[:, head], self.dst.at[self.number]
        recv = self.recv.at[self.number]
        return (
            local,
            lambda: pltpu.make_async_copy(src, dst, recv),
            lambda: remote(src, dst, self.send.at[head], recv, (self.dp, ctx, tensor)),
        )

    def start(self):
        def body(i, carry):
            local, inside, outside = self.copies(i)

            @pl.when(local)
            def _():
                inside().start()

            @pl.when(jnp.logical_not(local))
            def _():
                outside().start()

            return carry

        lax.fori_loop(0, HEADS, body, 0)

    def wait(self, first, last):
        def body(i, carry):
            src, dst, recv = self.src.at[:, 0], self.dst.at[i], self.recv.at[i]

            @pl.when(i == self.number)
            def _():
                pltpu.make_async_copy(src, dst, recv).wait()

            @pl.when(i != self.number)
            def _():
                remote(src, dst, self.send.at[0], recv, (self.dp, i // 2, i % 2)).wait_recv()

            return carry

        lax.fori_loop(first, last, body, 0)

    def sent(self):
        def body(i, carry):
            local, inside, outside = self.copies(i)

            @pl.when(jnp.logical_not(local))
            def _():
                outside().wait_send()

            return carry

        lax.fori_loop(0, HEADS, body, 0)


class FromHeads:
    def __init__(self, src, dst, send, recv):
        self.src, self.dst, self.send, self.recv = src, dst, send, recv
        self.dp, self.number = lax.axis_index("dp"), member_number()
        self.head = own_head(lax.axis_index("ctx"), lax.axis_index("tensor"))[0]

    def outside(self, to):
        return remote(
            self.src.at[to],
            self.dst.at[:, self.head],
            self.send.at[to],
            self.recv.at[self.head],
            (self.dp, to // 2, to % 2),
        )

    def start(self, to):
        @pl.when(to == self.number)
        def _():
            pltpu.make_async_copy(
                self.src.at[to], self.dst.at[:, self.head], self.recv.at[self.head]
            ).start()

        @pl.when(to != self.number)
        def _():
            self.outside(to).start()

    def wait(self):
        def body(i, carry):
            ctx, tensor = head_place(i)
            local = 2 * ctx + tensor == self.number
            src, dst, recv = self.src.at[0], self.dst.at[:, i], self.recv.at[i]

            @pl.when(local)
            def _():
                pltpu.make_async_copy(src, dst, recv).wait()

            @pl.when(jnp.logical_not(local))
            def _():
                remote(src, dst, self.send.at[0], recv, (self.dp, ctx, tensor)).wait_recv()

            return carry

        lax.fori_loop(0, HEADS, body, 0)

    def sent(self):
        def body(i, carry):
            self.outside((self.number + i) % MEMBERS).wait_send()
            return carry

        lax.fori_loop(1, MEMBERS, body, 0)


TILE = 512
TILES = 8


def turned(value):
    return jnp.transpose(value.astype(jnp.float32)).astype(jnp.bfloat16)


def allowed_tile():
    key = lax.broadcasted_iota(jnp.int32, (TILE, TILE), 0)
    query = lax.broadcasted_iota(jnp.int32, (TILE, TILE), 1)
    return query >= key


def two(ref, tile, *index):
    return jnp.concatenate([ref[(2 * tile,) + index], ref[(2 * tile + 1,) + index]], axis=1)


def put_two(ref, tile, part, value):
    ref[2 * tile, part] = value[:, :256]
    ref[2 * tile + 1, part] = value[:, 256:]


def dot(a, b):
    return jnp.dot(a, b, preferred_element_type=jnp.float32)


def dot_right(a, b):
    return lax.dot_general(a, b, (((1,), (1,)), ((), ())), preferred_element_type=jnp.float32)


def attend_tile(i, parts, keys, out, lse):
    own_rows = pl.ds(pl.multiple_of(i * TILE, TILE), TILE)
    keys[own_rows, :] = turned(two(parts, i, 1))
    query = two(parts, i, 0) * jnp.bfloat16(HEAD_DIM ** -0.5)

    def step(scores, values, state):
        top, total, weighted = state
        new_top = jnp.maximum(top, jnp.max(scores, axis=0, keepdims=True))
        fade = jnp.exp(top - new_top)
        raised = jnp.exp(scores - new_top)
        total = total * fade + jnp.sum(raised, axis=0, keepdims=True)
        weighted = weighted * fade + dot(values, raised.astype(jnp.bfloat16))
        return new_top, total, weighted

    def rows_of(j, tiles):
        return keys[pl.ds(pl.multiple_of(j * TILE, TILE), tiles * TILE), :]

    def pair(n, state):
        values = jnp.concatenate([two(parts, 2 * n, 2), two(parts, 2 * n + 1, 2)], axis=1)
        return step(dot(rows_of(2 * n, 2), query), values, state)

    def single(j, state):
        return step(dot(rows_of(j, 1), query), two(parts, j, 2), state)

    state = (
        jnp.full((1, TILE), neg_large, jnp.float32),
        jnp.zeros((1, TILE), jnp.float32),
        jnp.zeros((HEAD_DIM, TILE), jnp.float32),
    )
    state = lax.fori_loop(0, i // 2, pair, state)
    state = lax.fori_loop(2 * (i // 2), i, single, state)
    masked = jnp.where(allowed_tile(), dot(rows_of(i, 1), query), neg_large)
    top, total, weighted = step(masked, two(parts, i, 2), state)
    put_two(out, i, 0, (weighted / total).astype(jnp.bfloat16))
    lse[i] = top + jnp.log(total)


def norm_parts(values):
    center = values - jnp.mean(values, axis=-1, keepdims=True)
    inv_std = lax.rsqrt(jnp.mean(center * center, axis=-1, keepdims=True) + epsilon)
    return center * inv_std, inv_std


def norm_back(upstream, gain_row, normed, inv_std):
    scaled = upstream * gain_row
    return inv_std * (
        scaled
        - jnp.mean(scaled, axis=-1, keepdims=True)
        - normed * jnp.mean(scaled * normed, axis=-1, keepdims=True)
    )


def gelu_and_slope(v):
    scale, cubic = (2.0 / np.pi) ** 0.5, 0.044715
    square = v * v
    bend = jnp.tanh(scale * v * (1.0 + cubic * square))
    half = 0.5 * (1.0 + bend)
    slope = half + (0.5 * scale) * v * (1.0 - bend * bend) * (1.0 + 3.0 * cubic * square)
    return v * half, slope


def owned_columns():
    owner = lax.axis_index("dp") * 8 + lax.axis_index("ctx")
    column = lax.broadcasted_iota(jnp.int32, (ROWS, 768), 1)
    row = lax.broadcasted_iota(jnp.int32, (ROWS, 768), 0)
    return jnp.where(column == owner * ROWS + row, 1.0, 0.0)


def back_tile(j, parts, grad_att, lse, delta, query_sum, out):
    key_cols, value_cols = two(parts, j, 1), two(parts, j, 2)
    key_rows, value_rows = turned(key_cols), turned(value_cols)

    def step(i, state, diagonal):
        key_sum, value_sum = state
        query = two(parts, i, 0) * jnp.bfloat16(HEAD_DIM ** -0.5)
        grad = two(grad_att, i, 0)
        shares = jnp.exp(dot(key_rows, query) - lse[i])
        if diagonal:
            shares = jnp.where(allowed_tile(), shares, 0.0)
        grad_scores = (shares * (dot(value_rows, grad) - delta[i])).astype(jnp.bfloat16)
        query_sum[i] += dot(key_cols, grad_scores)
        key_sum = key_sum + dot_right(query, grad_scores)
        value_sum = value_sum + dot_right(grad, shares.astype(jnp.bfloat16))
        return key_sum, value_sum

    zero = jnp.zeros((HEAD_DIM, TILE), jnp.float32)
    state = step(j, (zero, zero), True)
    pairs = (TILES - 1 - j) // 2
    rest = j + 1 + 2 * pairs

    def pair(n, state):
        i = j + 1 + 2 * n
        return step(i + 1, step(i, state, False), False)

    state = lax.fori_loop(0, pairs, pair, state)
    key_sum, value_sum = lax.fori_loop(
        rest, TILES, lambda i, state: step(i, state, False), state
    )
    put_two(out, j, 0, (query_sum[j] * HEAD_DIM ** -0.5).astype(jnp.bfloat16))
    put_two(out, j, 1, key_sum.astype(jnp.bfloat16))
    put_two(out, j, 2, value_sum.astype(jnp.bfloat16))


def layer_kernel(
    tokens, cotangent, a_qkv, a_out, b, c, gain, select, shuffle, unshuffle,
    result, grad_tokens, grad_qkv, grad_out, grad_up, grad_down, grad_gains,
    pre, thirds, wholes, qkv, out, projected, keys, ring, pair, last_ring, last_pair,
    forth_sum, back_sum, own_gain, kept_gains, normed, parts, head_out, lse, attended, second,
    act, hid, middle_grad, grad_att, turned_in, grad_projected, head_grad, head_back,
    query_sum, delta, post,
    cores_w, ends1_w, ends2_w, ends3_w, cores_t, ends1_t, ends2_t, ends3_t,
    third_send, third_recv, whole_send, whole_recv, pre_send, pre_recv, small_send, small_recv,
    to_send, to_recv, from_send, from_recv,
    back_third_send, back_third_recv, back_whole_send, back_whole_recv, post_send, post_recv,
    last_small_send, last_small_recv, to_grad_send, to_grad_recv, from_grad_send, from_grad_recv,
):
    pos = place()
    active = own_head(lax.axis_index("ctx"), lax.axis_index("tensor"))[1]
    group = Group(pos, pre_send, pre_recv)
    owners = Group(pos, post_send, post_recv)
    small = SmallSum(pos, ring, pair, small_send, small_recv)
    last_small = SmallSum(pos, last_ring, last_pair, last_small_send, last_small_recv)
    started = []
    first = [
        Gather(pos, order, u, thirds, third_send, third_recv, started)
        for u, order in enumerate(THIRDS)
    ]
    later = [
        Gather(pos, order, u, wholes, whole_send, whole_recv, started)
        for u, order in enumerate(LATER)
    ]
    spread = ToHeads(projected, parts, to_send, to_recv)
    back = FromHeads(head_out, attended, from_send, from_recv)
    head_spread = ToHeads(grad_att, head_grad, to_grad_send, to_grad_recv)
    head_return = FromHeads(head_back, grad_projected, from_grad_send, from_grad_recv)
    slots = (
        sum(dot(select[j], a_qkv[j]) for j in range(3)) + dot(select[3], a_out[...]),
        sum(dot(select[j], b[:, j * WIDTH : (j + 1) * WIDTH]) for j in range(4)),
        sum(dot(select[j], c[:, j * WIDTH : (j + 1) * WIDTH]) for j in range(4)),
    )
    for k in range(3):
        pre[k, group.member] = slots[k].astype(jnp.bfloat16)
    own_gain[...] = jnp.zeros_like(own_gain)
    own_gain[0:2] = 0.5 * dot(gain[...], owned_columns().astype(jnp.bfloat16))
    greet(pos)
    for k in range(3):
        group.start(pre, k)
    small.start(0, own_gain[...])

    def sorted_piece(k):
        return dot(shuffle[group.member], group.finish(pre, k)).astype(jnp.bfloat16)

    piece = sorted_piece(0)
    for u, unit in enumerate(first):
        thirds[unit.at(0, 0)] = piece[16 * u : 16 * (u + 1)]
        unit.begin(0)
    for k in (1, 2):
        piece = sorted_piece(k)
        for u in range(3):
            wholes[later[3 * k - 3 + u].at(0, 0)] = piece[16 * u : 16 * (u + 1)]
    normed_one, inv_one = norm_parts(wide(tokens[...]))
    normed[...] = normed_one
    for stage in range(3):
        for unit in first:
            unit.finish(stage)
            if stage < 2:
                unit.begin(stage + 1)
        total = small.finish(stage)
        if stage < 2:
            small.start(stage + 1, total)
        else:
            small.start_pair(total)
        if stage == 1:
            for unit in later:
                unit.begin(0)
    for unit in later:
        unit.finish(0)
        unit.begin(1)
    for unit in first:
        unit.settle()
    copy_thirds(thirds, (qkv, out))
    gains = small.finish_pair()
    kept_gains[...] = gains
    first_in = (normed[...] * gains[0:1]).astype(jnp.bfloat16)
    for part in range(3):
        for tensor in range(2):
            column = (part * 2 + tensor) * WIDTH
            cols = jnp.transpose(dot(first_in, qkv[:, pl.ds(column, WIDTH)])).astype(jnp.bfloat16)
            for head in range(6):
                projected[part, tensor * 6 + head] = cols[head * HEAD_DIM : (head + 1) * HEAD_DIM]
    spread.start()
    for unit in later:
        unit.finish(1)
        unit.begin(2)

    def flip(n, value):
        turned_in[n] = jnp.transpose(value).astype(jnp.bfloat16)

    flip(0, wide(cotangent[...]))
    flip(1, wide(first_in))

    def per_queries(i, carry):
        @pl.when(active)
        def _():
            spread.wait(2 * i, 2 * i + 2)
            attend_tile(i, parts, keys, head_out, lse)
            back.start(2 * i)
            back.start(2 * i + 1)

        return carry

    lax.fori_loop(0, 7, per_queries, 0)
    for unit in later:
        unit.finish(2)
    lax.fori_loop(7, 8, per_queries, 0)
    for unit in later:
        unit.settle()
    back.wait()
    weighted = jnp.transpose(dot(out[...], attended[0].reshape(768, 256)))
    middle = wide(tokens[...]) + weighted
    normed_two, inv_two = norm_parts(middle)
    second_in = (normed_two * kept_gains[1:2]).astype(jnp.bfloat16)
    second[...] = second_in
    forth_sum[...] = middle
    back_sum[...] = jnp.zeros_like(back_sum)

    def feed(p, carry):
        columns = pl.ds(pl.multiple_of(p * WIDTH, WIDTH), WIDTH)
        up = collect(wholes, 0, LATER[:3], p // 4, p % 4)
        down = collect(wholes, 3, LATER[3:], p // 4, p % 4)
        bent, slope = gelu_and_slope(dot(second[...], up))
        bent = bent.astype(jnp.bfloat16)
        act[:, columns] = bent
        low = (dot(cotangent[...], down) * slope).astype(jnp.bfloat16)
        hid[:, columns] = low
        forth_sum[...] += dot_right(bent, down)
        back_sum[...] += dot_right(low, up)
        return carry

    lax.fori_loop(0, 8, feed, 0)
    result[...] = forth_sum[...].astype(jnp.bfloat16)
    grad_second = back_sum[...]
    gain_two_term = jnp.sum(grad_second * normed_two, axis=0, keepdims=True)
    grad_middle = wide(cotangent[...]) + norm_back(
        grad_second, kept_gains[1:2], normed_two, inv_two
    )
    middle_grad[...] = grad_middle
    kept_gains[2:3] = gain_two_term
    grads = jnp.transpose(dot(grad_middle.astype(jnp.bfloat16), out[...])).astype(jnp.bfloat16)
    for head in range(HEADS):
        grad_att[0, head] = grads[head * HEAD_DIM : (head + 1) * HEAD_DIM]
    head_spread.start()
    flip(2, wide(second[...]))
    flip(3, middle_grad[...])
    spread.sent()

    @pl.when(active)
    def _():
        back.sent()

    for k in range(3):
        group.sent(pre, k)
    for copy in started:
        copy.wait_send()
    started = []
    units = [
        Reduce(
            pos, order, u, wholes, (cores_w, ends1_w, ends2_w, ends3_w), back_whole_send, back_whole_recv,
            started,
        )
        for u, order in enumerate(LATER)
    ]
    last = [
        Reduce(
            pos, order, u, thirds, (cores_t, ends1_t, ends2_t, ends3_t), back_third_send, back_third_recv,
            started,
        )
        for u, order in enumerate(THIRDS)
    ]
    def give(p, carry):
        columns = pl.ds(pl.multiple_of(p * WIDTH, WIDTH), WIDTH)
        for k, (left, right) in enumerate(((2, hid), (0, act))):
            value = dot(turned_in[left], right[:, columns]).astype(jnp.bfloat16)
            fill(wholes, 3 * k, LATER[3 * k : 3 * k + 3], p // 4, p % 4, value)
        return carry

    lax.fori_loop(0, 8, give, 0)
    for unit in units:
        unit.cross()
    for tensor in range(2):
        rows = attended[0, 6 * tensor : 6 * (tensor + 1)].reshape(WIDTH, 256)
        fill(thirds, 0, THIRDS, tensor, 3, dot_right(turned_in[3], rows).astype(jnp.bfloat16))

    @pl.when(active)
    def _():
        head_spread.wait(0, MEMBERS)

        def prepare(i, carry):
            delta[i] = jnp.sum(
                wide(two(head_out, i, 0)) * wide(two(head_grad, i, 0)), axis=0, keepdims=True
            )
            query_sum[i] = jnp.zeros((HEAD_DIM, TILE), jnp.float32)
            return carry

        lax.fori_loop(0, TILES, prepare, 0)

    def per_keys(j, carry):
        @pl.when(active)
        def _():
            back_tile(j, parts, head_grad, lse, delta, query_sum, head_back)
            head_return.start(2 * j)
            head_return.start(2 * j + 1)

        return carry

    lax.fori_loop(0, 1, per_keys, 0)
    for unit in units:
        unit.begin(2)
    lax.fori_loop(1, 5, per_keys, 0)
    for unit in units:
        unit.finish(2)
        unit.begin(1)
    lax.fori_loop(5, 8, per_keys, 0)
    for unit in units:
        unit.finish(1)
        unit.begin(0)
    head_return.wait()

    def project(p, carry):
        part, tensor = p // 2, p % 2
        rows = grad_projected[part, pl.ds(6 * tensor, 6)].reshape(WIDTH, 256)
        fill(thirds, 0, THIRDS, tensor, part, dot_right(turned_in[1], rows).astype(jnp.bfloat16))
        return carry

    lax.fori_loop(0, 6, project, 0)
    for unit in last:
        unit.cross()
    grad_first = jnp.transpose(dot(qkv[...], grad_projected[...].reshape(2304, 256)))
    term = jnp.sum(grad_first * normed[...], axis=0, keepdims=True)
    row = lax.broadcasted_iota(jnp.int32, (8, 768), 0)
    last_small.start(0, jnp.where(row == 0, term, jnp.where(row == 1, kept_gains[2:3], 0.0)))
    for unit in last:
        unit.begin(2)
    grad_tokens[...] = middle_grad[...] + norm_back(
        grad_first, kept_gains[0:1], normed[...], inv_one
    )
    for u, unit in enumerate(units):
        unit.finish(0)
        post[u // 3, owners.member, pl.ds(16 * (u % 3), 16)] = wholes[unit.at(0, 0)]
    for k in range(2):
        owners.start(post, k)
    for stage in (2, 1, 0):
        total = last_small.finish(2 - stage)
        if stage > 0:
            last_small.start(3 - stage, total)
        else:
            last_small.start_pair(total)
        for unit in last:
            unit.finish(stage)
            if stage > 0:
                unit.begin(stage - 1)
    for u, unit in enumerate(last):
        post[2, owners.member, pl.ds(16 * u, 16)] = thirds[unit.at(0, 0)]
    owners.start(post, 2)
    grad_gains[...] = lax.dot_general(
        last_small.finish_pair(),
        owned_columns(),
        (((1,), (1,)), ((), ())),
        precision=lax.Precision.HIGHEST,
        preferred_element_type=jnp.float32,
    )[0:2]

    def own_rows(held, piece):
        return dot(unshuffle[owners.member, piece], held)

    for k, out in enumerate((grad_up, grad_down)):
        held = owners.finish(post, k)
        for piece in range(4):
            out[:, piece * WIDTH : (piece + 1) * WIDTH] = own_rows(held, piece)[:ROWS]
    held = owners.finish(post, 2)
    for piece in range(3):
        grad_qkv[piece] = own_rows(held, piece)[:ROWS]
    grad_out[...] = own_rows(held, 3)[:ROWS]
    for k in range(3):
        owners.sent(post, k)
    head_spread.sent()

    @pl.when(active)
    def _():
        head_return.sent()

    for copy in started:
        copy.wait_send()


def shuffle_matrix():
    matrix = np.zeros((4, SLOT, 4 * SLOT), np.float32)
    for piece in range(4):
        for member in range(4):
            for row in range(ROWS):
                matrix[piece, member * ROWS + row, member * SLOT + piece * ROWS + row] = 1
    return jnp.asarray(matrix, jnp.bfloat16)


def unshuffle_matrix():
    matrix = np.zeros((4, 4, 16, 4 * SLOT), np.float32)
    for member in range(4):
        for piece in range(4):
            for row in range(ROWS):
                matrix[member, piece, row, piece * SLOT + member * ROWS + row] = 1
    return jnp.asarray(matrix, jnp.bfloat16)


def select_matrix():
    matrix = np.zeros((4, SLOT, ROWS), np.float32)
    for piece in range(4):
        for row in range(ROWS):
            matrix[piece, piece * ROWS + row, row] = 1
    return jnp.asarray(matrix, jnp.bfloat16)


def vmem_specs(count):
    return [pl.BlockSpec(memory_space=pltpu.VMEM)] * count


def any_specs(count):
    return [pl.BlockSpec(memory_space=pl.ANY)] * count


def sems(count):
    return [pltpu.SemaphoreType.DMA((count,))] * 2


def low_array(*shape):
    return jax.ShapeDtypeStruct(shape, jnp.bfloat16)


def wide_array(*shape):
    return jax.ShapeDtypeStruct(shape, jnp.float32)


SMALL_SCRATCH = [
    pltpu.VMEM((3, 4, 8, 768), jnp.float32),
    pltpu.VMEM((2, 8, 768), jnp.float32),
]


def layer(tokens, cotangent, shards):
    low = jnp.bfloat16
    return pl.pallas_call(
        layer_kernel,
        name="layer",
        out_shape=[
            low_array(256, 768),
            wide_array(256, 768),
            wide_array(3, ROWS, WIDTH),
            wide_array(ROWS, WIDTH),
            wide_array(ROWS, 4 * WIDTH),
            wide_array(ROWS, 4 * WIDTH),
            wide_array(2, ROWS),
        ],
        in_specs=vmem_specs(10),
        out_specs=vmem_specs(7),
        scratch_shapes=[
            pltpu.VMEM((3, 4, SLOT, WIDTH), low),
            pltpu.VMEM((3, 2, 4, 4, 4, 16, WIDTH), low),
            pltpu.VMEM((6, 2, 4, 4, 4, 16, WIDTH), low),
            pltpu.VMEM((768, 2304), low),
            pltpu.VMEM((768, 768), low),
            pltpu.VMEM((3, HEADS, HEAD_DIM, 256), low),
            pltpu.VMEM((TILES * TILE, HEAD_DIM), low),
        ]
        + SMALL_SCRATCH
        + SMALL_SCRATCH
        + [
            pltpu.VMEM((256, 768), jnp.float32),
            pltpu.VMEM((256, 768), jnp.float32),
            pltpu.VMEM((8, 768), jnp.float32),
            pltpu.VMEM((8, 768), jnp.float32),
            pltpu.VMEM((256, 768), jnp.float32),
            pltpu.VMEM((MEMBERS, 3, HEAD_DIM, 256), low),
            pltpu.VMEM((MEMBERS, 1, HEAD_DIM, 256), low),
            pltpu.VMEM((TILES, 1, TILE), jnp.float32),
            pltpu.VMEM((1, HEADS, HEAD_DIM, 256), low),
            pltpu.VMEM((256, 768), low),
            pltpu.VMEM((256, 3072), low),
            pltpu.VMEM((256, 3072), low),
            pltpu.VMEM((256, 768), jnp.float32),
            pltpu.VMEM((1, HEADS, HEAD_DIM, 256), low),
            pltpu.VMEM((4, 768, 256), low),
            pltpu.VMEM((3, HEADS, HEAD_DIM, 256), low),
            pltpu.VMEM((MEMBERS, 1, HEAD_DIM, 256), low),
            pltpu.VMEM((MEMBERS, 3, HEAD_DIM, 256), low),
            pltpu.VMEM((TILES, HEAD_DIM, TILE), jnp.float32),
            pltpu.VMEM((TILES, 1, TILE), jnp.float32),
            pltpu.VMEM((3, 4, SLOT, WIDTH), low),
        ]
        + landing_scratch(6, 16)
        + landing_scratch(3, 16)
        + sems(48)
        + sems(96)
        + sems(9)
        + sems(10)
        + sems(MEMBERS)
        + sems(MEMBERS)
        + sems(48)
        + sems(96)
        + sems(9)
        + sems(10)
        + sems(MEMBERS)
        + sems(MEMBERS),
        compiler_params=pltpu.CompilerParams(
            collective_id=0, has_side_effects=True, vmem_limit_bytes=VMEM_BYTES
        ),
    )(tokens, cotangent, *shards, select_matrix(), shuffle_matrix(), unshuffle_matrix())


def hand_over_kernel(*refs):
    count = len(refs) // 2
    for source, target in zip(refs[:count], refs[count:]):
        target[...] = source[...]


def hand_over(arrays):
    return pl.pallas_call(
        hand_over_kernel,
        name="hand_over",
        out_shape=[jax.ShapeDtypeStruct(array.shape, array.dtype) for array in arrays],
        in_specs=vmem_specs(len(arrays)),
        out_specs=vmem_specs(len(arrays)),
    )(*arrays)


def per_device(tokens, cotangent, w_qkv, w_out, w_up, w_down, norm_gains):
    result, grad_tokens, grad_qkv, grad_out, grad_up, grad_down, grad_gains = hand_over(
        layer(tokens, cotangent, (w_qkv, w_out.T, w_up, w_down.T, norm_gains))
    )
    return (result, grad_tokens, grad_qkv, grad_out.T, grad_up, grad_down.T, grad_gains)


def solution(mesh):
    return jax.shard_map(
        per_device,
        mesh=mesh,
        in_specs=(
            P(("dp", "ctx", "tensor"), None),
            P(("dp", "ctx", "tensor"), None),
            P(None, ("dp", "ctx"), "tensor"),
            P("tensor", ("dp", "ctx")),
            P(("dp", "ctx"), "tensor"),
            P("tensor", ("dp", "ctx")),
            P(None, ("dp", "ctx")),
        ),
        out_specs=(
            P(("dp", "ctx", "tensor"), None),
            P(("dp", "ctx", "tensor"), None),
            P(None, ("dp", "ctx"), "tensor"),
            P("tensor", ("dp", "ctx")),
            P(("dp", "ctx"), "tensor"),
            P("tensor", ("dp", "ctx")),
            P(None, ("dp", "ctx")),
        ),
        check_vma=False,
    )
```

```python
import functools

import jax
import jax.numpy as jnp
import numpy as np
from jax import lax
from jax.experimental import pallas as pl
from jax.experimental.pallas import tpu as pltpu
from jax.sharding import PartitionSpec as P

HEAD_DIM = 64
HEADS = 12
MEMBERS = 16
ROWS = 12
WIDTH = 384
SLOT = 4 * ROWS
THIRDS = (("w", "x", "y"), ("x", "y", "w"), ("y", "w", "x"))
LATER = (
    ("z", "x", "y"), ("x", "y", "z"), ("y", "z", "x"),
    ("z", "y", "x"), ("y", "x", "z"), ("z", "y", "x"),
)
SIZES = dict(x=4, y=4, z=4, w=2, c=2)
MESH = pl.DeviceIdType.MESH
VMEM_BYTES = 62 * 1024 * 1024
epsilon = 1e-05
neg_large = -1e30


def place():
    dp, ctx, tensor = lax.axis_index("dp"), lax.axis_index("ctx"), lax.axis_index("tensor")
    return dict(x=dp // 2, y=ctx // 2, z=2 * tensor + dp % 2, w=dp % 2, c=ctx % 2)


def device_at(pos, axis, index):
    at = dict(pos)
    if axis == "w":
        axis, index = "z", 2 * (pos["z"] // 2) + index
    at[axis] = index
    return (at["x"] * 2 + at["z"] % 2, at["y"] * 2 + at["c"], at["z"] // 2)


def beside(pos, axis, by):
    if axis == "c":
        return device_at(pos, "c", 1 - pos["c"])
    return device_at(pos, axis, (pos[axis] + by) % SIZES[axis])


def greet(pos):
    barrier = pltpu.get_barrier_semaphore()
    dp, number = lax.axis_index("dp"), member_number()

    def signal(i, carry):
        to = (number + i) % MEMBERS
        pl.semaphore_signal(
            barrier, inc=1, device_id=(dp, to // 2, to % 2), device_id_type=MESH
        )
        return carry

    lax.fori_loop(1, MEMBERS, signal, 0)
    for axis, by in (("x", 1), ("x", 2), ("x", 3), ("z", 1), ("z", 3)):
        pl.semaphore_signal(barrier, inc=1, device_id=beside(pos, axis, by), device_id_type=MESH)
    pl.semaphore_wait(barrier, MEMBERS - 1 + 5)


def member_number():
    return 2 * lax.axis_index("ctx") + lax.axis_index("tensor")


def remote(src, dst, send, recv, device):
    return pltpu.make_async_remote_copy(
        src_ref=src,
        dst_ref=dst,
        send_sem=send,
        recv_sem=recv,
        device_id=device,
        device_id_type=MESH,
    )


class SmallSum:
    def __init__(self, pos, ring, pair, send, recv):
        self.pos, self.ring, self.pair, self.send, self.recv = pos, ring, pair, send, recv

    def copy(self, n, by, coming=False):
        axis = ("x", "y", "z")[n]
        slot = (self.pos[axis] + 4 - by) % 4 if coming else self.pos[axis]
        ref, sem = self.ring.at[n, slot], n * 3 + by - 1
        return remote(
            ref, ref, self.send.at[sem], self.recv.at[sem], beside(self.pos, axis, by)
        )

    def start(self, n, value):
        self.ring[n, self.pos[("x", "y", "z")[n]]] = value
        for by in (1, 2, 3):
            self.copy(n, by).start()

    def finish(self, n):
        for by in (1, 2, 3):
            self.copy(n, by, coming=True).wait_recv()
            self.copy(n, by).wait_send()
        return (self.ring[n, 0] + self.ring[n, 1]) + (self.ring[n, 2] + self.ring[n, 3])

    def pair_copy(self, slot):
        ref = self.pair.at[slot]
        return remote(ref, ref, self.send.at[9], self.recv.at[9], beside(self.pos, "c", 1))

    def start_pair(self, value):
        self.pair[self.pos["c"]] = value
        self.pair_copy(self.pos["c"]).start()

    def finish_pair(self):
        self.pair_copy(1 - self.pos["c"]).wait_recv()
        self.pair_copy(self.pos["c"]).wait_send()
        return self.pair[0] + self.pair[1]


class Group:
    def __init__(self, pos, send, recv):
        self.pos, self.send, self.recv = pos, send, recv
        self.member = (pos["y"] % 2) * 2 + pos["c"]
        y = pos["y"] + 1 - 2 * (pos["y"] % 2)
        c = 1 - pos["c"]
        self.partners = []
        for to_y, to_c in ((pos["y"], c), (y, pos["c"]), (y, c)):
            device = device_at({**pos, "y": to_y}, "c", to_c)
            self.partners.append((device, (to_y % 2) * 2 + to_c))

    def copy(self, held, k, i, coming=False):
        device, member = self.partners[i]
        ref = held.at[k, member if coming else self.member]
        return remote(ref, ref, self.send.at[k * 3 + i], self.recv.at[k * 3 + i], device)

    def start(self, held, k):
        for i in range(3):
            self.copy(held, k, i).start()

    def finish(self, held, k):
        for i in range(3):
            self.copy(held, k, i, coming=True).wait_recv()
        return jnp.concatenate([held[k, member] for member in range(4)], axis=0)

    def sent(self, held, k):
        for i in range(3):
            self.copy(held, k, i).wait_send()


class Unit:
    def __init__(self, pos, order, held, lead, sems, number, started):
        self.pos, self.order, self.held, self.lead = pos, order, held, lead
        self.send, self.recv = sems
        self.number, self.started = number, started
        self.sibling = beside(pos, "c", 1)
        self.sizes = [SIZES[axis] for axis in order]

    def move(self, src, dst, sem, device):
        sem = self.number * 16 + sem
        copy = remote(src, dst, self.send.at[sem], self.recv.at[sem], device)
        copy.start()
        self.started.append(copy)

    def arrived(self, dst, sem):
        sem = self.number * 16 + sem
        remote(dst, dst, self.send.at[sem], self.recv.at[sem], self.sibling).wait_recv()

    def along(self, stage, by):
        return beside(self.pos, self.order[stage], by)

    def steps(self, stage):
        return (1, 3, 2) if self.sizes[stage] == 4 else (1,)

    def place3(self, by):
        return (self.pos[self.order[2]] + by) % self.sizes[2]

    def at(self, stage, by):
        index = ((self.pos[self.order[stage]] + by) % self.sizes[stage],)
        for later in range(stage + 1, 3):
            index = (self.pos[self.order[later]],) + index
        return self.lead + (self.pos["c"],) + index


class Gather(Unit):
    def pass_on(self, index, sem, device):
        self.move(self.held.at[index], self.held.at[index], sem, device)

    def begin(self, stage):
        for by in self.steps(stage):
            self.pass_on(self.at(stage, 0), stage * 3 + by - 1, self.along(stage, by))
        if stage == 2:
            self.share(0)

    def finish(self, stage):
        for by in self.steps(stage):
            back = self.sizes[stage] - by
            self.arrived(self.held.at[self.at(stage, back)], stage * 3 + by - 1)
            if stage == 2:
                self.share(back)

    def share(self, by):
        self.pass_on(self.at(2, by), 9 + by, self.sibling)

    def settle(self):
        for by in range(self.sizes[2]):
            index = self.lead + (1 - self.pos["c"], self.place3(by))
            self.arrived(self.held.at[index], 9 + by)


def wide(value):
    return value.astype(jnp.float32)


class Reduce(Unit):
    def __init__(self, pos, order, held, lead, landing, sems, number, started):
        super().__init__(pos, order, held, lead, sems, number, started)
        self.cores, self.coming = landing[0], landing[1:]

    def add(self, stage, index, sources):
        held, inner = self.held, self.sizes[:stage]

        def one(slot):
            terms = [held[index + slot]] + [source[at + slot] for source, at in sources]
            while len(terms) > 1:
                terms = [sum(terms[n : n + 2][1:], terms[n]) for n in range(0, len(terms), 2)]
            held[index + slot] = terms[0]

        def body(i, carry):
            one((i // inner[0], i % inner[0]) if stage == 2 else (i,))
            return carry

        if stage:
            lax.fori_loop(0, int(np.prod(inner)), body, 0)
        else:
            one(())

    def cross(self):
        for by in (*self.steps(2), 0):
            index = self.place3(by)
            self.move(
                self.held.at[self.lead + (1 - self.pos["c"], index)],
                self.cores.at[self.lead + (index,)],
                9 + by,
                self.sibling,
            )

    def take_core(self, by):
        index = self.lead + (self.place3(by),)
        self.arrived(self.cores.at[index], 9 + by)
        self.add(2, self.at(2, by), [(self.cores, index)])

    def begin(self, stage):
        for by in self.steps(stage):
            if stage == 2:
                self.take_core(by)
            self.move(
                self.held.at[self.at(stage, by)],
                self.coming[stage].at[self.lead + (by - 1,)],
                stage * 3 + by - 1,
                self.along(stage, by),
            )

    def finish(self, stage):
        if stage == 2:
            self.take_core(0)
        sources = [(self.coming[stage], self.lead + (by - 1,)) for by in self.steps(stage)]
        for by in self.steps(stage):
            self.arrived(self.coming[stage].at[self.lead + (by - 1,)], stage * 3 + by - 1)
        self.add(stage, self.at(stage, 0), sources)


def buffer_scratch(order, lead=()):
    n1, n2, n3 = (SIZES[axis] for axis in order)
    return pltpu.VMEM(lead + (2, n3, n2, n1, 16, WIDTH), jnp.bfloat16)


def landing_scratch(order, lead=()):
    n1, n2, n3 = (SIZES[axis] for axis in order)
    return [
        pltpu.VMEM(lead + shape + (16, WIDTH), jnp.bfloat16)
        for shape in ((n3, n2, n1), (n1 - 1,), (n2 - 1, n1), (n3 - 1, n2, n1))
    ]


def copy_thirds(thirds, qkv, out, tensor):
    def body(group, carry):
        for piece in range(4):
            for third, order in enumerate(THIRDS):
                rows = pl.ds(pl.multiple_of(group * SLOT + 16 * third, 16), 16)
                value = thirds[third][slot_index(order, group, 0, piece)]
                if piece < 3:
                    qkv[rows, piece * WIDTH : (piece + 1) * WIDTH] = value
                else:
                    out[tensor, rows] = value
        return carry

    lax.fori_loop(0, 16, body, 0)


def slot_index(order, group, tensor, piece):
    z_lo = (group // 2) % 2
    at = dict(x=group // 4, z=2 * tensor + z_lo, w=z_lo, y=2 * (group % 2) + piece // 2)
    return (piece % 2, at[order[2]], at[order[1]], at[order[0]])


def collect(slots, first, orders, tensor, piece):
    return jnp.concatenate(
        [
            slots[(first + third,) + slot_index(order, group, tensor, piece)]
            for group in range(16)
            for third, order in enumerate(orders)
        ],
        axis=0,
    )


def fill(slots, first, orders, tensor, piece, value):
    for group in range(16):
        for third, order in enumerate(orders):
            row = group * SLOT + 16 * third
            index = slot_index(order, group, tensor, piece)
            if first is None:
                slots[third][index] = value[row : row + 16]
            else:
                slots[(first + third,) + index] = value[row : row + 16]


def head_place(head):
    member = head % 6
    return (member * 2) % 8 + (member // 4) * (1 + (member % 4) * 2), head // 6


def own_head(ctx, tensor):
    core, y = ctx % 2, ctx // 2
    return tensor * 6 + (1 - core) * y + core * (4 + y // 2), core * (y % 2) == 0


class Sequence:
    members, heads = MEMBERS, HEADS

    def __init__(self):
        self.dp = lax.axis_index("dp")
        ctx, tensor = lax.axis_index("ctx"), lax.axis_index("tensor")
        self.number, self.head = 2 * ctx + tensor, own_head(ctx, tensor)[0]

    def device(self, number):
        return (self.dp, number // 2, number % 2)

    def of_head(self, head):
        ctx, tensor = head_place(head)
        return 2 * ctx + tensor


class Half(Sequence):
    members, heads = MEMBERS // 2, HEADS // 2

    def __init__(self):
        super().__init__()
        self.tensor = lax.axis_index("tensor")
        self.number, self.head = lax.axis_index("ctx"), self.head % 6

    def device(self, number):
        return (self.dp, number, self.tensor)

    def of_head(self, head):
        return head_place(head)[0]


class ToHeads:
    def __init__(self, seats, src, dst, sems):
        self.seats, self.src, self.dst, (self.send, self.recv) = seats, src, dst, sems

    def copies(self, i):
        seats = self.seats
        head = (seats.number + i) % seats.heads
        to = seats.of_head(head)
        src, dst = self.src.at[:, head], self.dst.at[seats.number]
        recv = self.recv.at[seats.number]
        return (
            to == seats.number,
            lambda: pltpu.make_async_copy(src, dst, recv),
            lambda: remote(src, dst, self.send.at[head], recv, seats.device(to)),
        )

    def start(self):
        def body(i, carry):
            local, inside, outside = self.copies(i)

            @pl.when(local)
            def _():
                inside().start()

            @pl.when(jnp.logical_not(local))
            def _():
                outside().start()

            return carry

        lax.fori_loop(0, self.seats.heads, body, 0)

    def wait(self, first, last):
        def body(i, carry):
            src, dst, recv = self.src.at[:, 0], self.dst.at[i], self.recv.at[i]

            @pl.when(i == self.seats.number)
            def _():
                pltpu.make_async_copy(src, dst, recv).wait()

            @pl.when(i != self.seats.number)
            def _():
                remote(src, dst, self.send.at[0], recv, self.seats.device(i)).wait_recv()

            return carry

        lax.fori_loop(first, last, body, 0)

    def sent(self):
        def body(i, carry):
            local, inside, outside = self.copies(i)

            @pl.when(jnp.logical_not(local))
            def _():
                outside().wait_send()

            return carry

        lax.fori_loop(0, self.seats.heads, body, 0)


class FromHeads:
    def __init__(self, seats, src, dst, sems):
        self.seats, self.src, self.dst, (self.send, self.recv) = seats, src, dst, sems

    def outside(self, to):
        head = self.seats.head
        return remote(
            self.src.at[to],
            self.dst.at[:, head],
            self.send.at[to],
            self.recv.at[head],
            self.seats.device(to),
        )

    def start(self, to):
        head = self.seats.head

        @pl.when(to == self.seats.number)
        def _():
            pltpu.make_async_copy(
                self.src.at[to], self.dst.at[:, head], self.recv.at[head]
            ).start()

        @pl.when(to != self.seats.number)
        def _():
            self.outside(to).start()

    def wait(self):
        def body(i, carry):
            owner = self.seats.of_head(i)
            src, dst, recv = self.src.at[0], self.dst.at[:, i], self.recv.at[i]

            @pl.when(owner == self.seats.number)
            def _():
                pltpu.make_async_copy(src, dst, recv).wait()

            @pl.when(owner != self.seats.number)
            def _():
                remote(src, dst, self.send.at[0], recv, self.seats.device(owner)).wait_recv()

            return carry

        lax.fori_loop(0, self.seats.heads, body, 0)

    def sent(self):
        def body(i, carry):
            self.outside((self.seats.number + i) % self.seats.members).wait_send()
            return carry

        lax.fori_loop(1, self.seats.members, body, 0)


TILE = 512
TILES = 8


def turned(value):
    return jnp.transpose(value.astype(jnp.float32)).astype(jnp.bfloat16)


def allowed_tile():
    key = lax.broadcasted_iota(jnp.int32, (TILE, TILE), 0)
    query = lax.broadcasted_iota(jnp.int32, (TILE, TILE), 1)
    return query >= key


def two(ref, tile, *index):
    return jnp.concatenate([ref[(2 * tile,) + index], ref[(2 * tile + 1,) + index]], axis=1)


def put_two(ref, tile, part, value):
    ref[2 * tile, part] = value[:, :256]
    ref[2 * tile + 1, part] = value[:, 256:]


def dot(a, b):
    return jnp.dot(a, b, preferred_element_type=jnp.float32)


def dot_right(a, b):
    return lax.dot_general(a, b, (((1,), (1,)), ((), ())), preferred_element_type=jnp.float32)


def attend_tile(i, parts, keys, out, lse):
    own_rows = pl.ds(pl.multiple_of(i * TILE, TILE), TILE)
    keys[own_rows, :] = turned(parts[i, 1])
    query = parts[i, 0] * jnp.bfloat16(HEAD_DIM ** -0.5)

    def step(scores, values, state):
        top, total, weighted = state
        new_top = jnp.maximum(top, jnp.max(scores, axis=0, keepdims=True))
        fade = jnp.exp(top - new_top)
        raised = jnp.exp(scores - new_top)
        total = total * fade + jnp.sum(raised, axis=0, keepdims=True)
        weighted = weighted * fade + dot(values, raised.astype(jnp.bfloat16))
        return new_top, total, weighted

    def rows_of(j, tiles):
        return keys[pl.ds(pl.multiple_of(j * TILE, TILE), tiles * TILE), :]

    def some(tiles, first):
        def body(n, state):
            j = first + tiles * n
            values = jnp.concatenate([parts[j + m, 2] for m in range(tiles)], axis=1)
            return step(dot(rows_of(j, tiles), query), values, state)

        return body

    state = (
        jnp.full((1, TILE), neg_large, jnp.float32),
        jnp.zeros((1, TILE), jnp.float32),
        jnp.zeros((HEAD_DIM, TILE), jnp.float32),
    )
    first = 0
    for tiles in (4, 2, 1):
        count = (i - first) // tiles
        state = lax.fori_loop(0, count, some(tiles, first), state)
        first = first + count * tiles
    masked = jnp.where(allowed_tile(), dot(rows_of(i, 1), query), neg_large)
    top, total, weighted = step(masked, parts[i, 2], state)
    put_two(out, i, 0, (weighted / total).astype(jnp.bfloat16))
    lse[i] = top + jnp.log(total)


def norm_parts(values):
    center = values - jnp.mean(values, axis=-1, keepdims=True)
    inv_std = lax.rsqrt(jnp.mean(center * center, axis=-1, keepdims=True) + epsilon)
    return center * inv_std, inv_std


def norm_back(upstream, gain_row, normed, inv_std):
    scaled = upstream * gain_row
    return inv_std * (
        scaled
        - jnp.mean(scaled, axis=-1, keepdims=True)
        - normed * jnp.mean(scaled * normed, axis=-1, keepdims=True)
    )


def gelu_and_slope(v):
    scale, cubic = (2.0 / np.pi) ** 0.5, 0.044715
    square = v * v
    bend = jnp.tanh(scale * v * (1.0 + cubic * square))
    half = 0.5 * (1.0 + bend)
    slope = half + (0.5 * scale) * v * (1.0 - bend * bend) * (1.0 + 3.0 * cubic * square)
    return v * half, slope


def owned_columns():
    owner = lax.axis_index("dp") * 8 + lax.axis_index("ctx")
    column = lax.broadcasted_iota(jnp.int32, (ROWS, 768), 1)
    row = lax.broadcasted_iota(jnp.int32, (ROWS, 768), 0)
    return jnp.where(column == owner * ROWS + row, 1.0, 0.0)


def back_tile(j, parts, grad_att, lse, delta, query_sum, out):
    key_cols, value_cols = parts[j, 1], parts[j, 2]
    key_rows, value_rows = turned(key_cols), turned(value_cols)

    def step(i, state, tiles, diagonal=False):
        key_sum, value_sum = state

        def side_by_side(piece):
            return jnp.concatenate([piece(i + m) for m in range(tiles)], axis=1)

        query = side_by_side(lambda n: parts[n, 0]) * jnp.bfloat16(HEAD_DIM ** -0.5)
        grad = side_by_side(lambda n: two(grad_att, n, 0))
        shares = jnp.exp(dot(key_rows, query) - side_by_side(lambda n: lse[n]))
        if diagonal:
            shares = jnp.where(allowed_tile(), shares, 0.0)
        grad_scores = shares * (dot(value_rows, grad) - side_by_side(lambda n: delta[n]))
        grad_scores = grad_scores.astype(jnp.bfloat16)
        query_add = dot(key_cols, grad_scores)
        for m in range(tiles):
            query_sum[i + m] += query_add[:, m * TILE : (m + 1) * TILE]
        key_sum = key_sum + dot_right(query, grad_scores)
        value_sum = value_sum + dot_right(grad, shares.astype(jnp.bfloat16))
        return key_sum, value_sum

    zero = jnp.zeros((HEAD_DIM, TILE), jnp.float32)
    state = step(j, (zero, zero), 1, True)
    pairs = (TILES - 1 - j) // 2
    state = lax.fori_loop(0, pairs, lambda n, state: step(j + 1 + 2 * n, state, 2), state)
    key_sum, value_sum = lax.fori_loop(
        j + 1 + 2 * pairs, TILES, lambda i, state: step(i, state, 1), state
    )
    out[j, 0] = (query_sum[j] * HEAD_DIM ** -0.5).astype(jnp.bfloat16)
    out[j, 1] = key_sum.astype(jnp.bfloat16)
    out[j, 2] = value_sum.astype(jnp.bfloat16)


def layer_kernel(
    tokens, cotangent, a_qkv, a_out, b, c, gain, select, shuffle, unshuffle,
    result, grad_tokens, grad_qkv, grad_out, grad_up, grad_down, grad_gains,
    pre, blocks, thirds, wholes, qkv, out, projected, keys, small_buffers, last_buffers,
    forth_sum, back_sum, own_gain, kept_gains, normed, parts, head_out, lse, attended, second,
    act, hid, middle_grad, grad_att, turned_in, first_turned, grad_projected, head_grad,
    head_back, query_sum, delta, post, out_grads, out_coming, first_grads, first_coming,
    landing_w, landing_t,
    third_sems, whole_sems, pre_sems, small_sems, to_sems, from_sems,
    back_third_sems, back_whole_sems, post_sems, last_small_sems, to_grad_sems, from_grad_sems,
    swap_sems,
):
    pos = place()
    active = own_head(lax.axis_index("ctx"), lax.axis_index("tensor"))[1]
    tensor = lax.axis_index("tensor")
    partner = beside(pos, "z", 2)
    group, owners = Group(pos, *pre_sems), Group(pos, *post_sems)
    small = SmallSum(pos, *small_buffers, *small_sems)
    last_small = SmallSum(pos, *last_buffers, *last_small_sems)
    started = []
    first = [
        Gather(pos, order, thirds[u], (), third_sems, u, started)
        for u, order in enumerate(THIRDS)
    ]
    later = [
        Gather(pos, order, wholes, (u,), whole_sems, u, started)
        for u, order in enumerate(LATER)
    ]
    spread = ToHeads(Half(), projected, parts, to_sems)
    back = FromHeads(Sequence(), head_out, attended, from_sems)
    head_spread = ToHeads(Sequence(), grad_att, head_grad, to_grad_sems)
    head_return = FromHeads(Half(), head_back, grad_projected, from_grad_sems)

    def swap(n, src, dst):
        return remote(src, dst, swap_sems[0].at[n], swap_sems[1].at[n], partner)

    blocks[tensor] = tokens[...]
    swap_tokens = swap(0, blocks.at[tensor], blocks.at[tensor])
    swap_out = swap(1, out.at[tensor], out.at[tensor])
    swap_grads = swap(2, out_grads.at[1 - tensor], out_coming)
    swap_first = swap(3, first_grads.at[1 - tensor], first_coming)
    slots = (
        sum(dot(select[j], a_qkv[j]) for j in range(3)) + dot(select[3], a_out[...]),
        sum(dot(select[j], b[:, j * WIDTH : (j + 1) * WIDTH]) for j in range(4)),
        sum(dot(select[j], c[:, j * WIDTH : (j + 1) * WIDTH]) for j in range(4)),
    )
    for k in range(3):
        pre[k, group.member] = slots[k].astype(jnp.bfloat16)
    own_gain[...] = jnp.zeros_like(own_gain)
    own_gain[0:2] = 0.5 * dot(gain[...], owned_columns().astype(jnp.bfloat16))
    greet(pos)
    for k in range(3):
        group.start(pre, k)
    swap_tokens.start()
    small.start(0, own_gain[...])

    def sorted_piece(k):
        return dot(shuffle[group.member], group.finish(pre, k)).astype(jnp.bfloat16)

    piece = sorted_piece(0)
    for u, unit in enumerate(first):
        thirds[u][unit.at(0, 0)] = piece[16 * u : 16 * (u + 1)]
        unit.begin(0)
    for k in (1, 2):
        piece = sorted_piece(k)
        for u in range(3):
            wholes[later[3 * k - 3 + u].at(0, 0)] = piece[16 * u : 16 * (u + 1)]
    normed_one, inv_one = norm_parts(wide(tokens[...]))
    normed[tensor] = normed_one
    swap(0, blocks.at[1 - tensor], blocks.at[1 - tensor]).wait_recv()
    normed[1 - tensor] = norm_parts(wide(blocks[1 - tensor]))[0]
    for stage in range(3):
        for unit in first:
            unit.finish(stage)
            if stage < 2:
                unit.begin(stage + 1)
        total = small.finish(stage)
        if stage < 2:
            small.start(stage + 1, total)
        else:
            small.start_pair(total)
        if stage == 1:
            for unit in later:
                unit.begin(0)
    for unit in later:
        unit.finish(0)
        unit.begin(1)
    for unit in first:
        unit.settle()
    copy_thirds(thirds, qkv, out, tensor)
    swap_out.start()
    gains = small.finish_pair()
    kept_gains[...] = gains
    first_in = (normed[...].reshape(512, 768) * gains[0:1]).astype(jnp.bfloat16)
    for part in range(3):
        cols = dot(first_in, qkv[:, part * WIDTH : (part + 1) * WIDTH])
        cols = jnp.transpose(cols).astype(jnp.bfloat16)
        for head in range(6):
            projected[part, head] = cols[head * HEAD_DIM : (head + 1) * HEAD_DIM]
    spread.start()
    for unit in later:
        unit.finish(1)
        unit.begin(2)

    def flip(n, value):
        turned_in[n] = jnp.transpose(value).astype(jnp.bfloat16)

    flip(0, wide(cotangent[...]))
    first_turned[...] = jnp.transpose(wide(first_in)).astype(jnp.bfloat16)

    def per_queries(i, carry):
        @pl.when(active)
        def _():
            spread.wait(i, i + 1)
            attend_tile(i, parts, keys, head_out, lse)
            back.start(2 * i)
            back.start(2 * i + 1)

        return carry

    lax.fori_loop(0, 6, per_queries, 0)
    later[0].finish(2)
    lax.fori_loop(6, 7, per_queries, 0)
    for unit in later[1:]:
        unit.finish(2)
    lax.fori_loop(7, 8, per_queries, 0)
    for unit in later:
        unit.settle()
    back.wait()
    swap(1, out.at[1 - tensor], out.at[1 - tensor]).wait_recv()

    def half_attended(half):
        return attended[0, 6 * half : 6 * (half + 1)].reshape(WIDTH, 256)

    weighted = jnp.transpose(dot(out[0], half_attended(0)) + dot(out[1], half_attended(1)))
    middle = wide(tokens[...]) + weighted
    normed_two, inv_two = norm_parts(middle)
    second_in = (normed_two * kept_gains[1:2]).astype(jnp.bfloat16)
    second[...] = second_in
    forth_sum[...] = middle
    back_sum[...] = jnp.zeros_like(back_sum)

    def feed(p, carry):
        columns = pl.ds(pl.multiple_of(p * WIDTH, WIDTH), WIDTH)
        up = collect(wholes, 0, LATER[:3], p // 4, p % 4)
        down = collect(wholes, 3, LATER[3:], p // 4, p % 4)
        bent, slope = gelu_and_slope(dot(second[...], up))
        bent = bent.astype(jnp.bfloat16)
        act[:, columns] = bent
        low = (dot(cotangent[...], down) * slope).astype(jnp.bfloat16)
        hid[:, columns] = low
        forth_sum[...] += dot_right(bent, down)
        back_sum[...] += dot_right(low, up)
        return carry

    lax.fori_loop(0, 8, feed, 0)
    result[...] = forth_sum[...].astype(jnp.bfloat16)
    grad_second = back_sum[...]
    gain_two_term = jnp.sum(grad_second * normed_two, axis=0, keepdims=True)
    grad_middle = wide(cotangent[...]) + norm_back(
        grad_second, kept_gains[1:2], normed_two, inv_two
    )
    middle_grad[...] = grad_middle
    kept_gains[2:3] = gain_two_term
    for half in range(2):
        grads = dot(grad_middle.astype(jnp.bfloat16), out[half])
        grads = jnp.transpose(grads).astype(jnp.bfloat16)
        for head in range(6):
            grad_att[0, 6 * half + head] = grads[head * HEAD_DIM : (head + 1) * HEAD_DIM]
    head_spread.start()
    flip(1, wide(second[...]))
    flip(2, middle_grad[...])
    spread.sent()

    @pl.when(active)
    def _():
        back.sent()

    for k in range(3):
        group.sent(pre, k)
    for copy in started:
        copy.wait_send()
    started = []
    units = [
        Reduce(pos, order, wholes, (u,), landing_w, back_whole_sems, u, started)
        for u, order in enumerate(LATER)
    ]
    last = [
        Reduce(pos, order, thirds[u], (), landing_t[u], back_third_sems, u, started)
        for u, order in enumerate(THIRDS)
    ]

    def give(p, carry):
        columns = pl.ds(pl.multiple_of(p * WIDTH, WIDTH), WIDTH)
        for k, (left, right) in enumerate(((1, hid), (0, act))):
            value = dot(turned_in[left], right[:, columns]).astype(jnp.bfloat16)
            fill(wholes, 3 * k, LATER[3 * k : 3 * k + 3], p // 4, p % 4, value)
        return carry

    lax.fori_loop(0, 8, give, 0)
    for unit in units:
        unit.cross()
    for half in range(2):
        out_grads[half] = dot_right(turned_in[2], half_attended(half)).astype(jnp.bfloat16)
    swap_grads.start()

    @pl.when(active)
    def _():
        head_spread.wait(0, MEMBERS)

        def prepare(i, carry):
            delta[i] = jnp.sum(
                wide(two(head_out, i, 0)) * wide(two(head_grad, i, 0)), axis=0, keepdims=True
            )
            query_sum[i] = jnp.zeros((HEAD_DIM, TILE), jnp.float32)
            return carry

        lax.fori_loop(0, TILES, prepare, 0)

    def per_keys(j, carry):
        @pl.when(active)
        def _():
            back_tile(j, parts, head_grad, lse, delta, query_sum, head_back)
            head_return.start(j)

        return carry

    lax.fori_loop(0, 1, per_keys, 0)
    for unit in units:
        unit.begin(2)
    lax.fori_loop(1, 8, per_keys, 0)
    for unit in units:
        unit.finish(2)
        unit.begin(1)
    head_return.wait()

    swap(2, out_grads.at[0], out_coming).wait_recv()
    fill(thirds, None, THIRDS, 0, 3, out_grads[tensor] + out_coming[...])
    for part in range(3):
        rows = grad_projected[part].reshape(WIDTH, 512)
        fill(thirds, None, THIRDS, 0, part, dot_right(first_turned[...], rows).astype(jnp.bfloat16))
    for unit in last:
        unit.cross()
    first_parts = jnp.transpose(dot(qkv[...], grad_projected[...].reshape(3 * WIDTH, 512)))
    first_grads[...] = first_parts.astype(jnp.bfloat16).reshape(2, 256, 768)
    swap_first.start()
    term = jnp.sum(first_parts * normed[...].reshape(512, 768), axis=0, keepdims=True)
    row = lax.broadcasted_iota(jnp.int32, (8, 768), 0)
    last_small.start(0, jnp.where(row == 0, term, jnp.where(row == 1, kept_gains[2:3], 0.0)))
    for unit in last:
        unit.begin(2)
    for unit in units:
        unit.finish(1)
        unit.begin(0)
    swap(3, first_grads.at[0], first_coming).wait_recv()
    grad_first = wide(first_grads[tensor]) + wide(first_coming[...])
    grad_tokens[...] = middle_grad[...] + norm_back(
        grad_first, kept_gains[0:1], normed[tensor], inv_one
    )
    for u, unit in enumerate(units):
        unit.finish(0)
        post[u // 3, owners.member, pl.ds(16 * (u % 3), 16)] = wholes[unit.at(0, 0)]
    for k in range(2):
        owners.start(post, k)
    for stage in (2, 1, 0):
        total = last_small.finish(2 - stage)
        if stage > 0:
            last_small.start(3 - stage, total)
        else:
            last_small.start_pair(total)
        for unit in last:
            unit.finish(stage)
            if stage > 0:
                unit.begin(stage - 1)
    for u, unit in enumerate(last):
        post[2, owners.member, pl.ds(16 * u, 16)] = thirds[u][unit.at(0, 0)]
    owners.start(post, 2)
    grad_gains[...] = lax.dot_general(
        last_small.finish_pair(),
        owned_columns(),
        (((1,), (1,)), ((), ())),
        precision=lax.Precision.HIGHEST,
        preferred_element_type=jnp.float32,
    )[0:2]

    def own_rows(held, piece):
        return dot(unshuffle[owners.member, piece], held)

    for k, out in enumerate((grad_up, grad_down)):
        held = owners.finish(post, k)
        for piece in range(4):
            out[:, piece * WIDTH : (piece + 1) * WIDTH] = own_rows(held, piece)[:ROWS]
    held = owners.finish(post, 2)
    for piece in range(3):
        grad_qkv[piece] = own_rows(held, piece)[:ROWS]
    grad_out[...] = own_rows(held, 3)[:ROWS]
    for k in range(3):
        owners.sent(post, k)
    head_spread.sent()
    for copy in (swap_tokens, swap_out, swap_grads, swap_first):
        copy.wait_send()

    @pl.when(active)
    def _():
        head_return.sent()

    for copy in started:
        copy.wait_send()


def shuffle_matrix():
    matrix = np.zeros((4, SLOT, 4 * SLOT), np.float32)
    for piece in range(4):
        for member in range(4):
            for row in range(ROWS):
                matrix[piece, member * ROWS + row, member * SLOT + piece * ROWS + row] = 1
    return jnp.asarray(matrix, jnp.bfloat16)


def unshuffle_matrix():
    matrix = np.zeros((4, 4, 16, 4 * SLOT), np.float32)
    for member in range(4):
        for piece in range(4):
            for row in range(ROWS):
                matrix[member, piece, row, piece * SLOT + member * ROWS + row] = 1
    return jnp.asarray(matrix, jnp.bfloat16)


def select_matrix():
    matrix = np.zeros((4, SLOT, ROWS), np.float32)
    for piece in range(4):
        for row in range(ROWS):
            matrix[piece, piece * ROWS + row, row] = 1
    return jnp.asarray(matrix, jnp.bfloat16)


def vmem_specs(count):
    return [pl.BlockSpec(memory_space=pltpu.VMEM)] * count


def any_specs(count):
    return [pl.BlockSpec(memory_space=pl.ANY)] * count


def sems(count):
    return [pltpu.SemaphoreType.DMA((count,))] * 2


def low_array(*shape):
    return jax.ShapeDtypeStruct(shape, jnp.bfloat16)


def wide_array(*shape):
    return jax.ShapeDtypeStruct(shape, jnp.float32)


SMALL_SCRATCH = [
    pltpu.VMEM((3, 4, 8, 768), jnp.float32),
    pltpu.VMEM((2, 8, 768), jnp.float32),
]


def layer(tokens, cotangent, shards):
    low = jnp.bfloat16
    return pl.pallas_call(
        layer_kernel,
        name="layer",
        out_shape=[
            low_array(256, 768),
            wide_array(256, 768),
            wide_array(3, ROWS, WIDTH),
            wide_array(ROWS, WIDTH),
            wide_array(ROWS, 4 * WIDTH),
            wide_array(ROWS, 4 * WIDTH),
            wide_array(2, ROWS),
        ],
        in_specs=vmem_specs(10),
        out_specs=vmem_specs(7),
        scratch_shapes=[
            pltpu.VMEM((3, 4, SLOT, WIDTH), low),
            pltpu.VMEM((2, 256, 768), low),
            [buffer_scratch(order) for order in THIRDS],
            buffer_scratch(LATER[0], (6,)),
            pltpu.VMEM((768, 3 * WIDTH), low),
            pltpu.VMEM((2, 768, WIDTH), low),
            pltpu.VMEM((3, HEADS // 2, HEAD_DIM, 512), low),
            pltpu.VMEM((TILES * TILE, HEAD_DIM), low),
            SMALL_SCRATCH,
            SMALL_SCRATCH,
            pltpu.VMEM((256, 768), jnp.float32),
            pltpu.VMEM((256, 768), jnp.float32),
            pltpu.VMEM((8, 768), jnp.float32),
            pltpu.VMEM((8, 768), jnp.float32),
            pltpu.VMEM((2, 256, 768), jnp.float32),
            pltpu.VMEM((TILES, 3, HEAD_DIM, TILE), low),
            pltpu.VMEM((MEMBERS, 1, HEAD_DIM, 256), low),
            pltpu.VMEM((TILES, 1, TILE), jnp.float32),
            pltpu.VMEM((1, HEADS, HEAD_DIM, 256), low),
            pltpu.VMEM((256, 768), low),
            pltpu.VMEM((256, 3072), low),
            pltpu.VMEM((256, 3072), low),
            pltpu.VMEM((256, 768), jnp.float32),
            pltpu.VMEM((1, HEADS, HEAD_DIM, 256), low),
            pltpu.VMEM((3, 768, 256), low),
            pltpu.VMEM((768, 512), low),
            pltpu.VMEM((3, HEADS // 2, HEAD_DIM, 512), low),
            pltpu.VMEM((MEMBERS, 1, HEAD_DIM, 256), low),
            pltpu.VMEM((TILES, 3, HEAD_DIM, TILE), low),
            pltpu.VMEM((TILES, HEAD_DIM, TILE), jnp.float32),
            pltpu.VMEM((TILES, 1, TILE), jnp.float32),
            pltpu.VMEM((3, 4, SLOT, WIDTH), low),
            pltpu.VMEM((2, 768, WIDTH), low),
            pltpu.VMEM((768, WIDTH), low),
            pltpu.VMEM((2, 256, 768), low),
            pltpu.VMEM((256, 768), low),
            landing_scratch(LATER[0], (6,)),
            [landing_scratch(order) for order in THIRDS],
        ]
        + [sems(count) for count in (48, 96, 9, 10, MEMBERS, MEMBERS) * 2 + (4,)],
        compiler_params=pltpu.CompilerParams(
            collective_id=0, has_side_effects=True, vmem_limit_bytes=VMEM_BYTES
        ),
    )(tokens, cotangent, *shards, select_matrix(), shuffle_matrix(), unshuffle_matrix())


def hand_over_kernel(*refs):
    count = len(refs) // 2
    for source, target in zip(refs[:count], refs[count:]):
        target[...] = source[...]


def hand_over(arrays):
    return pl.pallas_call(
        hand_over_kernel,
        name="hand_over",
        out_shape=[jax.ShapeDtypeStruct(array.shape, array.dtype) for array in arrays],
        in_specs=vmem_specs(len(arrays)),
        out_specs=vmem_specs(len(arrays)),
    )(*arrays)


def per_device(tokens, cotangent, w_qkv, w_out, w_up, w_down, norm_gains):
    result, grad_tokens, grad_qkv, grad_out, grad_up, grad_down, grad_gains = hand_over(
        layer(tokens, cotangent, (w_qkv, w_out.T, w_up, w_down.T, norm_gains))
    )
    return (result, grad_tokens, grad_qkv, grad_out.T, grad_up, grad_down.T, grad_gains)


def solution(mesh):
    return jax.shard_map(
        per_device,
        mesh=mesh,
        in_specs=(
            P(("dp", "ctx", "tensor"), None),
            P(("dp", "ctx", "tensor"), None),
            P(None, ("dp", "ctx"), "tensor"),
            P("tensor", ("dp", "ctx")),
            P(("dp", "ctx"), "tensor"),
            P("tensor", ("dp", "ctx")),
            P(None, ("dp", "ctx")),
        ),
        out_specs=(
            P(("dp", "ctx", "tensor"), None),
            P(("dp", "ctx", "tensor"), None),
            P(None, ("dp", "ctx"), "tensor"),
            P("tensor", ("dp", "ctx")),
            P(("dp", "ctx"), "tensor"),
            P("tensor", ("dp", "ctx")),
            P(None, ("dp", "ctx")),
        ),
        check_vma=False,
    )
```
